32 devices in a mesh: vox: 4 (over x, core), dp: 8 (over z, y).
Axes of the slice: x: 2, y: 2, z: 4, core: 2. Of those that a mesh axis runs over, the one named last changes fastest.
Arguments:
- fmri: bfloat16 [2048, 8192], P('dp', 'vox'), may hold values from -6 to 6
- subject: int32 [2048, 1], P('dp'), may hold values from 0 to 7; in each aligned block of 256 rows (0 to 255, 256 to 511, ...) at most 64 rows name the same one
- ridge_maps: bfloat16 [8, 8192, 4096], P('dp', 'vox'), may hold values from -0.09375 to 0.09375
- voxel_count: int32 [8], replicated, may hold values from 4096 to 8192, as said below
- w_first: bfloat16 [8192, 256], replicated, may hold values from -0.125 to 0.125
- w_second: bfloat16 [4096, 128], replicated, may hold values from -0.1875 to 0.1875
- w_third: bfloat16 [2048, 64], replicated, may hold values from -0.25 to 0.25
- target: bfloat16 [2048, 16, 32, 64], P(('dp', 'vox')), may hold values from -6 to 6
Outputs:
- decoded: bfloat16 [2048, 16, 32, 64], P(('dp', 'vox'))
- grad_first: bfloat16 [8192, 256], replicated
- grad_second: bfloat16 [4096, 128], replicated
- grad_third: bfloat16 [2048, 64], replicated
The draws below stay inside these ranges and needn't reach their ends.
Inputs may be any that keep to these rules, and one draw needn't show every extreme that they name: Among the 256 samples of one index of dp (aligned blocks) no subject appears more than 64 times, and in some block some subject appears exactly 64 times; every subject appears somewhere. Readings of a subject at voxel positions voxel_count or beyond are unused; some subject has 8192 and some 8192 // 2.
All inputs are finite; a program needn't handle non-finite values.
Results may differ from the reference program's by a relative error of at most 0.008.
Values may be sent and summed in bfloat16 or wider, within the bound.
No kernel may reach another device: no remote copies, remote signals or barrier semaphores. Data moves between devices by JAX's collectives and lax.ppermute only.
A program may use at most 384 MiB of HBM per device.

```python
import math
import jax
import jax.numpy as jnp
import numpy as np
from jax import lax

VOX = 8192
C0 = 512
C1 = 256
C2 = 128
C3 = 64
H0 = 2
W0 = 4
SAMP_DEV = 256
L = 4096
SUBJ = 8
SAMPLES = 2048
CAP = 64
H3 = 16
W3 = 32
N_DP = 8


def draw_voxel_count(key, part):
    count_key = jax.random.fold_in(key, 11)
    ranking_key = jax.random.fold_in(key, 12)
    counts = jax.random.randint(count_key, (SUBJ,), VOX // 2, VOX + 1, dtype=jnp.int32)
    ranking = jax.random.permutation(ranking_key, SUBJ)
    counts = counts.at[ranking[0]].set(VOX)
    counts = counts.at[ranking[1]].set(VOX // 2)
    return counts.astype(jnp.int32)


def spiked(result, rng, source, target, blocks, factor):
    def block_of(axis_at):
        return (jnp.arange(result.shape[axis_at]) // (result.shape[axis_at] // blocks)).reshape((-1,) + (1,) * (result.ndim - 1 - axis_at))

    near = jax.random.permutation(rng, blocks)[block_of(target)]
    second = (block_of(target) + blocks // 2) % blocks
    return jnp.where((block_of(source) == near) | (block_of(source) == second), factor * result, result)


def steps_of(rng, shape, shards, smallest, high):
    gain = 1.0
    for position, blocks in shards:
        steps = jax.random.uniform(jax.random.fold_in(jax.random.fold_in(rng, 6), position), (blocks,), jnp.float32, smallest / len(shards), high / len(shards))
        gain = gain * jnp.repeat(jnp.exp(steps), shape[position] // blocks).reshape((-1,) + (1,) * (len(shape) - 1 - position))
    return gain


def assign_block(own_key, own, number, rows, amount, top, limit, skew):
    order = jax.random.permutation(own_key, amount)
    crowded, usual = portions_of(amount, rows * top, limit, skew, True), portions_of(amount, rows * top, limit, skew, False)
    places = jnp.arange(amount)

    def named(tallies, offset_by):
        used = int((tallies > 0).sum())
        fixed = max(1, used // 4)
        shifted = fixed + (places - fixed + offset_by * (used - fixed)) % max(1, amount - fixed)
        return jnp.zeros((amount,), jnp.int32).at[order[jnp.where(places < fixed, places, shifted)]].set(jnp.asarray(tallies, jnp.int32))

    tallies = jnp.where(number % 4 == 0, named(crowded, number // 4), named(usual, number - number // 4 - 1))
    mixed = jax.random.permutation(jax.random.fold_in(own, 3), amount)
    giver, taker = mixed[0:amount // 2 * 2:2], mixed[1:amount // 2 * 2:2]
    margin = jnp.minimum(tallies[giver] - 1, limit - tallies[taker]) // 2
    margin = jnp.where((giver == order[0]) | (taker == order[0]) | (tallies[taker] == 0), 0, jnp.maximum(margin, 0))
    shifted = jax.random.randint(jax.random.fold_in(own, 4), (amount // 2,), 0, 1 << 20) % (margin + 1)
    tallies = tallies.at[giver].add(-shifted).at[taker].add(shifted)
    members = jnp.searchsorted(jnp.cumsum(tallies), jnp.arange(rows * top), side="right").astype(jnp.int32)
    listing = members.reshape(top, rows).T
    listing = listing[jax.random.permutation(jax.random.fold_in(own, 1), rows)]
    offset_by = jax.random.randint(jax.random.fold_in(own, 2), (rows, 1), 0, top)
    return jnp.take_along_axis(listing, (jnp.arange(top)[None, :] + offset_by) % top, axis=1)


def portions_of(amount, total, reach, slope, full):
    loads = [(1 << 20) // math.isqrt(grade ** slope) + 1 for grade in range(1, amount + 1)]
    largest = reach if full else min(reach, max(-(-total // amount), total * loads[0] // sum(loads)))
    least = 1 if total - largest >= amount - 1 else 0
    given, spare = [largest] + [least] * (amount - 1), total - largest - least * (amount - 1)
    while spare > 0:
        movable = [i for i in range(1, amount) if given[i] < largest] or [i for i in range(1, amount) if given[i] < reach]
        mass, left = sum([loads[i] for i in movable]), spare
        for i in movable:
            addition = min(reach - given[i], max(1, left * loads[i] // mass), spare)
            given[i] = given[i] + addition
            spare = spare - addition
    return np.array(given)


def scatter_about(key, extent, deviation, bound, split=(), kind=jnp.bfloat16):
    gain = steps_of(key, extent, split, -0.22, 0.18) if split else 1.0
    array = jax.random.normal(key, extent, jnp.float32) * deviation * gain
    return jnp.minimum(jnp.maximum(array, -bound), bound).astype(kind)


def gaussian_with(own_key, shape, scale, bound, cuts, heavy, held_as=jnp.bfloat16):
    drawn = scale * jax.random.normal(own_key, shape, jnp.float32)
    if cuts:
        drawn = drawn * steps_of(own_key, shape, cuts, -0.22, 0.18)
    return jnp.clip(spiked(drawn, jax.random.fold_in(own_key, 3), *heavy), -bound, bound).astype(held_as)


def setup_inputs(seed: int = 0) -> dict:
    key_list = jax.random.split(jax.random.key(seed), 9)
    fmri = scatter_about(key_list[0], (SAMPLES, VOX), 1.0, 6.0, ((0, 8), (1, 4)))
    subject_keys = jax.random.split(jax.random.fold_in(key_list[1], 1), SAMPLES // SAMP_DEV)
    subject_turns = jax.random.permutation(jax.random.fold_in(key_list[1], 3), SAMPLES // SAMP_DEV)
    subject = jax.vmap(lambda own, number: assign_block(jax.random.fold_in(key_list[1], 2), own, number, SAMP_DEV, SUBJ, 1, CAP, 2))(subject_keys, subject_turns).reshape((SAMPLES, 1))
    ridge_maps = gaussian_with(key_list[2], (SUBJ, VOX, L), VOX ** -0.5, 0.09375, ((0, 8), (1, 4)), (1, 2, 4, 2.0))
    voxel_count = draw_voxel_count(jax.random.fold_in(key_list[8], 71), 0)
    w_first = scatter_about(key_list[4], (16 * C0, C1), (4 * C0) ** -0.5, 0.125)
    w_second = scatter_about(key_list[5], (16 * C1, C2), (4 * C1) ** -0.5, 0.1875)
    w_third = scatter_about(key_list[6], (16 * C2, C3), (4 * C2) ** -0.5, 0.25)
    target = scatter_about(key_list[7], (SAMPLES, H3, W3, C3), 1.0, 6.0, ((0, 32),))
    return dict(fmri=fmri, subject=subject, ridge_maps=ridge_maps, voxel_count=voxel_count, w_first=w_first, w_second=w_second, w_third=w_third, target=target)


TAPS = (((0, 1), (-1, 3)), ((0, 2), (1, 0)))

def rounded(values):
    return lax.optimization_barrier(values.astype(jnp.bfloat16))

def product(form, left, right):
    return jnp.einsum(form, left.astype(jnp.float32), right.astype(jnp.float32))

def parity_inputs(inputs, row_par, col_par):
    height = inputs.shape[1]
    breadth = inputs.shape[2]
    padded = jnp.pad(inputs, ((0, 0), (1, 1), (1, 1), (0, 0)))
    pieces = []
    for row_shift, row_tap in TAPS[row_par]:
        for col_shift, col_tap in TAPS[col_par]:
            pieces.append(padded[:, 1 + row_shift:1 + row_shift + height, 1 + col_shift:1 + col_shift + breadth, :])
    return jnp.concatenate(pieces, axis=3)

def parity_weight(kernel, row_par, col_par):
    pieces = []
    for row_shift, row_tap in TAPS[row_par]:
        for col_shift, col_tap in TAPS[col_par]:
            pieces.append(kernel[row_tap, col_tap])
    return jnp.concatenate(pieces, axis=0)

def transpose_conv(inputs, weights):
    in_chan = inputs.shape[3]
    kernel = weights.reshape(4, 4, in_chan, weights.shape[1])
    row_list = []
    for row_par in (0, 1):
        col_list = []
        for col_par in (0, 1):
            col_list.append(product('nhwk,kc->nhwc', parity_inputs(inputs, row_par, col_par), parity_weight(kernel, row_par, col_par)))
        row_list.append(jnp.stack(col_list, axis=3))
    stacked = jnp.stack(row_list, axis=2)
    shape_now = stacked.shape
    return stacked.reshape(shape_now[0], 2 * shape_now[1], 2 * shape_now[3], shape_now[5])

def adjoint_conv(grad_out, weights, in_chan):
    kernel = weights.reshape(4, 4, in_chan, weights.shape[1])
    sample_count = grad_out.shape[0]
    height = grad_out.shape[1] // 2
    breadth = grad_out.shape[2] // 2
    summed = jnp.zeros((sample_count, height + 2, breadth + 2, in_chan), jnp.float32)
    for row_par in (0, 1):
        for col_par in (0, 1):
            grad_part = grad_out[:, row_par::2, col_par::2, :]
            grad_cat = product('nhwc,kc->nhwk', grad_part, parity_weight(kernel, row_par, col_par))
            tap_index = 0
            for row_shift, row_tap in TAPS[row_par]:
                for col_shift, col_tap in TAPS[col_par]:
                    tap_piece = grad_cat[..., tap_index * in_chan:(tap_index + 1) * in_chan]
                    summed = summed + jnp.pad(tap_piece, ((0, 0), (1 + row_shift, 1 - row_shift), (1 + col_shift, 1 - col_shift), (0, 0)))
                    tap_index += 1
    return summed[:, 1:-1, 1:-1, :]

def weight_grad(inputs, grad_out):
    in_chan = inputs.shape[3]
    tap_blocks = {}
    for row_par in (0, 1):
        for col_par in (0, 1):
            grad_cat = product('nhwk,nhwc->kc', parity_inputs(inputs, row_par, col_par), grad_out[:, row_par::2, col_par::2, :])
            tap_index = 0
            for row_shift, row_tap in TAPS[row_par]:
                for col_shift, col_tap in TAPS[col_par]:
                    tap_blocks[row_tap, col_tap] = grad_cat[tap_index * in_chan:(tap_index + 1) * in_chan]
                    tap_index += 1
    return jnp.concatenate([tap_blocks[row_tap, col_tap] for row_tap in range(4) for col_tap in range(4)], axis=0)

def gelu_back(pre_act, upstream):
    return jax.vjp(jax.nn.gelu, pre_act)[1](upstream)[0]

def decode_block(latent, target, w_first, w_second, w_third):
    sample_count = latent.shape[0]
    in_chan = w_first.shape[0] // 16
    grid_in = latent.reshape(sample_count, H0, W0, in_chan)
    pre_one = transpose_conv(grid_in, w_first)
    act_one = rounded(jax.nn.gelu(pre_one))
    pre_two = transpose_conv(act_one, w_second)
    act_two = rounded(jax.nn.gelu(pre_two))
    output = transpose_conv(act_two, w_third)
    decoded = output.astype(jnp.bfloat16)
    grad_out = rounded((output - target.astype(jnp.float32)) / SAMP_DEV)
    grad_third = weight_grad(act_two, grad_out)
    grad_act_two = rounded(adjoint_conv(grad_out, w_third, act_two.shape[3]))
    grad_pre_two = rounded(gelu_back(pre_two, grad_act_two.astype(jnp.float32)))
    grad_second = weight_grad(act_one, grad_pre_two)
    grad_act_one = rounded(adjoint_conv(grad_pre_two, w_second, act_one.shape[3]))
    grad_pre_one = rounded(gelu_back(pre_one, grad_act_one.astype(jnp.float32)))
    grad_first = weight_grad(grid_in, grad_pre_one)
    return (decoded, (grad_first, grad_second, grad_third))

def reference(fmri, subject, ridge_maps, voxel_count, w_first, w_second, w_third, target):
    owners = subject[:, 0].astype(jnp.int32)
    slot_total = N_DP * CAP
    voxel_ids = jnp.arange(VOX, dtype=jnp.int32)
    slot_ids = jnp.arange(slot_total, dtype=jnp.int32)

    def project(subject_id, latent_sum):
        subject_id = jnp.asarray(subject_id).astype(jnp.int32)
        matches = owners == subject_id
        chosen = jnp.nonzero(matches, size=slot_total, fill_value=0)[0].astype(jnp.int32)
        live_rows = (slot_ids < jnp.sum(matches.astype(jnp.int32))).astype(jnp.float32)
        voxel_keep = (voxel_ids < voxel_count[subject_id]).astype(fmri.dtype)
        readings = fmri[chosen] * voxel_keep[None, :]
        weights = lax.dynamic_index_in_dim(ridge_maps, subject_id, 0, keepdims=False)
        projected = jnp.dot(readings, weights, preferred_element_type=jnp.float32)
        projected = projected * live_rows[:, None]
        return latent_sum.at[chosen].add(projected)
    latent_sum = lax.fori_loop(0, SUBJ, project, jnp.zeros((SAMPLES, L), jnp.float32))
    latent = rounded(latent_sum)
    block_count = SAMPLES // SAMP_DEV
    latent_blocks = latent.reshape(block_count, SAMP_DEV, L)
    target_blocks = target.reshape(block_count, SAMP_DEV, H3, W3, C3)

    def run_block(running, inputs):
        decoded, grads = decode_block(inputs[0], inputs[1], w_first, w_second, w_third)
        return ((running[0] + grads[0], running[1] + grads[1], running[2] + grads[2]), decoded)
    zero_grads = (jnp.zeros(w_first.shape, jnp.float32), jnp.zeros(w_second.shape, jnp.float32), jnp.zeros(w_third.shape, jnp.float32))
    totals, decoded = lax.scan(run_block, zero_grads, (latent_blocks, target_blocks))
    return (decoded.reshape(SAMPLES, H3, W3, C3), totals[0].astype(jnp.bfloat16), totals[1].astype(jnp.bfloat16), totals[2].astype(jnp.bfloat16))
```

```python
import functools
import jax
import jax.numpy as jnp
from jax import lax
from jax.experimental import pallas as pl
from jax.sharding import PartitionSpec as P
from jax.experimental.pallas import tpu as pltpu

H0 = 2
W0 = 4
SAMP_DEV = 256
ROW_TAPS = ((1, 3), (2, 0))
ROW_SHIFT = (-1, 1)
COL_TAPS = (1, 2, 3, 0)
VMEM_BYTES = 60 * 1024 * 1024


def paired_weight(weights, in_chan):
    out_chan = weights.shape[1]
    kernel = weights.reshape(4, 4, in_chan, out_chan)
    halves = []
    for parity in (0, 1):
        rows = []
        for row_tap in ROW_TAPS[parity]:
            rows.append(jnp.concatenate([kernel[row_tap, col_tap] for col_tap in COL_TAPS], axis=1))
        halves.append(jnp.concatenate(rows, axis=0))
    return jnp.stack(halves)


def product(left, right):
    return jnp.dot(left, right, preferred_element_type=jnp.float32)


def product_nt(left, right):
    return lax.dot_general(left, right, (((1,), (1,)), ((), ())), preferred_element_type=jnp.float32)


def product_tn(left, right):
    return lax.dot_general(left, right, (((0,), (0,)), ((), ())), preferred_element_type=jnp.float32)


def gelu_pair(value):
    root = 0.7978845608028654
    square = value * value
    tanh = jnp.tanh(root * (value + 0.044715 * (square * value)))
    half = 0.5 * (1.0 + tanh)
    slope = half + (0.5 * value) * (1.0 - tanh * tanh) * (root + (3 * 0.044715 * root) * square)
    return value * half, slope


def up_rows(product_ref, act_ref, slope_ref, act_row, slope_row, count, breadth, out_chan):
    width = 2 * out_chan
    for col in range(breadth):
        here = pl.ds(col * count, count)
        for col_par in (0, 1):
            lanes = pl.ds(col_par * out_chan, out_chan)
            side = pl.ds(width + col_par * out_chan, out_chan)
            value = product_ref[here, lanes]
            other = col - 1 if col_par == 0 else col + 1
            if 0 <= other < breadth:
                value = value + product_ref[pl.ds(other * count, count), side]
            act, slope = gelu_pair(value)
            rows = pl.ds((2 * col + col_par) * count, count)
            act_ref[act_row, rows, :] = act.astype(jnp.bfloat16)
            slope_ref[slope_row, rows, :] = slope


def forward_kernel(count, latent_ref, w_one_ref, w_two_ref, act_one_ref, slope_one_ref, act_two_ref, slope_two_ref, tmp_one, tmp_two):
    in_chan = w_one_ref.shape[1] // 2
    mid_chan = w_two_ref.shape[1] // 2
    out_chan = w_two_ref.shape[2] // 4

    def latent_row(row):
        return jnp.concatenate(
            [latent_ref[:, pl.ds((row * W0 + col) * in_chan, in_chan)] for col in range(W0)], axis=0
        )

    for row in range(H0):
        for parity in (0, 1):
            tmp_one[...] = product(latent_row(row), w_one_ref[parity, :in_chan, :])
            other = row + ROW_SHIFT[parity]
            if 0 <= other < H0:
                tmp_one[...] += product(latent_row(other), w_one_ref[parity, in_chan:, :])
            at = 2 * row + parity
            up_rows(tmp_one, act_one_ref, slope_one_ref, at, at, count, W0, mid_chan)
    height = 2 * H0
    breadth = 2 * W0
    act_two_ref[0] = jnp.zeros_like(act_two_ref[0])
    act_two_ref[2 * height + 1] = jnp.zeros_like(act_two_ref[0])
    for row in range(height):
        for parity in (0, 1):
            tmp_two[...] = product(act_one_ref[row], w_two_ref[parity, :mid_chan, :])
            other = row + ROW_SHIFT[parity]
            if 0 <= other < height:
                tmp_two[...] += product(act_one_ref[other], w_two_ref[parity, mid_chan:, :])
            at = 2 * row + parity
            up_rows(tmp_two, act_two_ref, slope_two_ref, at + 1, at, count, breadth, out_chan)


def last_kernel(count, act_ref, slope_ref, w_ref, target_ref, decoded_ref, grad_ref, kgrad_ref, tmp, grads, adj):
    step = pl.program_id(0)
    steps = pl.num_programs(0)
    breadth = act_ref.shape[1] // count
    in_chan = act_ref.shape[2]
    lanes = 2 * (w_ref.shape[2] // 4)

    @pl.when(step == 0)
    def _():
        adj[...] = jnp.zeros_like(adj)
        kgrad_ref[...] = jnp.zeros_like(kgrad_ref)
        grads[...] = jnp.zeros_like(grads)

    low = lax.broadcasted_iota(jnp.int32, (count, lanes), 1) < lanes // 2
    for parity in (0, 1):
        other = step + 1 + ROW_SHIFT[parity]
        left = jnp.concatenate([act_ref[step + 1], act_ref[other]], axis=1)
        tmp[...] = product(left, w_ref[parity])
        zero = jnp.zeros((count, lanes), jnp.float32)
        for col in range(breadth):
            here = pl.ds(col * count, count)
            before = tmp[pl.ds((col - 1) * count, count), lanes:] if col > 0 else zero
            after = tmp[pl.ds((col + 1) * count, count), lanes:] if col < breadth - 1 else zero
            value = tmp[here, :lanes] + jnp.where(low, before, after)
            decoded_ref[parity, here, :] = value.astype(jnp.bfloat16)
            grad = (value - target_ref[parity, here, :].astype(jnp.float32)) * (1.0 / SAMP_DEV)
            grads[pl.ds((col + 1) * count, count), :] = grad
        pieces = []
        for col in range(breadth):
            before = grads[pl.ds(col * count, count), :]
            here = grads[pl.ds((col + 1) * count, count), :]
            after = grads[pl.ds((col + 2) * count, count), :]
            side = jnp.where(low, after, before)
            pieces.append(jnp.concatenate([here.astype(jnp.bfloat16), side.astype(jnp.bfloat16)], axis=1))
        taps = jnp.concatenate(pieces, axis=0)
        kgrad_ref[parity] += product_tn(left, taps)
        back = product_nt(taps, w_ref[parity])
        adj[step + 1] += back[:, :in_chan]
        adj[other] += back[:, in_chan:]

    @pl.when(step == steps - 1)
    def _():
        def finish(row, carry):
            upstream = adj[row + 1].astype(jnp.bfloat16).astype(jnp.float32)
            grad_ref[row] = (upstream * slope_ref[row]).astype(jnp.bfloat16)
            return carry

        lax.fori_loop(0, steps, finish, 0)


def side_taps(grad_ref, row, count, breadth):
    def at(col):
        if 0 <= col < 2 * breadth:
            return grad_ref[row, pl.ds(col * count, count), :]
        return jnp.zeros((count, grad_ref.shape[2]), jnp.bfloat16)

    pieces = []
    for col in range(breadth):
        pieces.append(jnp.concatenate([at(2 * col), at(2 * col + 1), at(2 * col + 2), at(2 * col - 1)], axis=1))
    return jnp.concatenate(pieces, axis=0)


def backward_kernel(count, latent_ref, act_ref, slope_ref, w_ref, grad_two_ref, kgrad_one_ref, kgrad_two_ref, grad_one, adj, total_one, total_two):
    height = act_ref.shape[0]
    breadth = act_ref.shape[1] // count
    mid_chan = act_ref.shape[2]
    out_chan = grad_two_ref.shape[2]
    for row in range(height):
        for parity in (0, 1):
            taps = side_taps(grad_two_ref, 2 * row + parity, count, breadth)
            back = product_nt(taps, w_ref[parity])
            other = row + ROW_SHIFT[parity]
            if parity == 0 and row == 0:
                adj[0] = back[:, :mid_chan]
            else:
                adj[row] += back[:, :mid_chan]
            if 0 <= other < height:
                if parity == 0:
                    adj[other] += back[:, mid_chan:]
                else:
                    adj[other] = back[:, mid_chan:]
            mine = product_tn(act_ref[row], taps)
            if row == 0:
                total_two[parity, :mid_chan, :] = mine
            else:
                total_two[parity, :mid_chan, :] += mine
            if 0 <= other < height:
                far = product_tn(act_ref[other], taps)
                if row == (1 if parity == 0 else 0):
                    total_two[parity, mid_chan:, :] = far
                else:
                    total_two[parity, mid_chan:, :] += far
    for parity in (0, 1):
        for which in (0, 1):
            row_tap = ROW_TAPS[parity][which]
            for slot, col_tap in enumerate(COL_TAPS):
                rows = pl.ds((row_tap * 4 + col_tap) * mid_chan, mid_chan)
                kgrad_two_ref[rows, :] = total_two[
                    parity, which * mid_chan:(which + 1) * mid_chan, slot * out_chan:(slot + 1) * out_chan
                ].astype(kgrad_two_ref.dtype)
    for row in range(height):
        upstream = adj[row].astype(jnp.bfloat16).astype(jnp.float32)
        grad_one[row] = (upstream * slope_ref[row]).astype(jnp.bfloat16)
    in_chan = latent_ref.shape[1] // (H0 * W0)

    def latent_row(row):
        return jnp.concatenate(
            [latent_ref[:, pl.ds((row * W0 + col) * in_chan, in_chan)] for col in range(W0)], axis=0
        )

    for parity in (0, 1):
        for which in (0, 1):
            lefts = []
            rights = []
            for row in range(H0):
                source = row + (ROW_SHIFT[parity] if which else 0)
                if 0 <= source < H0:
                    lefts.append(latent_row(source))
                    rights.append(side_taps(grad_one, 2 * row + parity, count, W0))
            left = jnp.concatenate(lefts, axis=0) if len(lefts) > 1 else lefts[0]
            right = jnp.concatenate(rights, axis=0) if len(rights) > 1 else rights[0]
            total_one[...] = product_tn(left, right)
            row_tap = ROW_TAPS[parity][which]
            for slot, col_tap in enumerate(COL_TAPS):
                rows = pl.ds((row_tap * 4 + col_tap) * in_chan, in_chan)
                kgrad_one_ref[rows, :] = total_one[:, slot * mid_chan:(slot + 1) * mid_chan].astype(kgrad_one_ref.dtype)


def params(steps=0):
    if steps:
        return pltpu.CompilerParams(vmem_limit_bytes=VMEM_BYTES, dimension_semantics=("arbitrary",))
    return pltpu.CompilerParams(vmem_limit_bytes=VMEM_BYTES)


def forward(latent, w_one, w_two):
    count = latent.shape[0]
    mid_chan = w_two.shape[1] // 2
    out_chan = w_two.shape[2] // 4
    height, breadth = 2 * H0, 2 * W0
    return pl.pallas_call(
        functools.partial(forward_kernel, count),
        name="decoder_forward",
        out_shape=(
            jax.ShapeDtypeStruct((height, breadth * count, mid_chan), jnp.bfloat16),
            jax.ShapeDtypeStruct((height, breadth * count, mid_chan), jnp.float32),
            jax.ShapeDtypeStruct((2 * height + 2, 2 * breadth * count, out_chan), jnp.bfloat16),
            jax.ShapeDtypeStruct((2 * height, 2 * breadth * count, out_chan), jnp.float32),
        ),
        scratch_shapes=[
            pltpu.VMEM((W0 * count, 4 * mid_chan), jnp.float32),
            pltpu.VMEM((breadth * count, 4 * out_chan), jnp.float32),
        ],
        compiler_params=params(),
    )(latent, w_one, w_two)


def last_layer(act_two, slope_two, w_three, target):
    steps, rows, in_chan = slope_two.shape
    count = rows // (4 * W0)
    lanes = target.shape[2]
    whole = lambda shape: pl.BlockSpec(shape, lambda step: (0,) * len(shape))
    return pl.pallas_call(
        functools.partial(last_kernel, count),
        name="decoder_last",
        grid=(steps,),
        in_specs=[
            whole(act_two.shape),
            whole(slope_two.shape),
            whole(w_three.shape),
            pl.BlockSpec((2, rows, lanes), lambda step: (step, 0, 0)),
        ],
        out_specs=(
            pl.BlockSpec((2, rows, lanes), lambda step: (step, 0, 0)),
            whole(slope_two.shape),
            whole(w_three.shape),
        ),
        out_shape=(
            jax.ShapeDtypeStruct(target.shape, jnp.bfloat16),
            jax.ShapeDtypeStruct(slope_two.shape, jnp.bfloat16),
            jax.ShapeDtypeStruct(w_three.shape, jnp.float32),
        ),
        scratch_shapes=[
            pltpu.VMEM((rows, 2 * lanes), jnp.float32),
            pltpu.VMEM((rows + 2 * count, lanes), jnp.float32),
            pltpu.VMEM((steps + 2, rows, in_chan), jnp.float32),
        ],
        compiler_params=params(1),
    )(act_two, slope_two, w_three, target)


def backward(latent, act_one, slope_one, w_two, grad_two, kind):
    count = latent.shape[0]
    in_chan = latent.shape[1] // (H0 * W0)
    mid_chan = act_one.shape[2]
    out_chan = grad_two.shape[2]
    return pl.pallas_call(
        functools.partial(backward_kernel, count),
        name="decoder_backward",
        out_shape=(
            jax.ShapeDtypeStruct((16 * in_chan, mid_chan), kind),
            jax.ShapeDtypeStruct((16 * mid_chan, out_chan), kind),
        ),
        scratch_shapes=[
            pltpu.VMEM(act_one.shape, jnp.bfloat16),
            pltpu.VMEM(act_one.shape, jnp.float32),
            pltpu.VMEM((in_chan, 4 * mid_chan), jnp.float32),
            pltpu.VMEM(w_two.shape, jnp.float32),
        ],
        compiler_params=params(),
    )(latent, act_one, slope_one, w_two, grad_two)


def unpaired_third(paired, in_chan):
    out_chan = paired.shape[2] // 4
    view = paired.reshape(2, 2, in_chan, 4, out_chan)
    pieces = [None] * 16
    for parity in (0, 1):
        for which in (0, 1):
            for slot, col_tap in enumerate(COL_TAPS):
                pieces[ROW_TAPS[parity][which] * 4 + col_tap] = view[parity, which, :, slot, :]
    return jnp.concatenate(pieces, axis=0)


def spatial_first(grid):
    count, height, breadth, chan = grid.shape
    return (
        grid.reshape(count, height, breadth // 2, 2 * chan)
        .transpose(1, 2, 0, 3)
        .reshape(height, breadth // 2 * count, 2 * chan)
    )


def sample_first(rows, count, chan):
    height = rows.shape[0]
    return (
        rows.reshape(height, -1, count, 2 * chan)
        .transpose(2, 0, 1, 3)
        .reshape(count, height, -1, chan)
    )


def rounded(values):
    return lax.optimization_barrier(values.astype(jnp.bfloat16))


def shards(fmri, subject, ridge_maps, voxel_count, w_first, w_second, w_third, target):
    dp_count = lax.axis_size("dp")
    samp_dev = fmri.shape[0]
    vox_local = fmri.shape[1]
    capacity = max(2, 2 * samp_dev // dp_count)
    mid_chan = w_first.shape[1]
    last_chan = w_second.shape[1]
    pair_one = paired_weight(w_first, w_first.shape[0] // 16)
    pair_two = paired_weight(w_second, mid_chan)
    pair_three = paired_weight(w_third, last_chan)
    target_rows = spatial_first(target)
    owners = subject[:, 0]
    onehot = (owners[:, None] == jnp.arange(dp_count, dtype=jnp.int32)[None, :]).astype(jnp.int32)
    earlier = jnp.cumsum(onehot, axis=0) - onehot
    slot_index = jnp.sum(earlier * onehot, axis=1)
    position = owners * capacity + slot_index
    buckets = jnp.zeros((dp_count * capacity, vox_local), fmri.dtype).at[position].set(fmri)
    arrived = lax.all_to_all(
        buckets.reshape(dp_count, capacity, vox_local),
        "dp",
        split_axis=0,
        concat_axis=0,
        tiled=True,
    )
    subject_here = lax.axis_index("dp")
    voxel_ids = lax.axis_index("vox") * vox_local + jnp.arange(vox_local, dtype=jnp.int32)
    voxel_keep = (voxel_ids < voxel_count[subject_here]).astype(fmri.dtype)
    readings = arrived.reshape(dp_count * capacity, vox_local) * voxel_keep[None, :]
    partial_value = jnp.dot(readings, ridge_maps[0], preferred_element_type=jnp.float32)
    latent_part = rounded(lax.psum_scatter(partial_value, "vox", scatter_dimension=1, tiled=True))
    feat_local = latent_part.shape[1]
    returned = lax.all_to_all(
        latent_part.reshape(dp_count, capacity, feat_local),
        "dp",
        split_axis=0,
        concat_axis=0,
        tiled=True,
    )
    own_rows = returned.reshape(dp_count * capacity, feat_local)[position]
    latent = lax.all_to_all(own_rows, "vox", split_axis=0, concat_axis=1, tiled=True)
    count = latent.shape[0]
    act_one, slope_one, act_two, slope_two = forward(latent, pair_one, pair_two)
    decoded_rows, grad_two, paired_three = last_layer(act_two, slope_two, pair_three, target_rows)
    grad_first, grad_second = backward(latent, act_one, slope_one, pair_two, grad_two, jnp.float32)
    grad_third = unpaired_third(paired_three, last_chan)
    decoded = sample_first(decoded_rows, count, w_third.shape[1])
    sum_first, sum_second, sum_third = lax.psum(
        (grad_first, grad_second, grad_third), ("vox", "dp")
    )
    total_first = sum_first.astype(jnp.bfloat16)
    total_second = sum_second.astype(jnp.bfloat16)
    total_third = sum_third.astype(jnp.bfloat16)
    return (decoded, total_first, total_second, total_third)


def solution(mesh):
    placed = (
        P("dp", "vox"),
        P("dp", None),
        P("dp", "vox", None),
        P(),
        P(),
        P(),
        P(),
        P(("dp", "vox"), None, None, None),
    )
    return jax.shard_map(
        shards,
        mesh=mesh,
        in_specs=placed,
        out_specs=(P(("dp", "vox"), None, None, None), P(), P(), P()),
        check_vma=False,
    )
```

```python
import functools
import jax
import jax.numpy as jnp
from jax import lax
from jax.experimental import pallas as pl
from jax.sharding import PartitionSpec as P
from jax.experimental.pallas import tpu as pltpu

H0 = 2
W0 = 4
SAMP_DEV = 256
ROW_TAPS = ((1, 3), (2, 0))
ROW_SHIFT = (-1, 1)
COL_TAPS = (1, 2, 3, 0)
VMEM_BYTES = 60 * 1024 * 1024


def paired_weight(weights, in_chan):
    out_chan = weights.shape[1]
    kernel = weights.reshape(4, 4, in_chan, out_chan)
    halves = []
    for parity in (0, 1):
        rows = []
        for row_tap in ROW_TAPS[parity]:
            rows.append(jnp.concatenate([kernel[row_tap, col_tap] for col_tap in COL_TAPS], axis=1))
        halves.append(jnp.concatenate(rows, axis=0))
    return jnp.stack(halves)


def product(left, right):
    return jnp.dot(left, right, preferred_element_type=jnp.float32)


def product_nt(left, right):
    return lax.dot_general(left, right, (((1,), (1,)), ((), ())), preferred_element_type=jnp.float32)


def product_tn(left, right):
    return lax.dot_general(left, right, (((0,), (0,)), ((), ())), preferred_element_type=jnp.float32)


def gelu_pair(value):
    root = 0.7978845608028654
    square = value * value
    tanh = jnp.tanh(root * (value + 0.044715 * (square * value)))
    half = 0.5 * (1.0 + tanh)
    slope = half + (0.5 * value) * (1.0 - tanh * tanh) * (root + (3 * 0.044715 * root) * square)
    return value * half, slope


def up_rows(product_ref, act_ref, slope_ref, act_row, slope_row, count, breadth, out_chan):
    width = 2 * out_chan
    for col in range(breadth):
        here = pl.ds(col * count, count)
        for col_par in (0, 1):
            lanes = pl.ds(col_par * out_chan, out_chan)
            side = pl.ds(width + col_par * out_chan, out_chan)
            value = product_ref[here, lanes]
            other = col - 1 if col_par == 0 else col + 1
            if 0 <= other < breadth:
                value = value + product_ref[pl.ds(other * count, count), side]
            act, slope = gelu_pair(value)
            rows = pl.ds((2 * col + col_par) * count, count)
            act_ref[act_row, rows, :] = act.astype(jnp.bfloat16)
            slope_ref[slope_row, rows, :] = slope


def forward_kernel(count, latent_ref, w_one_ref, w_two_ref, act_one_ref, slope_one_ref, act_two_ref, slope_two_ref, tmp_one, tmp_two):
    in_chan = w_one_ref.shape[1] // 2
    mid_chan = w_two_ref.shape[1] // 2
    out_chan = w_two_ref.shape[2] // 4

    def latent_row(row):
        return jnp.concatenate(
            [latent_ref[:, pl.ds((row * W0 + col) * in_chan, in_chan)] for col in range(W0)], axis=0
        )

    for row in range(H0):
        for parity in (0, 1):
            tmp_one[...] = product(latent_row(row), w_one_ref[parity, :in_chan, :])
            other = row + ROW_SHIFT[parity]
            if 0 <= other < H0:
                tmp_one[...] += product(latent_row(other), w_one_ref[parity, in_chan:, :])
            at = 2 * row + parity
            up_rows(tmp_one, act_one_ref, slope_one_ref, at, at, count, W0, mid_chan)
    height = 2 * H0
    breadth = 2 * W0
    act_two_ref[0] = jnp.zeros_like(act_two_ref[0])
    act_two_ref[2 * height + 1] = jnp.zeros_like(act_two_ref[0])
    for row in range(height):
        for parity in (0, 1):
            tmp_two[...] = product(act_one_ref[row], w_two_ref[parity, :mid_chan, :])
            other = row + ROW_SHIFT[parity]
            if 0 <= other < height:
                tmp_two[...] += product(act_one_ref[other], w_two_ref[parity, mid_chan:, :])
            at = 2 * row + parity
            up_rows(tmp_two, act_two_ref, slope_two_ref, at + 1, at, count, breadth, out_chan)


def last_kernel(count, act_ref, slope_ref, w_ref, target_ref, decoded_ref, grad_ref, kgrad_ref, tmp, grads, adj):
    step = pl.program_id(0)
    steps = pl.num_programs(0)
    breadth = act_ref.shape[1] // count
    in_chan = act_ref.shape[2]
    lanes = 2 * (w_ref.shape[2] // 4)

    @pl.when(step == 0)
    def _():
        adj[...] = jnp.zeros_like(adj)
        kgrad_ref[...] = jnp.zeros_like(kgrad_ref)
        grads[...] = jnp.zeros_like(grads)

    low = lax.broadcasted_iota(jnp.int32, (count, lanes), 1) < lanes // 2
    for parity in (0, 1):
        other = step + 1 + ROW_SHIFT[parity]
        left = jnp.concatenate([act_ref[step + 1], act_ref[other]], axis=1)
        tmp[...] = product(left, w_ref[parity])
        zero = jnp.zeros((count, lanes), jnp.float32)
        for col in range(breadth):
            here = pl.ds(col * count, count)
            before = tmp[pl.ds((col - 1) * count, count), lanes:] if col > 0 else zero
            after = tmp[pl.ds((col + 1) * count, count), lanes:] if col < breadth - 1 else zero
            value = tmp[here, :lanes] + jnp.where(low, before, after)
            decoded_ref[parity, here, :] = value.astype(jnp.bfloat16)
            grad = (value - target_ref[parity, here, :].astype(jnp.float32)) * (1.0 / SAMP_DEV)
            grads[pl.ds((col + 1) * count, count), :] = grad
        pieces = []
        for col in range(breadth):
            before = grads[pl.ds(col * count, count), :]
            here = grads[pl.ds((col + 1) * count, count), :]
            after = grads[pl.ds((col + 2) * count, count), :]
            side = jnp.where(low, after, before)
            pieces.append(jnp.concatenate([here.astype(jnp.bfloat16), side.astype(jnp.bfloat16)], axis=1))
        taps = jnp.concatenate(pieces, axis=0)
        kgrad_ref[parity] += product_tn(left, taps)
        back = product_nt(taps, w_ref[parity])
        adj[step + 1] += back[:, :in_chan]
        adj[other] += back[:, in_chan:]

    @pl.when(step == steps - 1)
    def _():
        def finish(row, carry):
            upstream = adj[row + 1].astype(jnp.bfloat16).astype(jnp.float32)
            grad_ref[row] = (upstream * slope_ref[row]).astype(jnp.bfloat16)
            return carry

        lax.fori_loop(0, steps, finish, 0)


def side_taps(grad_ref, row, count, breadth):
    def at(col):
        if 0 <= col < 2 * breadth:
            return grad_ref[row, pl.ds(col * count, count), :]
        return jnp.zeros((count, grad_ref.shape[2]), jnp.bfloat16)

    pieces = []
    for col in range(breadth):
        pieces.append(jnp.concatenate([at(2 * col), at(2 * col + 1), at(2 * col + 2), at(2 * col - 1)], axis=1))
    return jnp.concatenate(pieces, axis=0)


def backward_kernel(count, latent_ref, act_ref, slope_ref, w_ref, grad_two_ref, kgrad_one_ref, kgrad_two_ref, grad_one, adj, total_one, total_two):
    height = act_ref.shape[0]
    breadth = act_ref.shape[1] // count
    mid_chan = act_ref.shape[2]
    out_chan = grad_two_ref.shape[2]
    for row in range(height):
        for parity in (0, 1):
            taps = side_taps(grad_two_ref, 2 * row + parity, count, breadth)
            back = product_nt(taps, w_ref[parity])
            other = row + ROW_SHIFT[parity]
            if parity == 0 and row == 0:
                adj[0] = back[:, :mid_chan]
            else:
                adj[row] += back[:, :mid_chan]
            if 0 <= other < height:
                if parity == 0:
                    adj[other] += back[:, mid_chan:]
                else:
                    adj[other] = back[:, mid_chan:]
            mine = product_tn(act_ref[row], taps)
            if row == 0:
                total_two[parity, :mid_chan, :] = mine
            else:
                total_two[parity, :mid_chan, :] += mine
            if 0 <= other < height:
                far = product_tn(act_ref[other], taps)
                if row == (1 if parity == 0 else 0):
                    total_two[parity, mid_chan:, :] = far
                else:
                    total_two[parity, mid_chan:, :] += far
    for parity in (0, 1):
        for which in (0, 1):
            row_tap = ROW_TAPS[parity][which]
            for slot, col_tap in enumerate(COL_TAPS):
                rows = pl.ds((row_tap * 4 + col_tap) * mid_chan, mid_chan)
                kgrad_two_ref[rows, :] = total_two[
                    parity, which * mid_chan:(which + 1) * mid_chan, slot * out_chan:(slot + 1) * out_chan
                ].astype(kgrad_two_ref.dtype)
    for row in range(height):
        upstream = adj[row].astype(jnp.bfloat16).astype(jnp.float32)
        grad_one[row] = (upstream * slope_ref[row]).astype(jnp.bfloat16)
    in_chan = latent_ref.shape[1] // (H0 * W0)

    def latent_row(row):
        return jnp.concatenate(
            [latent_ref[:, pl.ds((row * W0 + col) * in_chan, in_chan)] for col in range(W0)], axis=0
        )

    for parity in (0, 1):
        for which in (0, 1):
            lefts = []
            rights = []
            for row in range(H0):
                source = row + (ROW_SHIFT[parity] if which else 0)
                if 0 <= source < H0:
                    lefts.append(latent_row(source))
                    rights.append(side_taps(grad_one, 2 * row + parity, count, W0))
            left = jnp.concatenate(lefts, axis=0) if len(lefts) > 1 else lefts[0]
            right = jnp.concatenate(rights, axis=0) if len(rights) > 1 else rights[0]
            total_one[...] = product_tn(left, right)
            row_tap = ROW_TAPS[parity][which]
            for slot, col_tap in enumerate(COL_TAPS):
                rows = pl.ds((row_tap * 4 + col_tap) * in_chan, in_chan)
                kgrad_one_ref[rows, :] = total_one[:, slot * mid_chan:(slot + 1) * mid_chan].astype(kgrad_one_ref.dtype)


def params(steps=0):
    if steps:
        return pltpu.CompilerParams(vmem_limit_bytes=VMEM_BYTES, dimension_semantics=("arbitrary",))
    return pltpu.CompilerParams(vmem_limit_bytes=VMEM_BYTES)


def forward(latent, w_one, w_two):
    count = latent.shape[0]
    mid_chan = w_two.shape[1] // 2
    out_chan = w_two.shape[2] // 4
    height, breadth = 2 * H0, 2 * W0
    return pl.pallas_call(
        functools.partial(forward_kernel, count),
        name="decoder_forward",
        out_shape=(
            jax.ShapeDtypeStruct((height, breadth * count, mid_chan), jnp.bfloat16),
            jax.ShapeDtypeStruct((height, breadth * count, mid_chan), jnp.float32),
            jax.ShapeDtypeStruct((2 * height + 2, 2 * breadth * count, out_chan), jnp.bfloat16),
            jax.ShapeDtypeStruct((2 * height, 2 * breadth * count, out_chan), jnp.float32),
        ),
        scratch_shapes=[
            pltpu.VMEM((W0 * count, 4 * mid_chan), jnp.float32),
            pltpu.VMEM((breadth * count, 4 * out_chan), jnp.float32),
        ],
        compiler_params=params(),
    )(latent, w_one, w_two)


def last_layer(act_two, slope_two, w_three, target):
    steps, rows, in_chan = slope_two.shape
    count = rows // (4 * W0)
    lanes = target.shape[2]
    whole = lambda shape: pl.BlockSpec(shape, lambda step: (0,) * len(shape))
    return pl.pallas_call(
        functools.partial(last_kernel, count),
        name="decoder_last",
        grid=(steps,),
        in_specs=[
            whole(act_two.shape),
            whole(slope_two.shape),
            whole(w_three.shape),
            pl.BlockSpec((2, rows, lanes), lambda step: (step, 0, 0)),
        ],
        out_specs=(
            pl.BlockSpec((2, rows, lanes), lambda step: (step, 0, 0)),
            whole(slope_two.shape),
            whole(w_three.shape),
        ),
        out_shape=(
            jax.ShapeDtypeStruct(target.shape, jnp.bfloat16),
            jax.ShapeDtypeStruct(slope_two.shape, jnp.bfloat16),
            jax.ShapeDtypeStruct(w_three.shape, jnp.float32),
        ),
        scratch_shapes=[
            pltpu.VMEM((rows, 2 * lanes), jnp.float32),
            pltpu.VMEM((rows + 2 * count, lanes), jnp.float32),
            pltpu.VMEM((steps + 2, rows, in_chan), jnp.float32),
        ],
        compiler_params=params(1),
    )(act_two, slope_two, w_three, target)


def backward(latent, act_one, slope_one, w_two, grad_two, kind):
    count = latent.shape[0]
    in_chan = latent.shape[1] // (H0 * W0)
    mid_chan = act_one.shape[2]
    out_chan = grad_two.shape[2]
    return pl.pallas_call(
        functools.partial(backward_kernel, count),
        name="decoder_backward",
        out_shape=(
            jax.ShapeDtypeStruct((16 * in_chan, mid_chan), kind),
            jax.ShapeDtypeStruct((16 * mid_chan, out_chan), kind),
        ),
        scratch_shapes=[
            pltpu.VMEM(act_one.shape, jnp.bfloat16),
            pltpu.VMEM(act_one.shape, jnp.float32),
            pltpu.VMEM((in_chan, 4 * mid_chan), jnp.float32),
            pltpu.VMEM(w_two.shape, jnp.float32),
        ],
        compiler_params=params(),
    )(latent, act_one, slope_one, w_two, grad_two)


def unpaired_third(paired, in_chan):
    out_chan = paired.shape[2] // 4
    view = paired.reshape(2, 2, in_chan, 4, out_chan)
    pieces = [None] * 16
    for parity in (0, 1):
        for which in (0, 1):
            for slot, col_tap in enumerate(COL_TAPS):
                pieces[ROW_TAPS[parity][which] * 4 + col_tap] = view[parity, which, :, slot, :]
    return jnp.concatenate(pieces, axis=0)


def spatial_first(grid):
    count, height, breadth, chan = grid.shape
    return (
        grid.reshape(count, height, breadth // 2, 2 * chan)
        .transpose(1, 2, 0, 3)
        .reshape(height, breadth // 2 * count, 2 * chan)
    )


def sample_first(rows, count, chan):
    height = rows.shape[0]
    return (
        rows.reshape(height, -1, count, 2 * chan)
        .transpose(2, 0, 1, 3)
        .reshape(count, height, -1, chan)
    )


def rounded(values):
    return lax.optimization_barrier(values.astype(jnp.bfloat16))


def bit_pairs(axis):
    size = lax.axis_size(axis)
    bits = []
    bit = 1
    while bit < size:
        bits.append((axis, bit))
        bit *= 2
    return bits


def exchanged(values, hop):
    axis, bit = hop
    return lax.ppermute(values, axis, [(at, at ^ bit) for at in range(lax.axis_size(axis))])


def upper(hop):
    axis, bit = hop
    return (lax.axis_index(axis) // bit) % 2


def summed_share(values, hops):
    for hop in hops:
        half = values.shape[0] // 2
        side = upper(hop)
        sent = lax.dynamic_slice_in_dim(values, (1 - side) * half, half, 0).astype(jnp.bfloat16)
        kept = lax.dynamic_slice_in_dim(values, side * half, half, 0).astype(jnp.float32)
        values = kept + exchanged(sent, hop).astype(jnp.float32)
    return values


def all_shares(values, hops):
    for hop in reversed(hops):
        other = exchanged(values, hop)
        first = upper(hop) == 0
        values = jnp.concatenate(
            [jnp.where(first, values, other), jnp.where(first, other, values)], axis=0
        )
    return values


def all_summed(values, hops):
    return all_shares(summed_share(values, hops).astype(jnp.bfloat16), hops)


def shards(fmri, subject, ridge_maps, voxel_count, w_first, w_second, w_third, target):
    dp_count = lax.axis_size("dp")
    samp_dev = fmri.shape[0]
    vox_local = fmri.shape[1]
    capacity = max(2, 2 * samp_dev // dp_count)
    mid_chan = w_first.shape[1]
    last_chan = w_second.shape[1]
    owners = subject[:, 0]
    onehot = (owners[:, None] == jnp.arange(dp_count, dtype=jnp.int32)[None, :]).astype(jnp.int32)
    earlier = jnp.cumsum(onehot, axis=0) - onehot
    slot_index = jnp.sum(earlier * onehot, axis=1)
    position = owners * capacity + slot_index
    buckets = jnp.zeros((dp_count * capacity, vox_local), fmri.dtype).at[position].set(fmri)
    buckets, target, w_first, w_second, w_third = lax.optimization_barrier(
        (buckets, target, w_first, w_second, w_third)
    )
    arrived = lax.all_to_all(
        buckets.reshape(dp_count, capacity, vox_local),
        "dp",
        split_axis=0,
        concat_axis=0,
        tiled=True,
    )
    pair_one = paired_weight(w_first, w_first.shape[0] // 16)
    pair_two = paired_weight(w_second, mid_chan)
    pair_three = paired_weight(w_third, last_chan)
    target_rows = spatial_first(target)
    arrived, pair_one, pair_two, pair_three, target_rows = lax.optimization_barrier(
        (arrived, pair_one, pair_two, pair_three, target_rows)
    )
    subject_here = lax.axis_index("dp")
    voxel_ids = lax.axis_index("vox") * vox_local + jnp.arange(vox_local, dtype=jnp.int32)
    voxel_keep = (voxel_ids < voxel_count[subject_here]).astype(fmri.dtype)
    readings = arrived.reshape(dp_count * capacity, vox_local) * voxel_keep[None, :]
    partial_value = jnp.dot(readings, ridge_maps[0], preferred_element_type=jnp.float32)
    latent_part = rounded(lax.psum_scatter(partial_value, "vox", scatter_dimension=1, tiled=True))
    feat_local = latent_part.shape[1]
    returned = lax.all_to_all(
        latent_part.reshape(dp_count, capacity, feat_local),
        "dp",
        split_axis=0,
        concat_axis=0,
        tiled=True,
    )
    own_rows = returned.reshape(dp_count * capacity, feat_local)[position]
    latent = lax.all_to_all(own_rows, "vox", split_axis=0, concat_axis=1, tiled=True)
    count = latent.shape[0]
    act_one, slope_one, act_two, slope_two = forward(latent, pair_one, pair_two)
    decoded_rows, grad_two, paired_three = last_layer(act_two, slope_two, pair_three, target_rows)
    grad_first, grad_second = backward(latent, act_one, slope_one, pair_two, grad_two, jnp.bfloat16)
    vox_bits = bit_pairs("vox")
    dp_bits = bit_pairs("dp")
    core, across = vox_bits[:1], vox_bits[1:]
    near, along = dp_bits[:1], dp_bits[:0:-1]
    half = grad_first.shape[0] // 2
    lanes = grad_second.shape[1]
    flat_three = paired_three.astype(jnp.bfloat16)
    pieces = [flat_three[:, :, at:at + lanes].reshape(-1, lanes) for at in range(0, flat_three.shape[2], lanes)]
    small = jnp.concatenate([grad_second] + pieces, axis=0)
    small = all_summed(small, core + along + across + near)
    upper_half = all_summed(grad_first[:half], core + across + near + along)
    lower_half = all_summed(grad_first[half:], core + near + across + along)
    total_first = jnp.concatenate([upper_half, lower_half], axis=0)
    total_second = small[: grad_second.shape[0]]
    tail = small[grad_second.shape[0]:].reshape(len(pieces), 2, -1, lanes)
    total_third = unpaired_third(jnp.concatenate([tail[at] for at in range(len(pieces))], axis=2), last_chan)
    decoded = sample_first(decoded_rows, count, w_third.shape[1])
    return (decoded, total_first, total_second, total_third)


def solution(mesh):
    placed = (
        P("dp", "vox"),
        P("dp", None),
        P("dp", "vox", None),
        P(),
        P(),
        P(),
        P(),
        P(("dp", "vox"), None, None, None),
    )
    return jax.shard_map(
        shards,
        mesh=mesh,
        in_specs=placed,
        out_specs=(P(("dp", "vox"), None, None, None), P(), P(), P()),
        check_vma=False,
    )
```

```python
import functools
import jax
import jax.numpy as jnp
from jax import lax
from jax.experimental import pallas as pl
from jax.sharding import PartitionSpec as P
from jax.experimental.pallas import tpu as pltpu

H0 = 2
W0 = 4
SAMP_DEV = 256
ROW_TAPS = ((1, 3), (2, 0))
ROW_SHIFT = (-1, 1)
COL_TAPS = (1, 2, 3, 0)
VMEM_BYTES = 60 * 1024 * 1024


def paired_weight(weights, in_chan):
    out_chan = weights.shape[1]
    kernel = weights.reshape(4, 4, in_chan, out_chan)
    halves = []
    for parity in (0, 1):
        rows = []
        for row_tap in ROW_TAPS[parity]:
            rows.append(jnp.concatenate([kernel[row_tap, col_tap] for col_tap in COL_TAPS], axis=1))
        halves.append(jnp.concatenate(rows, axis=0))
    return jnp.stack(halves)


def product(left, right):
    return jnp.dot(left, right, preferred_element_type=jnp.float32)


def product_nt(left, right):
    return lax.dot_general(left, right, (((1,), (1,)), ((), ())), preferred_element_type=jnp.float32)


def product_tn(left, right):
    return lax.dot_general(left, right, (((0,), (0,)), ((), ())), preferred_element_type=jnp.float32)


def gelu_pair(value):
    root = 0.7978845608028654
    square = value * value
    tanh = jnp.tanh(root * (value + 0.044715 * (square * value)))
    half = 0.5 * (1.0 + tanh)
    slope = half + (0.5 * value) * (1.0 - tanh * tanh) * (root + (3 * 0.044715 * root) * square)
    return value * half, slope


def up_rows(product_ref, act_ref, slope_ref, act_row, slope_row, count, breadth, out_chan):
    width = 2 * out_chan
    for col in range(breadth):
        here = pl.ds(col * count, count)
        for col_par in (0, 1):
            lanes = pl.ds(col_par * out_chan, out_chan)
            side = pl.ds(width + col_par * out_chan, out_chan)
            value = product_ref[here, lanes]
            other = col - 1 if col_par == 0 else col + 1
            if 0 <= other < breadth:
                value = value + product_ref[pl.ds(other * count, count), side]
            act, slope = gelu_pair(value)
            rows = pl.ds((2 * col + col_par) * count, count)
            act_ref[act_row, rows, :] = act.astype(jnp.bfloat16)
            slope_ref[slope_row, rows, :] = slope


def holder_of(block, holders):
    bits = holders.bit_length() - 1
    depth = (H0 * W0).bit_length() - 1
    owner = sum(((block >> (depth - 1 - at)) & 1) << at for at in range(bits))
    return owner, block & (2 ** (depth - bits) - 1)


def latent_row(latent_ref, row):
    holders = latent_ref.shape[0]
    width = latent_ref.shape[2] * holders // (H0 * W0)
    pieces = []
    for col in range(W0):
        owner, place = holder_of(row * W0 + col, holders)
        pieces.append(latent_ref[owner, :, pl.ds(place * width, width)])
    return jnp.concatenate(pieces, axis=0)


def forward_kernel(count, latent_ref, w_one_ref, w_two_ref, act_one_ref, slope_one_ref, act_two_ref, slope_two_ref, tmp_one, tmp_two):
    in_chan = w_one_ref.shape[0] // 16
    mid_chan = w_two_ref.shape[1] // 2
    out_chan = w_two_ref.shape[2] // 4

    for row in range(H0):
        for parity in (0, 1):
            other = row + ROW_SHIFT[parity]
            for slot, col_tap in enumerate(COL_TAPS):
                lanes = pl.ds(slot * mid_chan, mid_chan)
                taps = pl.ds((ROW_TAPS[parity][0] * 4 + col_tap) * in_chan, in_chan)
                value = product(latent_row(latent_ref, row), w_one_ref[taps, :])
                if 0 <= other < H0:
                    taps = pl.ds((ROW_TAPS[parity][1] * 4 + col_tap) * in_chan, in_chan)
                    value = value + product(latent_row(latent_ref, other), w_one_ref[taps, :])
                tmp_one[:, lanes] = value
            at = 2 * row + parity
            up_rows(tmp_one, act_one_ref, slope_one_ref, at, at, count, W0, mid_chan)
    height = 2 * H0
    breadth = 2 * W0
    act_two_ref[0] = jnp.zeros_like(act_two_ref[0])
    act_two_ref[2 * height + 1] = jnp.zeros_like(act_two_ref[0])
    for row in range(height):
        for parity in (0, 1):
            tmp_two[...] = product(act_one_ref[row], w_two_ref[parity, :mid_chan, :])
            other = row + ROW_SHIFT[parity]
            if 0 <= other < height:
                tmp_two[...] += product(act_one_ref[other], w_two_ref[parity, mid_chan:, :])
            at = 2 * row + parity
            up_rows(tmp_two, act_two_ref, slope_two_ref, at + 1, at, count, breadth, out_chan)


def last_kernel(count, act_ref, slope_ref, w_ref, target_ref, decoded_ref, grad_ref, kgrad_ref, tmp, grads, adj):
    step = pl.program_id(0)
    steps = pl.num_programs(0)
    breadth = act_ref.shape[1] // count
    in_chan = act_ref.shape[2]
    lanes = 2 * (w_ref.shape[2] // 4)

    @pl.when(step == 0)
    def _():
        adj[...] = jnp.zeros_like(adj)
        kgrad_ref[...] = jnp.zeros_like(kgrad_ref)
        grads[...] = jnp.zeros_like(grads)

    low = lax.broadcasted_iota(jnp.int32, (count, lanes), 1) < lanes // 2
    for parity in (0, 1):
        other = step + 1 + ROW_SHIFT[parity]
        left = jnp.concatenate([act_ref[step + 1], act_ref[other]], axis=1)
        tmp[...] = product(left, w_ref[parity])
        zero = jnp.zeros((count, lanes), jnp.float32)
        for col in range(breadth):
            here = pl.ds(col * count, count)
            before = tmp[pl.ds((col - 1) * count, count), lanes:] if col > 0 else zero
            after = tmp[pl.ds((col + 1) * count, count), lanes:] if col < breadth - 1 else zero
            value = tmp[here, :lanes] + jnp.where(low, before, after)
            decoded_ref[parity, here, :] = value.astype(jnp.bfloat16)
            grad = (value - target_ref[parity, here, :].astype(jnp.float32)) * (1.0 / SAMP_DEV)
            grads[pl.ds((col + 1) * count, count), :] = grad
        pieces = []
        for col in range(breadth):
            before = grads[pl.ds(col * count, count), :]
            here = grads[pl.ds((col + 1) * count, count), :]
            after = grads[pl.ds((col + 2) * count, count), :]
            side = jnp.where(low, after, before)
            pieces.append(jnp.concatenate([here.astype(jnp.bfloat16), side.astype(jnp.bfloat16)], axis=1))
        taps = jnp.concatenate(pieces, axis=0)
        kgrad_ref[parity] += product_tn(left, taps)
        back = product_nt(taps, w_ref[parity])
        adj[step + 1] += back[:, :in_chan]
        adj[other] += back[:, in_chan:]

    @pl.when(step == steps - 1)
    def _():
        def finish(row, carry):
            upstream = adj[row + 1].astype(jnp.bfloat16).astype(jnp.float32)
            grad_ref[row] = (upstream * slope_ref[row]).astype(jnp.bfloat16)
            return carry

        lax.fori_loop(0, steps, finish, 0)


def side_taps(grad_ref, row, count, breadth):
    def at(col):
        if 0 <= col < 2 * breadth:
            return grad_ref[row, pl.ds(col * count, count), :]
        return jnp.zeros((count, grad_ref.shape[2]), jnp.bfloat16)

    pieces = []
    for col in range(breadth):
        pieces.append(jnp.concatenate([at(2 * col), at(2 * col + 1), at(2 * col + 2), at(2 * col - 1)], axis=1))
    return jnp.concatenate(pieces, axis=0)


def backward_kernel(count, latent_ref, act_ref, slope_ref, w_ref, grad_two_ref, kgrad_one_ref, kgrad_two_ref, grad_one, adj, total_one, total_two):
    height = act_ref.shape[0]
    breadth = act_ref.shape[1] // count
    mid_chan = act_ref.shape[2]
    out_chan = grad_two_ref.shape[2]
    for row in range(height):
        for parity in (0, 1):
            taps = side_taps(grad_two_ref, 2 * row + parity, count, breadth)
            back = product_nt(taps, w_ref[parity])
            other = row + ROW_SHIFT[parity]
            if parity == 0 and row == 0:
                adj[0] = back[:, :mid_chan]
            else:
                adj[row] += back[:, :mid_chan]
            if 0 <= other < height:
                if parity == 0:
                    adj[other] += back[:, mid_chan:]
                else:
                    adj[other] = back[:, mid_chan:]
            mine = product_tn(act_ref[row], taps)
            if row == 0:
                total_two[parity, :mid_chan, :] = mine
            else:
                total_two[parity, :mid_chan, :] += mine
            if 0 <= other < height:
                far = product_tn(act_ref[other], taps)
                if row == (1 if parity == 0 else 0):
                    total_two[parity, mid_chan:, :] = far
                else:
                    total_two[parity, mid_chan:, :] += far
    for parity in (0, 1):
        for which in (0, 1):
            row_tap = ROW_TAPS[parity][which]
            for slot, col_tap in enumerate(COL_TAPS):
                rows = pl.ds((row_tap * 4 + col_tap) * mid_chan, mid_chan)
                kgrad_two_ref[rows, :] = total_two[
                    parity, which * mid_chan:(which + 1) * mid_chan, slot * out_chan:(slot + 1) * out_chan
                ].astype(kgrad_two_ref.dtype)
    for row in range(height):
        upstream = adj[row].astype(jnp.bfloat16).astype(jnp.float32)
        grad_one[row] = (upstream * slope_ref[row]).astype(jnp.bfloat16)
    in_chan = latent_ref.shape[0] * latent_ref.shape[2] // (H0 * W0)
    for parity in (0, 1):
        for which in (0, 1):
            lefts = []
            rights = []
            for row in range(H0):
                source = row + (ROW_SHIFT[parity] if which else 0)
                if 0 <= source < H0:
                    lefts.append(latent_row(latent_ref, source))
                    rights.append(side_taps(grad_one, 2 * row + parity, count, W0))
            left = jnp.concatenate(lefts, axis=0) if len(lefts) > 1 else lefts[0]
            right = jnp.concatenate(rights, axis=0) if len(rights) > 1 else rights[0]
            total_one[...] = product_tn(left, right)
            row_tap = ROW_TAPS[parity][which]
            for slot, col_tap in enumerate(COL_TAPS):
                rows = pl.ds((row_tap * 4 + col_tap) * in_chan, in_chan)
                kgrad_one_ref[rows, :] = total_one[:, slot * mid_chan:(slot + 1) * mid_chan].astype(kgrad_one_ref.dtype)


def params(steps=0):
    if steps:
        return pltpu.CompilerParams(vmem_limit_bytes=VMEM_BYTES, dimension_semantics=("arbitrary",))
    return pltpu.CompilerParams(vmem_limit_bytes=VMEM_BYTES)


def forward(latent, w_one, w_two):
    count = latent.shape[1]
    mid_chan = w_two.shape[1] // 2
    out_chan = w_two.shape[2] // 4
    height, breadth = 2 * H0, 2 * W0
    return pl.pallas_call(
        functools.partial(forward_kernel, count),
        name="decoder_forward",
        out_shape=(
            jax.ShapeDtypeStruct((height, breadth * count, mid_chan), jnp.bfloat16),
            jax.ShapeDtypeStruct((height, breadth * count, mid_chan), jnp.float32),
            jax.ShapeDtypeStruct((2 * height + 2, 2 * breadth * count, out_chan), jnp.bfloat16),
            jax.ShapeDtypeStruct((2 * height, 2 * breadth * count, out_chan), jnp.float32),
        ),
        scratch_shapes=[
            pltpu.VMEM((W0 * count, 4 * mid_chan), jnp.float32),
            pltpu.VMEM((breadth * count, 4 * out_chan), jnp.float32),
        ],
        compiler_params=params(),
    )(latent, w_one, w_two)


def last_layer(act_two, slope_two, w_three, target):
    steps, rows, in_chan = slope_two.shape
    count = rows // (4 * W0)
    lanes = target.shape[2]
    whole = lambda shape: pl.BlockSpec(shape, lambda step: (0,) * len(shape))
    return pl.pallas_call(
        functools.partial(last_kernel, count),
        name="decoder_last",
        grid=(steps,),
        in_specs=[
            whole(act_two.shape),
            whole(slope_two.shape),
            whole(w_three.shape),
            pl.BlockSpec((2, rows, lanes), lambda step: (step, 0, 0)),
        ],
        out_specs=(
            pl.BlockSpec((2, rows, lanes), lambda step: (step, 0, 0)),
            whole(slope_two.shape),
            whole(w_three.shape),
        ),
        out_shape=(
            jax.ShapeDtypeStruct(target.shape, jnp.bfloat16),
            jax.ShapeDtypeStruct(slope_two.shape, jnp.bfloat16),
            jax.ShapeDtypeStruct(w_three.shape, jnp.float32),
        ),
        scratch_shapes=[
            pltpu.VMEM((rows, 2 * lanes), jnp.float32),
            pltpu.VMEM((rows + 2 * count, lanes), jnp.float32),
            pltpu.VMEM((steps + 2, rows, in_chan), jnp.float32),
        ],
        compiler_params=params(1),
    )(act_two, slope_two, w_three, target)


def backward(latent, act_one, slope_one, w_two, grad_two, kind):
    count = latent.shape[1]
    in_chan = latent.shape[0] * latent.shape[2] // (H0 * W0)
    mid_chan = act_one.shape[2]
    out_chan = grad_two.shape[2]
    return pl.pallas_call(
        functools.partial(backward_kernel, count),
        name="decoder_backward",
        out_shape=(
            jax.ShapeDtypeStruct((16 * in_chan, mid_chan), kind),
            jax.ShapeDtypeStruct((16 * mid_chan, out_chan), kind),
        ),
        scratch_shapes=[
            pltpu.VMEM(act_one.shape, jnp.bfloat16),
            pltpu.VMEM(act_one.shape, jnp.float32),
            pltpu.VMEM((in_chan, 4 * mid_chan), jnp.float32),
            pltpu.VMEM(w_two.shape, jnp.float32),
        ],
        compiler_params=params(),
    )(latent, act_one, slope_one, w_two, grad_two)


def unpaired_third(paired, in_chan):
    out_chan = paired.shape[2] // 4
    view = paired.reshape(2, 2, in_chan, 4, out_chan)
    pieces = [None] * 16
    for parity in (0, 1):
        for which in (0, 1):
            for slot, col_tap in enumerate(COL_TAPS):
                pieces[ROW_TAPS[parity][which] * 4 + col_tap] = view[parity, which, :, slot, :]
    return jnp.concatenate(pieces, axis=0)


def spatial_first(grid):
    count, height, breadth, chan = grid.shape
    return (
        grid.reshape(count, height, breadth // 2, 2 * chan)
        .transpose(1, 2, 0, 3)
        .reshape(height, breadth // 2 * count, 2 * chan)
    )


def sample_first(rows, count, chan):
    height = rows.shape[0]
    return (
        rows.reshape(height, -1, count, 2 * chan)
        .transpose(2, 0, 1, 3)
        .reshape(count, height, -1, chan)
    )


def bucket_kernel(subject_ref, count_ref, shift_ref, fmri_ref, first_ref, second_ref, place_ref):
    samples, voxels = fmri_ref.shape
    slots = first_ref.shape[0]
    subjects = count_ref.shape[0]
    room = slots // subjects
    owner = subject_ref[...]
    lane = lax.broadcasted_iota(jnp.int32, (samples, 128), 1)
    onehot = jnp.where(owner == lane, 1.0, 0.0)
    row = lax.broadcasted_iota(jnp.int32, (samples, samples), 0)
    col = lax.broadcasted_iota(jnp.int32, (samples, samples), 1)
    before = jnp.where(col < row, 1.0, 0.0).astype(jnp.bfloat16)
    earlier = product(before, onehot.astype(jnp.bfloat16))
    rank = jnp.sum(earlier * onehot, axis=1, keepdims=True).astype(jnp.int32)
    position = owner * room + rank + jnp.where(rank >= room, slots - room, 0)
    slot = lax.broadcasted_iota(jnp.int32, (samples, 2 * slots), 1)
    place_ref[...] = jnp.where(slot == position, 1.0, 0.0).astype(jnp.bfloat16)
    voxel = lax.broadcasted_iota(jnp.int32, (room, voxels), 1) + shift_ref[0]
    for half, out_ref in enumerate((first_ref, second_ref)):
        for target in range(subjects):
            here = pl.ds(half * slots + target * room, room)
            if room * target % 128 == 0:
                width = min(128, slots)
                rows = product_tn(place_ref[:, pl.ds(half * slots + target * room, width)], fmri_ref[...])
                for inner in range(width // room):
                    keep = voxel < count_ref[target + inner]
                    kept = jnp.where(keep, rows[inner * room:(inner + 1) * room], 0.0)
                    out_ref[pl.ds((target + inner) * room, room), :] = kept.astype(jnp.bfloat16)


def bucketed(subject, voxel_count, shift, fmri, slots):
    samples, voxels = fmri.shape
    vmem = pl.BlockSpec(memory_space=pltpu.VMEM)
    smem = pl.BlockSpec(memory_space=pltpu.SMEM)
    return pl.pallas_call(
        bucket_kernel,
        name="bucket_rows",
        in_specs=[vmem, smem, smem, vmem],
        out_specs=(vmem, vmem, vmem),
        out_shape=(
            jax.ShapeDtypeStruct((slots, voxels), jnp.bfloat16),
            jax.ShapeDtypeStruct((slots, voxels), jnp.bfloat16),
            jax.ShapeDtypeStruct((samples, 2 * slots), jnp.bfloat16),
        ),
        compiler_params=params(),
    )(subject, voxel_count, shift, fmri)


def project_kernel(rows_ref, map_ref, out_ref):
    out_ref[0] = product(rows_ref[...], map_ref[0]).astype(jnp.bfloat16)


def projected(rows, maps):
    count, voxels = rows.shape
    blocks = H0 * W0
    width = maps.shape[2] // blocks
    return pl.pallas_call(
        project_kernel,
        name="project_rows",
        grid=(blocks,),
        in_specs=[
            pl.BlockSpec((count, voxels), lambda step: (0, 0)),
            pl.BlockSpec((1, voxels, width), lambda step: (0, 0, step)),
        ],
        out_specs=pl.BlockSpec((1, count, width), lambda step: (step, 0, 0)),
        out_shape=jax.ShapeDtypeStruct((blocks, count, width), jnp.bfloat16),
        compiler_params=params(1),
        cost_estimate=pl.CostEstimate(
            flops=2 * count * voxels * maps.shape[2],
            bytes_accessed=2 * voxels * maps.shape[2],
            transcendentals=0,
        ),
    )(rows, maps)


def collect_kernel(place_ref, first_ref, second_ref, out_ref):
    subjects, blocks, room, width = first_ref.shape
    for block in range(blocks):
        rows = [ref[subject, block] for ref in (first_ref, second_ref) for subject in range(subjects)]
        value = product(place_ref[...], jnp.concatenate(rows, axis=0))
        out_ref[:, pl.ds(block * width, width)] = value.astype(jnp.bfloat16)


def collected(place, first, second):
    samples = place.shape[0]
    return pl.pallas_call(
        collect_kernel,
        name="collect_rows",
        out_shape=jax.ShapeDtypeStruct((samples, first.shape[1] * first.shape[3]), jnp.bfloat16),
        compiler_params=params(),
    )(place, first, second)


def rounded(values):
    return lax.optimization_barrier(values.astype(jnp.bfloat16))


def bit_pairs(axis):
    size = lax.axis_size(axis)
    bits = []
    bit = 1
    while bit < size:
        bits.append((axis, bit))
        bit *= 2
    return bits


def exchanged(values, hop):
    axis, bit = hop
    return lax.ppermute(values, axis, [(at, at ^ bit) for at in range(lax.axis_size(axis))])


def upper(hop):
    axis, bit = hop
    return (lax.axis_index(axis) // bit) % 2


def summed_share(values, hops):
    for hop in hops:
        half = values.shape[0] // 2
        side = upper(hop)
        sent = lax.dynamic_slice_in_dim(values, (1 - side) * half, half, 0).astype(jnp.bfloat16)
        kept = lax.dynamic_slice_in_dim(values, side * half, half, 0).astype(jnp.float32)
        values = kept + exchanged(sent, hop).astype(jnp.float32)
    return values


def all_shares(values, hops):
    for hop in reversed(hops):
        other = exchanged(values, hop)
        first = upper(hop) == 0
        values = jnp.concatenate(
            [jnp.where(first, values, other), jnp.where(first, other, values)], axis=0
        )
    return values


def all_summed(values, hops):
    return all_shares(summed_share(values, hops).astype(jnp.bfloat16), hops)


def shards(fmri, subject, ridge_maps, voxel_count, w_first, w_second, w_third, target):
    dp_count = lax.axis_size("dp")
    samp_dev = fmri.shape[0]
    vox_local = fmri.shape[1]
    mid_chan = w_first.shape[1]
    last_chan = w_second.shape[1]
    slots = samp_dev
    room = slots // dp_count
    vox_bits = bit_pairs("vox")
    dp_bits = bit_pairs("dp")
    shift = (lax.axis_index("vox") * vox_local).astype(jnp.int32).reshape(1)
    first, second, place = bucketed(subject, voxel_count, shift, fmri, slots)
    first, second, target, w_second, w_third = lax.optimization_barrier(
        (first, second, target, w_second, w_third)
    )

    def routed(rows):
        sent = rows.reshape(dp_count, room, rows.shape[1])
        return lax.all_to_all(sent, "dp", split_axis=0, concat_axis=0, tiled=True).reshape(rows.shape)

    def returned(rows):
        partial_value = projected(rows, ridge_maps)
        latent_part = rounded(summed_share(partial_value, vox_bits))
        blocks, _, width = latent_part.shape
        sent = latent_part.reshape(blocks, dp_count, room, width).swapaxes(0, 1)
        return lax.all_to_all(sent, "dp", split_axis=0, concat_axis=0, tiled=True)

    first = routed(first)
    second = routed(second)
    pair_two = paired_weight(w_second, mid_chan)
    pair_three = paired_weight(w_third, last_chan)
    target_rows = spatial_first(target)
    second, pair_two, pair_three, target_rows = lax.optimization_barrier(
        (second, pair_two, pair_three, target_rows)
    )
    own_rows = collected(place, returned(first), returned(second))
    holders = lax.axis_size("vox")
    own_rows = own_rows.reshape(holders, samp_dev // holders, own_rows.shape[1])
    latent = lax.all_to_all(own_rows, "vox", split_axis=0, concat_axis=0, tiled=True)
    count = latent.shape[1]
    act_one, slope_one, act_two, slope_two = forward(latent, w_first, pair_two)
    decoded_rows, grad_two, paired_three = last_layer(act_two, slope_two, pair_three, target_rows)
    grad_first, grad_second = backward(latent, act_one, slope_one, pair_two, grad_two, jnp.bfloat16)
    core, across = vox_bits[:1], vox_bits[1:]
    near, along = dp_bits[:1], dp_bits[:0:-1]
    half = grad_first.shape[0] // 2
    lanes = grad_second.shape[1]
    flat_three = paired_three.astype(jnp.bfloat16)
    pieces = [flat_three[:, :, at:at + lanes].reshape(-1, lanes) for at in range(0, flat_three.shape[2], lanes)]
    small = jnp.concatenate([grad_second] + pieces, axis=0)
    small = all_summed(small, core + along + across + near)
    upper_half = all_summed(grad_first[:half], core + across + near + along)
    lower_half = all_summed(grad_first[half:], core + near + across + along)
    total_first = jnp.concatenate([upper_half, lower_half], axis=0)
    total_second = small[: grad_second.shape[0]]
    tail = small[grad_second.shape[0]:].reshape(len(pieces), 2, -1, lanes)
    total_third = unpaired_third(jnp.concatenate([tail[at] for at in range(len(pieces))], axis=2), last_chan)
    decoded = sample_first(decoded_rows, count, w_third.shape[1])
    return (decoded, total_first, total_second, total_third)


def solution(mesh):
    placed = (
        P("dp", "vox"),
        P("dp", None),
        P("dp", "vox", None),
        P(),
        P(),
        P(),
        P(),
        P(("dp", "vox"), None, None, None),
    )
    return jax.shard_map(
        shards,
        mesh=mesh,
        in_specs=placed,
        out_specs=(P(("dp", "vox"), None, None, None), P(), P(), P()),
        check_vma=False,
    )
```

```python
import functools
import jax
import jax.numpy as jnp
from jax import lax
from jax.experimental import pallas as pl
from jax.sharding import PartitionSpec as P
from jax.experimental.pallas import tpu as pltpu

H0 = 2
W0 = 4
SAMP_DEV = 256
ROW_TAPS = ((1, 3), (2, 0))
ROW_SHIFT = (-1, 1)
COL_TAPS = (1, 2, 3, 0)
VMEM_BYTES = 60 * 1024 * 1024


def paired_weight(weights, in_chan):
    out_chan = weights.shape[1]
    kernel = weights.reshape(4, 4, in_chan, out_chan)
    halves = []
    for parity in (0, 1):
        rows = []
        for row_tap in ROW_TAPS[parity]:
            rows.append(jnp.concatenate([kernel[row_tap, col_tap] for col_tap in COL_TAPS], axis=1))
        halves.append(jnp.concatenate(rows, axis=0))
    return jnp.stack(halves)


def product(left, right):
    return jnp.dot(left, right, preferred_element_type=jnp.float32)


def product_nt(left, right):
    return lax.dot_general(left, right, (((1,), (1,)), ((), ())), preferred_element_type=jnp.float32)


def product_tn(left, right):
    return lax.dot_general(left, right, (((0,), (0,)), ((), ())), preferred_element_type=jnp.float32)


def gelu_pair(value):
    root = 0.7978845608028654
    square = value * value
    tanh = jnp.tanh(root * (value + 0.044715 * (square * value)))
    half = 0.5 * (1.0 + tanh)
    slope = half + (0.5 * value) * (1.0 - tanh * tanh) * (root + (3 * 0.044715 * root) * square)
    return value * half, slope


def up_rows(product_ref, act_ref, slope_ref, act_row, slope_row, count, breadth, out_chan):
    width = 2 * out_chan
    for col in range(breadth):
        here = pl.ds(col * count, count)
        for col_par in (0, 1):
            lanes = pl.ds(col_par * out_chan, out_chan)
            side = pl.ds(width + col_par * out_chan, out_chan)
            value = product_ref[here, lanes]
            other = col - 1 if col_par == 0 else col + 1
            if 0 <= other < breadth:
                value = value + product_ref[pl.ds(other * count, count), side]
            act, slope = gelu_pair(value)
            rows = pl.ds((2 * col + col_par) * count, count)
            act_ref[act_row, rows, :] = act.astype(jnp.bfloat16)
            slope_ref[slope_row, rows, :] = slope


def holder_of(block, holders):
    bits = holders.bit_length() - 1
    depth = (H0 * W0).bit_length() - 1
    owner = sum(((block >> (depth - 1 - at)) & 1) << at for at in range(bits))
    return owner, block & (2 ** (depth - bits) - 1)


def latent_row(latent_ref, row):
    holders = latent_ref.shape[0]
    width = latent_ref.shape[2] * holders // (H0 * W0)
    pieces = []
    for col in range(W0):
        owner, place = holder_of(row * W0 + col, holders)
        pieces.append(latent_ref[owner, :, pl.ds(place * width, width)])
    return jnp.concatenate(pieces, axis=0)


def forward_kernel(count, latent_ref, w_one_ref, w_two_ref, act_one_ref, slope_one_ref, act_two_ref, slope_two_ref, tmp_one, tmp_two):
    in_chan = w_one_ref.shape[0] // 16
    mid_chan = w_two_ref.shape[1] // 2
    out_chan = w_two_ref.shape[2] // 4

    for row in range(H0):
        for parity in (0, 1):
            other = row + ROW_SHIFT[parity]
            for slot, col_tap in enumerate(COL_TAPS):
                lanes = pl.ds(slot * mid_chan, mid_chan)
                taps = pl.ds((ROW_TAPS[parity][0] * 4 + col_tap) * in_chan, in_chan)
                value = product(latent_row(latent_ref, row), w_one_ref[taps, :])
                if 0 <= other < H0:
                    taps = pl.ds((ROW_TAPS[parity][1] * 4 + col_tap) * in_chan, in_chan)
                    value = value + product(latent_row(latent_ref, other), w_one_ref[taps, :])
                tmp_one[:, lanes] = value
            at = 2 * row + parity
            up_rows(tmp_one, act_one_ref, slope_one_ref, at, at, count, W0, mid_chan)
    height = 2 * H0
    breadth = 2 * W0
    act_two_ref[0] = jnp.zeros_like(act_two_ref[0])
    act_two_ref[2 * height + 1] = jnp.zeros_like(act_two_ref[0])
    for row in range(height):
        for parity in (0, 1):
            tmp_two[...] = product(act_one_ref[row], w_two_ref[parity, :mid_chan, :])
            other = row + ROW_SHIFT[parity]
            if 0 <= other < height:
                tmp_two[...] += product(act_one_ref[other], w_two_ref[parity, mid_chan:, :])
            at = 2 * row + parity
            up_rows(tmp_two, act_two_ref, slope_two_ref, at + 1, at, count, breadth, out_chan)


def last_kernel(count, act_ref, slope_ref, w_ref, target_ref, decoded_ref, grad_ref, kgrad_ref, tmp, grads, adj):
    step = pl.program_id(0)
    steps = pl.num_programs(0)
    breadth = act_ref.shape[1] // count
    in_chan = act_ref.shape[2]
    lanes = 2 * (w_ref.shape[2] // 4)

    @pl.when(step == 0)
    def _():
        adj[...] = jnp.zeros_like(adj)
        kgrad_ref[...] = jnp.zeros_like(kgrad_ref)
        grads[...] = jnp.zeros_like(grads)

    low = lax.broadcasted_iota(jnp.int32, (count, lanes), 1) < lanes // 2
    for parity in (0, 1):
        other = step + 1 + ROW_SHIFT[parity]
        left = jnp.concatenate([act_ref[step + 1], act_ref[other]], axis=1)
        tmp[...] = product(left, w_ref[parity])
        zero = jnp.zeros((count, lanes), jnp.float32)
        for col in range(breadth):
            here = pl.ds(col * count, count)
            before = tmp[pl.ds((col - 1) * count, count), lanes:] if col > 0 else zero
            after = tmp[pl.ds((col + 1) * count, count), lanes:] if col < breadth - 1 else zero
            value = tmp[here, :lanes] + jnp.where(low, before, after)
            decoded_ref[parity, here, :] = value.astype(jnp.bfloat16)
            grad = (value - target_ref[parity, here, :].astype(jnp.float32)) * (1.0 / SAMP_DEV)
            grads[pl.ds((col + 1) * count, count), :] = grad
        pieces = []
        for col in range(breadth):
            before = grads[pl.ds(col * count, count), :]
            here = grads[pl.ds((col + 1) * count, count), :]
            after = grads[pl.ds((col + 2) * count, count), :]
            side = jnp.where(low, after, before)
            pieces.append(jnp.concatenate([here.astype(jnp.bfloat16), side.astype(jnp.bfloat16)], axis=1))
        taps = jnp.concatenate(pieces, axis=0)
        kgrad_ref[parity] += product_tn(left, taps)
        back = product_nt(taps, w_ref[parity])
        adj[step + 1] += back[:, :in_chan]
        adj[other] += back[:, in_chan:]

    @pl.when(step == steps - 1)
    def _():
        def finish(row, carry):
            upstream = adj[row + 1].astype(jnp.bfloat16).astype(jnp.float32)
            grad_ref[row] = (upstream * slope_ref[row]).astype(jnp.bfloat16)
            return carry

        lax.fori_loop(0, steps, finish, 0)


def side_taps(grad_ref, row, count, breadth):
    def at(col):
        if 0 <= col < 2 * breadth:
            return grad_ref[row, pl.ds(col * count, count), :]
        return jnp.zeros((count, grad_ref.shape[2]), jnp.bfloat16)

    pieces = []
    for col in range(breadth):
        pieces.append(jnp.concatenate([at(2 * col), at(2 * col + 1), at(2 * col + 2), at(2 * col - 1)], axis=1))
    return jnp.concatenate(pieces, axis=0)


def backward_kernel(count, side_ref, latent_ref, act_ref, slope_ref, w_ref, grad_two_ref, third_ref, kept_ref, sent_ref, grad_one, adj, total_one, total_two):
    side = side_ref[0]

    def put(half, rows, values):
        @pl.when(side == half)
        def _():
            kept_ref[rows, :] = values().astype(jnp.bfloat16)

        @pl.when(side != half)
        def _():
            sent_ref[rows, :] = values().astype(jnp.bfloat16)

    height = act_ref.shape[0]
    breadth = act_ref.shape[1] // count
    mid_chan = act_ref.shape[2]
    out_chan = grad_two_ref.shape[2]
    for row in range(height):
        for parity in (0, 1):
            taps = side_taps(grad_two_ref, 2 * row + parity, count, breadth)
            back = product_nt(taps, w_ref[parity])
            other = row + ROW_SHIFT[parity]
            if parity == 0 and row == 0:
                adj[0] = back[:, :mid_chan]
            else:
                adj[row] += back[:, :mid_chan]
            if 0 <= other < height:
                if parity == 0:
                    adj[other] += back[:, mid_chan:]
                else:
                    adj[other] = back[:, mid_chan:]
            mine = product_tn(act_ref[row], taps)
            if row == 0:
                total_two[parity, :mid_chan, :] = mine
            else:
                total_two[parity, :mid_chan, :] += mine
            if 0 <= other < height:
                far = product_tn(act_ref[other], taps)
                if row == (1 if parity == 0 else 0):
                    total_two[parity, mid_chan:, :] = far
                else:
                    total_two[parity, mid_chan:, :] += far
    for row in range(height):
        upstream = adj[row].astype(jnp.bfloat16).astype(jnp.float32)
        grad_one[row] = (upstream * slope_ref[row]).astype(jnp.bfloat16)
    in_chan = latent_ref.shape[0] * latent_ref.shape[2] // (H0 * W0)
    tail = 8 * in_chan
    lanes = 2 * out_chan
    for parity in (0, 1):
        for which in (0, 1):
            for pair in (0, 1):
                rows = pl.ds(tail + (2 * which + pair) * mid_chan, mid_chan)
                above, left_edge = which * mid_chan, pair * lanes
                put(
                    parity,
                    rows,
                    lambda: total_two[parity, above:above + mid_chan, left_edge:left_edge + lanes],
                )
        put(parity, pl.ds(tail + 4 * mid_chan, third_ref.shape[1]), lambda: third_ref[parity])
    for parity in (0, 1):
        for which in (0, 1):
            lefts = []
            rights = []
            for row in range(H0):
                source = row + (ROW_SHIFT[parity] if which else 0)
                if 0 <= source < H0:
                    lefts.append(latent_row(latent_ref, source))
                    rights.append(side_taps(grad_one, 2 * row + parity, count, W0))
            left = jnp.concatenate(lefts, axis=0) if len(lefts) > 1 else lefts[0]
            right = jnp.concatenate(rights, axis=0) if len(rights) > 1 else rights[0]
            total_one[...] = product_tn(left, right)
            row_tap = ROW_TAPS[parity][which]
            for slot, col_tap in enumerate(COL_TAPS):
                rows = pl.ds(((row_tap % 2) * 4 + col_tap) * in_chan, in_chan)
                put(row_tap // 2, rows, lambda: total_one[:, slot * mid_chan:(slot + 1) * mid_chan])


def params(steps=0):
    if steps:
        return pltpu.CompilerParams(vmem_limit_bytes=VMEM_BYTES, dimension_semantics=("arbitrary",))
    return pltpu.CompilerParams(vmem_limit_bytes=VMEM_BYTES)


def forward(latent, w_one, w_two):
    count = latent.shape[1]
    mid_chan = w_two.shape[1] // 2
    out_chan = w_two.shape[2] // 4
    height, breadth = 2 * H0, 2 * W0
    return pl.pallas_call(
        functools.partial(forward_kernel, count),
        name="decoder_forward",
        out_shape=(
            jax.ShapeDtypeStruct((height, breadth * count, mid_chan), jnp.bfloat16),
            jax.ShapeDtypeStruct((height, breadth * count, mid_chan), jnp.float32),
            jax.ShapeDtypeStruct((2 * height + 2, 2 * breadth * count, out_chan), jnp.bfloat16),
            jax.ShapeDtypeStruct((2 * height, 2 * breadth * count, out_chan), jnp.float32),
        ),
        scratch_shapes=[
            pltpu.VMEM((W0 * count, 4 * mid_chan), jnp.float32),
            pltpu.VMEM((breadth * count, 4 * out_chan), jnp.float32),
        ],
        compiler_params=params(),
    )(latent, w_one, w_two)


def last_layer(act_two, slope_two, w_three, target):
    steps, rows, in_chan = slope_two.shape
    count = rows // (4 * W0)
    lanes = target.shape[2]
    whole = lambda shape: pl.BlockSpec(shape, lambda step: (0,) * len(shape))
    return pl.pallas_call(
        functools.partial(last_kernel, count),
        name="decoder_last",
        grid=(steps,),
        in_specs=[
            whole(act_two.shape),
            whole(slope_two.shape),
            whole(w_three.shape),
            pl.BlockSpec((2, rows, lanes), lambda step: (step, 0, 0)),
        ],
        out_specs=(
            pl.BlockSpec((2, rows, lanes), lambda step: (step, 0, 0)),
            whole(slope_two.shape),
            whole(w_three.shape),
        ),
        out_shape=(
            jax.ShapeDtypeStruct(target.shape, jnp.bfloat16),
            jax.ShapeDtypeStruct(slope_two.shape, jnp.bfloat16),
            jax.ShapeDtypeStruct(w_three.shape, jnp.float32),
        ),
        scratch_shapes=[
            pltpu.VMEM((rows, 2 * lanes), jnp.float32),
            pltpu.VMEM((rows + 2 * count, lanes), jnp.float32),
            pltpu.VMEM((steps + 2, rows, in_chan), jnp.float32),
        ],
        compiler_params=params(1),
    )(act_two, slope_two, w_three, target)


def backward(side, latent, act_one, slope_one, w_two, grad_two, third):
    count = latent.shape[1]
    in_chan = latent.shape[0] * latent.shape[2] // (H0 * W0)
    mid_chan = act_one.shape[2]
    return pl.pallas_call(
        functools.partial(backward_kernel, count),
        name="decoder_backward",
        in_specs=[pl.BlockSpec(memory_space=pltpu.SMEM)] + [pl.BlockSpec(memory_space=pltpu.VMEM)] * 6,
        out_specs=(pl.BlockSpec(memory_space=pltpu.VMEM),) * 2,
        out_shape=(jax.ShapeDtypeStruct((8 * in_chan + 4 * mid_chan + third.shape[1], mid_chan), jnp.bfloat16),) * 2,
        scratch_shapes=[
            pltpu.VMEM(act_one.shape, jnp.bfloat16),
            pltpu.VMEM(act_one.shape, jnp.float32),
            pltpu.VMEM((in_chan, 4 * mid_chan), jnp.float32),
            pltpu.VMEM(w_two.shape, jnp.float32),
        ],
        compiler_params=params(),
    )(side, latent, act_one, slope_one, w_two, grad_two, third)


def spatial_first_kernel(grid_ref, after_ref, rows_ref, tmp):
    count, height, breadth, chan = grid_ref.shape
    for row in range(height):
        tmp[...] = grid_ref[:, row].astype(jnp.float32)
        even = tmp[:, pl.ds(0, breadth // 2, 2), :]
        odd = tmp[:, pl.ds(1, breadth // 2, 2), :]
        turned = jnp.swapaxes(jnp.concatenate([even, odd], axis=2), 0, 1)
        rows_ref[row] = turned.reshape(breadth // 2 * count, 2 * chan).astype(jnp.bfloat16)


def spatial_first(grid, after):
    count, height, breadth, chan = grid.shape
    per = 4
    flat = breadth // 2 * count
    return pl.pallas_call(
        spatial_first_kernel,
        name="spatial_first",
        grid=(height // per,),
        in_specs=[
            pl.BlockSpec((count, per, breadth, chan), lambda step: (0, step, 0, 0)),
            pl.BlockSpec(memory_space=pl.ANY),
        ],
        out_specs=pl.BlockSpec((per, flat, 2 * chan), lambda step: (step, 0, 0)),
        out_shape=jax.ShapeDtypeStruct((height, flat, 2 * chan), jnp.bfloat16),
        scratch_shapes=[pltpu.VMEM((count, breadth, chan), jnp.float32)],
        compiler_params=params(1),
        cost_estimate=pl.CostEstimate(flops=0, bytes_accessed=28000000, transcendentals=0),
    )(grid, after)


def sample_first_kernel(rows_ref, after_ref, out_ref, tmp):
    height = rows_ref.shape[0]
    count, _, breadth, chan = out_ref.shape
    for row in range(height):
        value = rows_ref[row].astype(jnp.float32).reshape(breadth // 2, count, 2 * chan)
        turned = jnp.swapaxes(value, 0, 1)
        tmp[:, pl.ds(0, breadth // 2, 2), :] = turned[:, :, :chan]
        tmp[:, pl.ds(1, breadth // 2, 2), :] = turned[:, :, chan:]
        out_ref[:, row] = tmp[...].astype(jnp.bfloat16)


def sample_first(rows, count, chan, after):
    height, flat, lanes = rows.shape
    breadth = 2 * flat // count
    per = 4
    return pl.pallas_call(
        sample_first_kernel,
        name="sample_first",
        grid=(height // per,),
        in_specs=[
            pl.BlockSpec((per, flat, lanes), lambda step: (step, 0, 0)),
            pl.BlockSpec(memory_space=pl.ANY),
        ],
        out_specs=pl.BlockSpec((count, per, breadth, chan), lambda step: (0, step, 0, 0)),
        out_shape=jax.ShapeDtypeStruct((count, height, breadth, chan), jnp.bfloat16),
        scratch_shapes=[pltpu.VMEM((count, breadth, chan), jnp.float32)],
        compiler_params=params(1),
        cost_estimate=pl.CostEstimate(flops=0, bytes_accessed=28000000, transcendentals=0),
    )(rows, after)


def bucket_kernel(subject_ref, count_ref, shift_ref, fmri_ref, first_ref, second_ref, place_ref):
    samples, voxels = fmri_ref.shape
    slots = first_ref.shape[0]
    subjects = count_ref.shape[0]
    room = slots // subjects
    owner = subject_ref[...]
    lane = lax.broadcasted_iota(jnp.int32, (samples, 128), 1)
    onehot = jnp.where(owner == lane, 1.0, 0.0)
    row = lax.broadcasted_iota(jnp.int32, (samples, samples), 0)
    col = lax.broadcasted_iota(jnp.int32, (samples, samples), 1)
    before = jnp.where(col < row, 1.0, 0.0).astype(jnp.bfloat16)
    earlier = product(before, onehot.astype(jnp.bfloat16))
    rank = jnp.sum(earlier * onehot, axis=1, keepdims=True).astype(jnp.int32)
    position = owner * room + rank + jnp.where(rank >= room, slots - room, 0)
    slot = lax.broadcasted_iota(jnp.int32, (samples, 2 * slots), 1)
    place_ref[...] = jnp.where(slot == position, 1.0, 0.0).astype(jnp.bfloat16)
    voxel = lax.broadcasted_iota(jnp.int32, (room, voxels), 1) + shift_ref[0]
    for half, out_ref in enumerate((first_ref, second_ref)):
        for target in range(subjects):
            here = pl.ds(half * slots + target * room, room)
            if room * target % 128 == 0:
                width = min(128, slots)
                rows = product_tn(place_ref[:, pl.ds(half * slots + target * room, width)], fmri_ref[...])
                for inner in range(width // room):
                    keep = voxel < count_ref[target + inner]
                    kept = jnp.where(keep, rows[inner * room:(inner + 1) * room], 0.0)
                    out_ref[pl.ds((target + inner) * room, room), :] = kept.astype(jnp.bfloat16)


def bucketed(subject, voxel_count, shift, fmri, slots):
    samples, voxels = fmri.shape
    vmem = pl.BlockSpec(memory_space=pltpu.VMEM)
    smem = pl.BlockSpec(memory_space=pltpu.SMEM)
    return pl.pallas_call(
        bucket_kernel,
        name="bucket_rows",
        in_specs=[vmem, smem, smem, vmem],
        out_specs=(vmem, vmem, vmem),
        out_shape=(
            jax.ShapeDtypeStruct((slots, voxels), jnp.bfloat16),
            jax.ShapeDtypeStruct((slots, voxels), jnp.bfloat16),
            jax.ShapeDtypeStruct((samples, 2 * slots), jnp.bfloat16),
        ),
        compiler_params=params(),
    )(subject, voxel_count, shift, fmri)


def project_kernel(half_ref, rows_ref, map_ref, after_ref, out_ref):
    out_ref[0] = product(rows_ref[...], map_ref[0]).astype(jnp.bfloat16)


def projected(rows, maps, half, after):
    count, voxels = rows.shape
    blocks = H0 * W0 // 2
    width = maps.shape[2] // (2 * blocks)
    return pl.pallas_call(
        project_kernel,
        name="project_rows",
        grid_spec=pltpu.PrefetchScalarGridSpec(
            num_scalar_prefetch=1,
            grid=(blocks,),
            in_specs=[
                pl.BlockSpec((count, voxels), lambda step, half: (0, 0)),
                pl.BlockSpec((1, voxels, width), lambda step, half: (0, 0, half[0] * blocks + step)),
                pl.BlockSpec(memory_space=pl.ANY),
            ],
            out_specs=pl.BlockSpec((1, count, width), lambda step, half: (step, 0, 0)),
        ),
        out_shape=jax.ShapeDtypeStruct((blocks, count, width), jnp.bfloat16),
        compiler_params=params(1),
        cost_estimate=pl.CostEstimate(
            flops=count * voxels * maps.shape[2],
            bytes_accessed=voxels * maps.shape[2],
            transcendentals=0,
        ),
    )(half, rows, maps, after)


def collect_kernel(place_ref, first_ref, second_ref, out_ref):
    subjects, blocks, room, width = first_ref.shape
    for block in range(blocks):
        rows = [ref[subject, block] for ref in (first_ref, second_ref) for subject in range(subjects)]
        value = product(place_ref[...], jnp.concatenate(rows, axis=0))
        out_ref[:, pl.ds(block * width, width)] = value.astype(jnp.bfloat16)


def collected(place, first, second):
    samples = place.shape[0]
    return pl.pallas_call(
        collect_kernel,
        name="collect_rows",
        out_shape=jax.ShapeDtypeStruct((samples, first.shape[1] * first.shape[3]), jnp.bfloat16),
        compiler_params=params(),
    )(place, first, second)


def finish_kernel(third_rows, side_ref, own_a, own_b, own_c, other_a, other_b, other_c, first_ref, second_ref, third_ref):
    side = side_ref[0]
    rows = own_a.shape[0]
    for at, (source, half) in enumerate(((own_a, side), (own_b, side), (other_a, 1 - side), (other_b, 1 - side))):
        start = pl.multiple_of((2 * half + at % 2) * rows, rows)
        first_ref[pl.ds(start, rows), :] = source[...]
    out_chan = second_ref.shape[1]
    mid_chan = second_ref.shape[0] // 16
    for parity in (0, 1):
        mine = side == parity
        for which in (0, 1):
            for pair in (0, 1):
                here = pl.ds((2 * which + pair) * mid_chan, mid_chan)
                value = jnp.where(mine, own_c[here, :].astype(jnp.float32), other_c[here, :].astype(jnp.float32))
                for inner in (0, 1):
                    col_tap = COL_TAPS[2 * pair + inner]
                    to = pl.ds((ROW_TAPS[parity][which] * 4 + col_tap) * mid_chan, mid_chan)
                    second_ref[to, :] = value[:, inner * out_chan:(inner + 1) * out_chan].astype(jnp.bfloat16)
        here = pl.ds(4 * mid_chan, third_rows)
        value = jnp.where(mine, own_c[here, :].astype(jnp.float32), other_c[here, :].astype(jnp.float32)).T
        chan = third_ref.shape[0]
        inputs = third_rows // 2
        for which in (0, 1):
            for slot, col_tap in enumerate(COL_TAPS):
                to = pl.ds((ROW_TAPS[parity][which] * 4 + col_tap) * inputs, inputs)
                piece = value[slot * chan:(slot + 1) * chan, which * inputs:(which + 1) * inputs]
                third_ref[:, to] = piece.astype(jnp.bfloat16)


def finished(side, own, other, third_rows):
    rows, lanes = own[0].shape
    mid_chan = (own[2].shape[0] - third_rows) // 4
    vmem = pl.BlockSpec(memory_space=pltpu.VMEM)
    return pl.pallas_call(
        functools.partial(finish_kernel, third_rows),
        name="finish_gradients",
        in_specs=[pl.BlockSpec(memory_space=pltpu.SMEM)] + [vmem] * 6,
        out_specs=(vmem, vmem, vmem),
        out_shape=(
            jax.ShapeDtypeStruct((4 * rows, lanes), jnp.bfloat16),
            jax.ShapeDtypeStruct((16 * mid_chan, lanes // 2), jnp.bfloat16),
            jax.ShapeDtypeStruct((lanes // 4, 8 * third_rows), jnp.bfloat16),
        ),
        compiler_params=params(),
    )(side, *own, *other)


def rounded(values):
    return lax.optimization_barrier(values.astype(jnp.bfloat16))


def bit_pairs(axis):
    size = lax.axis_size(axis)
    bits = []
    bit = 1
    while bit < size:
        bits.append((axis, bit))
        bit *= 2
    return bits


def upper(hop):
    axis, bit = hop
    return (lax.axis_index(axis) // bit) % 2


def place_of(step):
    return sum(upper(hop) * 2 ** at for at, hop in enumerate(step))


def exchanged(values, step, change):
    axis = step[0][0]
    flip = sum(hop[1] for at, hop in enumerate(step) if change >> at & 1)
    return lax.ppermute(values, axis, [(at, at ^ flip) for at in range(lax.axis_size(axis))])


def summed(terms):
    value = terms[0]
    for term in terms[1:]:
        value = value.astype(jnp.float32) + term.astype(jnp.float32)
    return value


def shared(chains, step):
    ways = 2 ** len(step)
    place = place_of(step)

    def part(terms, which):
        size = terms[0].shape[0] // ways
        return summed([lax.dynamic_slice_in_dim(term, which * size, size, 0) for term in terms])

    arrived = []
    for change in range(1, ways):
        sent = [part(terms, place ^ change).astype(jnp.bfloat16) for terms in chains]
        joined = jnp.concatenate(sent, axis=0) if len(sent) > 1 else sent[0]
        arrived.append(exchanged(joined, step, change))
    result = []
    start = 0
    for terms in chains:
        size = terms[0].shape[0] // ways
        result.append([part(terms, place)] + [values[start:start + size] for values in arrived])
        start += size
    return result


def gathered(chains, step):
    ways = 2 ** len(step)
    joined = jnp.concatenate(chains, axis=0) if len(chains) > 1 else chains[0]
    pieces = [joined] + [exchanged(joined, step, change) for change in range(1, ways)]
    place = place_of(step)
    result = []
    start = 0
    for values in chains:
        size = values.shape[0]
        out = jnp.concatenate([values] * ways, axis=0)
        for change in range(1, ways):
            piece = pieces[change][start:start + size]
            out = lax.dynamic_update_slice_in_dim(out, piece, (place ^ change) * size, 0)
        result.append(out)
        start += size
    return result


def over_chains(move, chains, steps):
    result = [None] * len(chains)
    for step in {tuple(step): step for step in steps}.values():
        members = [at for at, own in enumerate(steps) if own == step]
        for at, moved_chain in zip(members, move([chains[at] for at in members], step)):
            result[at] = moved_chain
    return result


def shards(fmri, subject, ridge_maps, voxel_count, w_first, w_second, w_third, target):
    dp_count = lax.axis_size("dp")
    holders = lax.axis_size("vox")
    samp_dev = fmri.shape[0]
    vox_local = fmri.shape[1]
    mid_chan = w_first.shape[1]
    last_chan = w_second.shape[1]
    room = samp_dev // dp_count
    vox_bits = bit_pairs("vox")
    dp_bits = bit_pairs("dp")
    side = upper(vox_bits[0]).astype(jnp.int32).reshape(1)
    shift = (lax.axis_index("vox") * vox_local).astype(jnp.int32).reshape(1)
    first, second, place = bucketed(subject, voxel_count, shift, fmri, samp_dev)

    def routed(rows):
        sent = rows.reshape(dp_count, room, rows.shape[1])
        return lax.all_to_all(sent, "dp", split_axis=0, concat_axis=0, tiled=True).reshape(rows.shape)

    def vox_summed(rows, after):
        sent = projected(rows, ridge_maps, 1 - side, after)
        received = exchanged(sent, vox_bits[:1], 1)
        terms = [projected(rows, ridge_maps, side, sent), received]
        for hop in vox_bits[1:]:
            terms, = shared([terms], [hop])
        return terms, received

    def returned(terms):
        latent_part = rounded(summed(terms))
        blocks, _, width = latent_part.shape
        sent = latent_part.reshape(blocks, dp_count, room, width).swapaxes(0, 1)
        return lax.all_to_all(sent, "dp", split_axis=0, concat_axis=0, tiled=True)

    first = routed(first)
    second = routed(second)
    terms_first, _ = vox_summed(first, voxel_count)
    terms_second, core_second = vox_summed(second, terms_first[1])
    pair_two = paired_weight(w_second, mid_chan)
    pair_three = paired_weight(w_third, last_chan)
    target_rows = spatial_first(target, core_second)
    own_rows = collected(place, returned(terms_first), returned(terms_second))
    own_rows = own_rows.reshape(holders, samp_dev // holders, own_rows.shape[1])
    latent = lax.all_to_all(own_rows, "vox", split_axis=0, concat_axis=0, tiled=True)
    count = latent.shape[1]
    act_one, slope_one, act_two, slope_two = forward(latent, w_first, pair_two)
    decoded_rows, grad_two, paired_three = last_layer(act_two, slope_two, pair_three, target_rows)
    kept, sent = backward(side, latent, act_one, slope_one, pair_two, grad_two, paired_three)
    third_rows = paired_three.shape[1]
    quarter = w_first.shape[0] // 4
    across = [[hop] for hop in vox_bits[1:]]
    near = [dp_bits[:1]]
    along = [dp_bits[at:at + 2] for at in range(1, len(dp_bits), 2)]
    routes = (across + near + along, near + across + along, along + across + near)
    received = exchanged(sent, vox_bits[:1], 1)
    cuts = ((0, quarter), (quarter, 2 * quarter), (2 * quarter, kept.shape[0]))
    parts = [[kept[low:high], received[low:high]] for low, high in cuts]
    decoded = sample_first(decoded_rows, count, w_third.shape[1], received)
    for stage in range(len(routes[0])):
        parts = over_chains(shared, parts, [route[stage] for route in routes])
        *tied, decoded = lax.optimization_barrier(tuple(terms[1] for terms in parts) + (decoded,))
        parts = [terms[:1] + [arrived] + terms[2:] for terms, arrived in zip(parts, tied)]
    shares = [summed(terms).astype(jnp.bfloat16) for terms in parts]
    for stage in reversed(range(len(routes[0]))):
        shares = over_chains(gathered, shares, [route[stage] for route in routes])
        shares = lax.optimization_barrier(tuple(shares))
    others = [exchanged(values, vox_bits[:1], 1) for values in shares]
    total_first, total_second, third = finished(side, shares, others, third_rows)
    total_third = third.T
    return (decoded, total_first, total_second, total_third)


def solution(mesh):
    placed = (
        P("dp", "vox"),
        P("dp", None),
        P("dp", "vox", None),
        P(),
        P(),
        P(),
        P(),
        P(("dp", "vox"), None, None, None),
    )
    return jax.shard_map(
        shards,
        mesh=mesh,
        in_specs=placed,
        out_specs=(P(("dp", "vox"), None, None, None), P(), P(), P()),
        check_vma=False,
    )
```

```python
import functools
import jax
import jax.numpy as jnp
from jax import lax
from jax.experimental import pallas as pl
from jax.sharding import PartitionSpec as P
from jax.experimental.pallas import tpu as pltpu

H0 = 2
W0 = 4
SAMP_DEV = 256
ROW_TAPS = ((1, 3), (2, 0))
ROW_SHIFT = (-1, 1)
COL_TAPS = (1, 2, 3, 0)


def paired_weight(weights, in_chan):
    out_chan = weights.shape[1]
    kernel = weights.reshape(4, 4, in_chan, out_chan)
    halves = []
    for parity in (0, 1):
        rows = []
        for row_tap in ROW_TAPS[parity]:
            rows.append(jnp.concatenate([kernel[row_tap, col_tap] for col_tap in COL_TAPS], axis=1))
        halves.append(jnp.concatenate(rows, axis=0))
    return jnp.stack(halves)


def product(left, right):
    return jnp.dot(left, right, preferred_element_type=jnp.float32)


def product_nt(left, right):
    return lax.dot_general(left, right, (((1,), (1,)), ((), ())), preferred_element_type=jnp.float32)


def product_tn(left, right):
    return lax.dot_general(left, right, (((0,), (0,)), ((), ())), preferred_element_type=jnp.float32)


def gelu_pair(value):
    root = 0.7978845608028654
    square = value * value
    tanh = jnp.tanh(root * (value + 0.044715 * (square * value)))
    half = 0.5 * (1.0 + tanh)
    slope = half + (0.5 * value) * (1.0 - tanh * tanh) * (root + (3 * 0.044715 * root) * square)
    return value * half, slope


def up_rows(product_ref, act_ref, slope_ref, act_row, slope_row, count, breadth, out_chan):
    width = 2 * out_chan
    for col in range(breadth):
        here = pl.ds(col * count, count)
        for col_par in (0, 1):
            lanes = pl.ds(col_par * out_chan, out_chan)
            side = pl.ds(width + col_par * out_chan, out_chan)
            value = product_ref[here, lanes]
            other = col - 1 if col_par == 0 else col + 1
            if 0 <= other < breadth:
                value = value + product_ref[pl.ds(other * count, count), side]
            act, slope = gelu_pair(value)
            rows = pl.ds((2 * col + col_par) * count, count)
            act_ref[act_row, rows, :] = act.astype(jnp.bfloat16)
            slope_ref[slope_row, rows, :] = slope


def holder_of(block, holders):
    bits = holders.bit_length() - 1
    depth = (H0 * W0).bit_length() - 1
    owner = sum(((block >> (depth - 1 - at)) & 1) << at for at in range(bits))
    return owner, block & (2 ** (depth - bits) - 1)


def latent_row(latent_ref, row):
    holders = latent_ref.shape[0]
    width = latent_ref.shape[2] * holders // (H0 * W0)
    pieces = []
    for col in range(W0):
        owner, place = holder_of(row * W0 + col, holders)
        pieces.append(latent_ref[owner, :, pl.ds(place * width, width)])
    return jnp.concatenate(pieces, axis=0)


def forward_part(count, latent_ref, w_one_ref, w_two_ref, act_one_ref, slope_one_ref, act_two_ref, slope_two_ref, tmp_one, tmp_two):
    in_chan = w_one_ref.shape[0] // 16
    mid_chan = w_two_ref.shape[1] // 2
    out_chan = w_two_ref.shape[2] // 4

    for row in range(H0):
        for parity in (0, 1):
            other = row + ROW_SHIFT[parity]
            for slot, col_tap in enumerate(COL_TAPS):
                lanes = pl.ds(slot * mid_chan, mid_chan)
                taps = pl.ds((ROW_TAPS[parity][0] * 4 + col_tap) * in_chan, in_chan)
                value = product(latent_row(latent_ref, row), w_one_ref[taps, :])
                if 0 <= other < H0:
                    taps = pl.ds((ROW_TAPS[parity][1] * 4 + col_tap) * in_chan, in_chan)
                    value = value + product(latent_row(latent_ref, other), w_one_ref[taps, :])
                tmp_one[:, lanes] = value
            at = 2 * row + parity
            up_rows(tmp_one, act_one_ref, slope_one_ref, at, at, count, W0, mid_chan)
    height = 2 * H0
    breadth = 2 * W0
    act_two_ref[0] = jnp.zeros_like(act_two_ref[0])
    act_two_ref[2 * height + 1] = jnp.zeros_like(act_two_ref[0])
    for row in range(height):
        for parity in (0, 1):
            tmp_two[...] = product(act_one_ref[row], w_two_ref[parity, :mid_chan, :])
            other = row + ROW_SHIFT[parity]
            if 0 <= other < height:
                tmp_two[...] += product(act_one_ref[other], w_two_ref[parity, mid_chan:, :])
            at = 2 * row + parity
            up_rows(tmp_two, act_two_ref, slope_two_ref, at + 1, at, count, breadth, out_chan)


def last_part(count, step, steps, act_ref, slope_ref, w_ref, target_ref, decoded_ref, grad_ref, kgrad_ref, tmp, grads, adj):
    breadth = act_ref.shape[1] // count
    in_chan = act_ref.shape[2]
    lanes = 2 * (w_ref.shape[2] // 4)

    @pl.when(step == 0)
    def _():
        adj[...] = jnp.zeros_like(adj)
        kgrad_ref[...] = jnp.zeros_like(kgrad_ref)
        grads[...] = jnp.zeros_like(grads)

    low = lax.broadcasted_iota(jnp.int32, (count, lanes), 1) < lanes // 2
    for parity in (0, 1):
        other = step + 1 + ROW_SHIFT[parity]
        left = jnp.concatenate([act_ref[step + 1], act_ref[other]], axis=1)
        tmp[...] = product(left, w_ref[parity])
        zero = jnp.zeros((count, lanes), jnp.float32)
        for col in range(breadth):
            here = pl.ds(col * count, count)
            before = tmp[pl.ds((col - 1) * count, count), lanes:] if col > 0 else zero
            after = tmp[pl.ds((col + 1) * count, count), lanes:] if col < breadth - 1 else zero
            value = tmp[here, :lanes] + jnp.where(low, before, after)
            decoded_ref[parity, here, :] = value.astype(jnp.bfloat16)
            grad = (value - target_ref[parity, here, :].astype(jnp.float32)) * (1.0 / SAMP_DEV)
            grads[pl.ds((col + 1) * count, count), :] = grad
        pieces = []
        for col in range(breadth):
            before = grads[pl.ds(col * count, count), :]
            here = grads[pl.ds((col + 1) * count, count), :]
            after = grads[pl.ds((col + 2) * count, count), :]
            side = jnp.where(low, after, before)
            pieces.append(jnp.concatenate([here.astype(jnp.bfloat16), side.astype(jnp.bfloat16)], axis=1))
        taps = jnp.concatenate(pieces, axis=0)
        kgrad_ref[parity] += product_tn(left, taps)
        back = product_nt(taps, w_ref[parity])
        adj[step + 1] += back[:, :in_chan]
        adj[other] += back[:, in_chan:]

    @pl.when(step == steps - 1)
    def _():
        def finish(row, carry):
            upstream = adj[row + 1].astype(jnp.bfloat16).astype(jnp.float32)
            grad_ref[row] = (upstream * slope_ref[row]).astype(jnp.bfloat16)
            return carry

        lax.fori_loop(0, steps, finish, 0)


def side_taps(grad_ref, row, count, breadth):
    def at(col):
        if 0 <= col < 2 * breadth:
            return grad_ref[row, pl.ds(col * count, count), :]
        return jnp.zeros((count, grad_ref.shape[2]), jnp.bfloat16)

    pieces = []
    for col in range(breadth):
        pieces.append(jnp.concatenate([at(2 * col), at(2 * col + 1), at(2 * col + 2), at(2 * col - 1)], axis=1))
    return jnp.concatenate(pieces, axis=0)


def second_part(count, side_ref, act_ref, slope_ref, w_ref, grad_two_ref, third_ref, grad_one, kept_ref, sent_ref, adj, total_two):
    side = side_ref[0]

    def put(half, rows, values):
        @pl.when(side == half)
        def _():
            kept_ref[rows, :] = values().astype(jnp.bfloat16)

        @pl.when(side != half)
        def _():
            sent_ref[rows, :] = values().astype(jnp.bfloat16)

    height = act_ref.shape[0]
    breadth = act_ref.shape[1] // count
    mid_chan = act_ref.shape[2]
    out_chan = grad_two_ref.shape[2]
    for row in range(height):
        for parity in (0, 1):
            taps = side_taps(grad_two_ref, 2 * row + parity, count, breadth)
            back = product_nt(taps, w_ref[parity])
            other = row + ROW_SHIFT[parity]
            if parity == 0 and row == 0:
                adj[0] = back[:, :mid_chan]
            else:
                adj[row] += back[:, :mid_chan]
            if 0 <= other < height:
                if parity == 0:
                    adj[other] += back[:, mid_chan:]
                else:
                    adj[other] = back[:, mid_chan:]
            mine = product_tn(act_ref[row], taps)
            if row == 0:
                total_two[parity, :mid_chan, :] = mine
            else:
                total_two[parity, :mid_chan, :] += mine
            if 0 <= other < height:
                far = product_tn(act_ref[other], taps)
                if row == (1 if parity == 0 else 0):
                    total_two[parity, mid_chan:, :] = far
                else:
                    total_two[parity, mid_chan:, :] += far
    for row in range(height):
        upstream = adj[row].astype(jnp.bfloat16).astype(jnp.float32)
        grad_one[row] = (upstream * slope_ref[row]).astype(jnp.bfloat16)
    lanes = 2 * out_chan
    for parity in (0, 1):
        for which in (0, 1):
            for pair in (0, 1):
                rows = pl.ds((2 * which + pair) * mid_chan, mid_chan)
                above, left_edge = which * mid_chan, pair * lanes
                put(
                    parity,
                    rows,
                    lambda: total_two[parity, above:above + mid_chan, left_edge:left_edge + lanes],
                )
        put(parity, pl.ds(4 * mid_chan, third_ref.shape[1]), lambda: third_ref[parity])


def first_kernel(count, half_ref, latent_ref, grad_one, out_ref, total_one):
    in_chan = latent_ref.shape[0] * latent_ref.shape[2] // (H0 * W0)
    mid_chan = grad_one.shape[2]
    for half in (0, 1):

        @pl.when(half_ref[0] == half)
        def _(half=half):
            for row_tap in (2 * half, 2 * half + 1):
                parity = 0 if row_tap in ROW_TAPS[0] else 1
                shift = ROW_SHIFT[parity] if ROW_TAPS[parity][1] == row_tap else 0
                rows = [row for row in range(H0) if 0 <= row + shift < H0]
                lefts = [latent_row(latent_ref, row + shift) for row in rows]
                rights = [side_taps(grad_one, 2 * row + parity, count, W0) for row in rows]
                left = jnp.concatenate(lefts, axis=0) if len(lefts) > 1 else lefts[0]
                right = jnp.concatenate(rights, axis=0) if len(rights) > 1 else rights[0]
                total_one[...] = product_tn(left, right)
                for slot, col_tap in enumerate(COL_TAPS):
                    to = pl.ds(((row_tap % 2) * 4 + col_tap) * in_chan, in_chan)
                    out_ref[to, :] = total_one[:, slot * mid_chan:(slot + 1) * mid_chan].astype(jnp.bfloat16)


def decoder_kernel(
    count, side_ref, latent_ref, w_one_ref, w_two_ref, w_three_ref, target_ref,
    decoded_ref, grad_one_ref, kept_ref, sent_ref,
    act_one, slope_one, act_two, slope_two, grad_two, kgrad_three, tmp_one, tmp_two, tmp_three, grads, adj_two, adj_one, total_two,
):
    step = pl.program_id(0)
    steps = pl.num_programs(0)

    @pl.when(step == 0)
    def _():
        forward_part(count, latent_ref, w_one_ref, w_two_ref, act_one, slope_one, act_two, slope_two, tmp_one, tmp_two)

    last_part(
        count, step, steps, act_two, slope_two, w_three_ref, target_ref, decoded_ref, grad_two, kgrad_three, tmp_three, grads, adj_two
    )

    @pl.when(step == steps - 1)
    def _():
        second_part(
            count, side_ref, act_one, slope_one, w_two_ref, grad_two, kgrad_three, grad_one_ref, kept_ref, sent_ref, adj_one, total_two
        )


def params(mebibytes, gridded=False):
    order = ("arbitrary",) if gridded else None
    return pltpu.CompilerParams(vmem_limit_bytes=mebibytes * 1024 * 1024, dimension_semantics=order)


def decoder(side, latent, w_one, w_two, w_three, target):
    count = latent.shape[1]
    mid_chan = w_two.shape[1] // 2
    out_chan = w_two.shape[2] // 4
    height, breadth = 2 * H0, 2 * W0
    steps, flat, lanes = target.shape[0] // 2, target.shape[1], target.shape[2]
    third_rows = w_three.shape[1]

    def whole(shape):
        return pl.BlockSpec(shape, lambda step: (0,) * len(shape))

    act_one = (height, breadth * count, mid_chan)
    act_two = (2 * height, flat, out_chan)
    padded = (2 * height + 2, flat, out_chan)
    tail = (4 * mid_chan + third_rows, mid_chan)
    single = pl.Buffered(1)
    return pl.pallas_call(
        functools.partial(decoder_kernel, count),
        name="decoder",
        grid=(steps,),
        in_specs=[
            pl.BlockSpec(memory_space=pltpu.SMEM),
            pl.BlockSpec(latent.shape, lambda step: (0, 0, 0), pipeline_mode=single),
            pl.BlockSpec(w_one.shape, lambda step: (0, 0), pipeline_mode=single),
            pl.BlockSpec(w_two.shape, lambda step: (0, 0, 0), pipeline_mode=single),
            pl.BlockSpec(w_three.shape, lambda step: (0, 0, 0), pipeline_mode=single),
            pl.BlockSpec((2, flat, lanes), lambda step: (step, 0, 0)),
        ],
        out_specs=(
            pl.BlockSpec((2, flat, lanes), lambda step: (step, 0, 0)),
            whole(act_one),
            whole(tail),
            whole(tail),
        ),
        out_shape=(
            jax.ShapeDtypeStruct(target.shape, jnp.bfloat16),
            jax.ShapeDtypeStruct(act_one, jnp.bfloat16),
            jax.ShapeDtypeStruct(tail, jnp.bfloat16),
            jax.ShapeDtypeStruct(tail, jnp.bfloat16),
        ),
        scratch_shapes=[
            pltpu.VMEM(act_one, jnp.bfloat16),
            pltpu.VMEM(act_one, jnp.float32),
            pltpu.VMEM(padded, jnp.bfloat16),
            pltpu.VMEM(act_two, jnp.float32),
            pltpu.VMEM(act_two, jnp.bfloat16),
            pltpu.VMEM(w_three.shape, jnp.float32),
            pltpu.VMEM((W0 * count, 4 * mid_chan), jnp.float32),
            pltpu.VMEM((breadth * count, 4 * out_chan), jnp.float32),
            pltpu.VMEM((flat, 2 * lanes), jnp.float32),
            pltpu.VMEM((flat + 2 * count, lanes), jnp.float32),
            pltpu.VMEM(padded, jnp.float32),
            pltpu.VMEM(act_one, jnp.float32),
            pltpu.VMEM(w_two.shape, jnp.float32),
        ],
        compiler_params=params(52, True),
    )(side, latent, w_one, w_two, w_three, target)


def first_grad(half, latent, grad_one, after):
    count = latent.shape[1]
    in_chan = latent.shape[0] * latent.shape[2] // (H0 * W0)
    mid_chan = grad_one.shape[2]
    vmem = pl.BlockSpec(memory_space=pltpu.VMEM)

    def kernel(half_ref, latent_ref, grad_ref, after_ref, out_ref, total_one):
        first_kernel(count, half_ref, latent_ref, grad_ref, out_ref, total_one)

    return pl.pallas_call(
        kernel,
        name="first_grad",
        in_specs=[pl.BlockSpec(memory_space=pltpu.SMEM), vmem, vmem, pl.BlockSpec(memory_space=pl.ANY)],
        out_specs=vmem,
        out_shape=jax.ShapeDtypeStruct((8 * in_chan, mid_chan), jnp.bfloat16),
        scratch_shapes=[pltpu.VMEM((in_chan, 4 * mid_chan), jnp.float32)],
        compiler_params=params(24),
        cost_estimate=pl.CostEstimate(
            flops=64 * count * in_chan * mid_chan, bytes_accessed=16 * in_chan * mid_chan, transcendentals=0
        ),
    )(half, latent, grad_one, after)


def spatial_first_kernel(grid_ref, after_ref, rows_ref, tmp):
    count, height, breadth, chan = grid_ref.shape
    for row in range(height):
        tmp[...] = grid_ref[:, row].astype(jnp.float32)
        even = tmp[:, pl.ds(0, breadth // 2, 2), :]
        odd = tmp[:, pl.ds(1, breadth // 2, 2), :]
        turned = jnp.swapaxes(jnp.concatenate([even, odd], axis=2), 0, 1)
        rows_ref[row] = turned.reshape(breadth // 2 * count, 2 * chan).astype(jnp.bfloat16)


def spatial_first(grid, after):
    count, height, breadth, chan = grid.shape
    per = 4
    flat = breadth // 2 * count
    return pl.pallas_call(
        spatial_first_kernel,
        name="spatial_first",
        grid=(height // per,),
        in_specs=[
            pl.BlockSpec((count, per, breadth, chan), lambda step: (0, step, 0, 0)),
            pl.BlockSpec(memory_space=pl.ANY),
        ],
        out_specs=pl.BlockSpec((per, flat, 2 * chan), lambda step: (step, 0, 0)),
        out_shape=jax.ShapeDtypeStruct((height, flat, 2 * chan), jnp.bfloat16),
        scratch_shapes=[pltpu.VMEM((count, breadth, chan), jnp.float32)],
        compiler_params=params(20, True),
        cost_estimate=pl.CostEstimate(flops=0, bytes_accessed=28000000, transcendentals=0),
    )(grid, after)


def sample_first_kernel(rows_ref, after_ref, out_ref, tmp):
    height = rows_ref.shape[0]
    count, _, breadth, chan = out_ref.shape
    for row in range(height):
        value = rows_ref[row].astype(jnp.float32).reshape(breadth // 2, count, 2 * chan)
        turned = jnp.swapaxes(value, 0, 1)
        tmp[:, pl.ds(0, breadth // 2, 2), :] = turned[:, :, :chan]
        tmp[:, pl.ds(1, breadth // 2, 2), :] = turned[:, :, chan:]
        out_ref[:, row] = tmp[...].astype(jnp.bfloat16)


def sample_first(rows, count, chan, after):
    height, flat, lanes = rows.shape
    breadth = 2 * flat // count
    per = 4
    return pl.pallas_call(
        sample_first_kernel,
        name="sample_first",
        grid=(height // per,),
        in_specs=[
            pl.BlockSpec((per, flat, lanes), lambda step: (step, 0, 0)),
            pl.BlockSpec(memory_space=pl.ANY),
        ],
        out_specs=pl.BlockSpec((count, per, breadth, chan), lambda step: (0, step, 0, 0)),
        out_shape=jax.ShapeDtypeStruct((count, height, breadth, chan), jnp.bfloat16),
        scratch_shapes=[pltpu.VMEM((count, breadth, chan), jnp.float32)],
        compiler_params=params(20, True),
        cost_estimate=pl.CostEstimate(flops=0, bytes_accessed=28000000, transcendentals=0),
    )(rows, after)


def bucket_kernel(half, subject_ref, count_ref, shift_ref, fmri_ref, after_ref, out_ref, place_ref):
    samples, voxels = fmri_ref.shape
    slots = out_ref.shape[0]
    subjects = count_ref.shape[0]
    room = slots // subjects
    owner = subject_ref[...]
    name = lax.broadcasted_iota(jnp.int32, (subjects, samples), 0)
    onehot = jnp.where(owner == name, 1.0, 0.0)
    row = lax.broadcasted_iota(jnp.int32, (samples, samples), 0)
    col = lax.broadcasted_iota(jnp.int32, (samples, samples), 1)
    before = jnp.where(row < col, 1.0, 0.0).astype(jnp.bfloat16)
    earlier = product(onehot.astype(jnp.bfloat16), before)
    rank = jnp.sum(earlier * onehot, axis=0, keepdims=True).astype(jnp.int32) - half * room
    position = jnp.where((rank >= 0) & (rank < room), owner * room + rank, -1)
    slot = lax.broadcasted_iota(jnp.int32, (slots, samples), 0)
    place_ref[...] = jnp.where(slot == position, 1.0, 0.0).astype(jnp.bfloat16)
    voxel = lax.broadcasted_iota(jnp.int32, (room, voxels), 1) + shift_ref[0]
    together = max(1, 64 // room)
    for start in range(0, subjects, together):
        rows = product(place_ref[pl.ds(start * room, together * room), :], fmri_ref[...])
        for inner in range(together):
            kept = jnp.where(voxel < count_ref[start + inner], rows[inner * room:(inner + 1) * room], 0.0)
            out_ref[pl.ds((start + inner) * room, room), :] = kept.astype(jnp.bfloat16)


def bucketed(half, subject, voxel_count, shift, fmri, after):
    samples, voxels = fmri.shape
    vmem = pl.BlockSpec(memory_space=pltpu.VMEM)
    smem = pl.BlockSpec(memory_space=pltpu.SMEM)
    return pl.pallas_call(
        functools.partial(bucket_kernel, half),
        name="bucket_rows",
        in_specs=[vmem, smem, smem, vmem, pl.BlockSpec(memory_space=pl.ANY)],
        out_specs=(vmem, vmem),
        out_shape=(
            jax.ShapeDtypeStruct((samples, voxels), jnp.bfloat16),
            jax.ShapeDtypeStruct((samples, samples), jnp.bfloat16),
        ),
        compiler_params=params(60),
    )(subject.reshape(1, samples), voxel_count, shift, fmri, after)


def project_kernel(half_ref, rows_ref, map_ref, after_ref, out_ref):
    width = out_ref.shape[2]
    for block in range(out_ref.shape[0]):
        value = product(rows_ref[...], map_ref[0, :, block * width:(block + 1) * width])
        out_ref[block] = value.astype(jnp.bfloat16)


def projected(rows, maps, half, after):
    count, voxels = rows.shape
    blocks = H0 * W0 // 2
    width = maps.shape[2] // (2 * blocks)
    return pl.pallas_call(
        project_kernel,
        name="project_rows",
        grid_spec=pltpu.PrefetchScalarGridSpec(
            num_scalar_prefetch=1,
            grid=(blocks // 2,),
            in_specs=[
                pl.BlockSpec((count, voxels), lambda step, half: (0, 0)),
                pl.BlockSpec((1, voxels, 2 * width), lambda step, half: (0, 0, half[0] * (blocks // 2) + step)),
                pl.BlockSpec(memory_space=pl.ANY),
            ],
            out_specs=pl.BlockSpec((2, count, width), lambda step, half: (step, 0, 0)),
        ),
        out_shape=jax.ShapeDtypeStruct((blocks, count, width), jnp.bfloat16),
        compiler_params=params(60, True),
        cost_estimate=pl.CostEstimate(
            flops=count * voxels * maps.shape[2],
            bytes_accessed=voxels * maps.shape[2],
            transcendentals=0,
        ),
    )(half, rows, maps, after)


def collect_kernel(place_a_ref, place_b_ref, first_ref, second_ref, out_ref):
    subjects, blocks, room, width = first_ref.shape
    for block in range(blocks):
        value = None
        for place_ref, ref in ((place_a_ref, first_ref), (place_b_ref, second_ref)):
            rows = jnp.concatenate([ref[subject, block] for subject in range(subjects)], axis=0)
            term = product_tn(place_ref[...], rows)
            value = term if value is None else value + term
        out_ref[:, pl.ds(block * width, width)] = value.astype(jnp.bfloat16)


def collected(places, first, second):
    samples = places[0].shape[1]
    return pl.pallas_call(
        collect_kernel,
        name="collect_rows",
        out_shape=jax.ShapeDtypeStruct((samples, first.shape[1] * first.shape[3]), jnp.bfloat16),
        compiler_params=params(16),
    )(*places, first, second)


def finish_kernel(third_rows, side_ref, own_a, own_b, own_c, other_a, other_b, other_c, first_ref, second_ref, third_ref):
    side = side_ref[0]
    rows = own_a.shape[0]
    for at, (source, half) in enumerate(((own_a, side), (own_b, side), (other_a, 1 - side), (other_b, 1 - side))):
        start = pl.multiple_of((2 * half + at % 2) * rows, rows)
        first_ref[pl.ds(start, rows), :] = source[...]
    out_chan = second_ref.shape[1]
    mid_chan = second_ref.shape[0] // 16
    for parity in (0, 1):
        mine = side == parity
        for which in (0, 1):
            for pair in (0, 1):
                here = pl.ds((2 * which + pair) * mid_chan, mid_chan)
                value = jnp.where(mine, own_c[here, :].astype(jnp.float32), other_c[here, :].astype(jnp.float32))
                for inner in (0, 1):
                    col_tap = COL_TAPS[2 * pair + inner]
                    to = pl.ds((ROW_TAPS[parity][which] * 4 + col_tap) * mid_chan, mid_chan)
                    second_ref[to, :] = value[:, inner * out_chan:(inner + 1) * out_chan].astype(jnp.bfloat16)
        here = pl.ds(4 * mid_chan, third_rows)
        value = jnp.where(mine, own_c[here, :].astype(jnp.float32), other_c[here, :].astype(jnp.float32)).T
        chan = third_ref.shape[0]
        inputs = third_rows // 2
        for which in (0, 1):
            for slot, col_tap in enumerate(COL_TAPS):
                to = pl.ds((ROW_TAPS[parity][which] * 4 + col_tap) * inputs, inputs)
                piece = value[slot * chan:(slot + 1) * chan, which * inputs:(which + 1) * inputs]
                third_ref[:, to] = piece.astype(jnp.bfloat16)


def finished(side, own, other, third_rows):
    rows, lanes = own[0].shape
    mid_chan = (own[2].shape[0] - third_rows) // 4
    vmem = pl.BlockSpec(memory_space=pltpu.VMEM)
    return pl.pallas_call(
        functools.partial(finish_kernel, third_rows),
        name="finish_gradients",
        in_specs=[pl.BlockSpec(memory_space=pltpu.SMEM)] + [vmem] * 6,
        out_specs=(vmem, vmem, vmem),
        out_shape=(
            jax.ShapeDtypeStruct((4 * rows, lanes), jnp.bfloat16),
            jax.ShapeDtypeStruct((16 * mid_chan, lanes // 2), jnp.bfloat16),
            jax.ShapeDtypeStruct((lanes // 4, 8 * third_rows), jnp.bfloat16),
        ),
        compiler_params=params(24),
    )(side, *own, *other)


def rounded(values):
    return lax.optimization_barrier(values.astype(jnp.bfloat16))


def bit_pairs(axis):
    size = lax.axis_size(axis)
    bits = []
    bit = 1
    while bit < size:
        bits.append((axis, bit))
        bit *= 2
    return bits


def upper(hop):
    axis, bit = hop
    return (lax.axis_index(axis) // bit) % 2


def place_of(step):
    return sum(upper(hop) * 2 ** at for at, hop in enumerate(step))


def exchanged(values, step, change):
    axis = step[0][0]
    flip = sum(hop[1] for at, hop in enumerate(step) if change >> at & 1)
    return lax.ppermute(values, axis, [(at, at ^ flip) for at in range(lax.axis_size(axis))])


def summed(terms):
    value = terms[0]
    for term in terms[1:]:
        value = value.astype(jnp.float32) + term.astype(jnp.float32)
    return value


def shared(chains, step):
    ways = 2 ** len(step)
    place = place_of(step)

    def part(terms, which):
        size = terms[0].shape[0] // ways
        return summed([lax.dynamic_slice_in_dim(term, which * size, size, 0) for term in terms])

    arrived = []
    for change in range(1, ways):
        sent = [part(terms, place ^ change).astype(jnp.bfloat16) for terms in chains]
        joined = jnp.concatenate(sent, axis=0) if len(sent) > 1 else sent[0]
        arrived.append(exchanged(joined, step, change))
    result = []
    start = 0
    for terms in chains:
        size = terms[0].shape[0] // ways
        result.append([part(terms, place)] + [values[start:start + size] for values in arrived])
        start += size
    return result


def gathered(chains, step):
    ways = 2 ** len(step)
    joined = jnp.concatenate(chains, axis=0) if len(chains) > 1 else chains[0]
    pieces = [joined] + [exchanged(joined, step, change) for change in range(1, ways)]
    place = place_of(step)
    result = []
    start = 0
    for values in chains:
        size = values.shape[0]
        out = jnp.concatenate([values] * ways, axis=0)
        for change in range(1, ways):
            piece = pieces[change][start:start + size]
            out = lax.dynamic_update_slice_in_dim(out, piece, (place ^ change) * size, 0)
        result.append(out)
        start += size
    return result


def over_chains(move, chains, steps):
    result = [None] * len(chains)
    for step in {tuple(step): step for step in steps}.values():
        members = [at for at, own in enumerate(steps) if own == step]
        for at, moved_chain in zip(members, move([chains[at] for at in members], step)):
            result[at] = moved_chain
    return result


def shards(fmri, subject, ridge_maps, voxel_count, w_first, w_second, w_third, target):
    dp_count = lax.axis_size("dp")
    holders = lax.axis_size("vox")
    samp_dev = fmri.shape[0]
    vox_local = fmri.shape[1]
    mid_chan = w_first.shape[1]
    last_chan = w_second.shape[1]
    room = samp_dev // dp_count
    vox_bits = bit_pairs("vox")
    dp_bits = bit_pairs("dp")
    side = upper(vox_bits[0]).astype(jnp.int32).reshape(1)
    shift = (lax.axis_index("vox") * vox_local).astype(jnp.int32).reshape(1)
    first, place_first = bucketed(0, subject, voxel_count, shift, fmri, voxel_count)
    second, place_second = bucketed(1, subject, voxel_count, shift, fmri, place_first)

    def routed(rows):
        sent = rows.reshape(dp_count, room, rows.shape[1])
        return lax.all_to_all(sent, "dp", split_axis=0, concat_axis=0, tiled=True).reshape(rows.shape)

    def core_summed(rows, after):
        sent = projected(rows, ridge_maps, 1 - side, after)
        received = exchanged(sent, vox_bits[:1], 1)
        return [projected(rows, ridge_maps, side, sent), received]

    def vox_summed(terms):
        for hop in vox_bits[1:]:
            terms, = shared([terms], [hop])
        return terms

    def returned(terms):
        latent_part = rounded(summed(terms))
        blocks, _, width = latent_part.shape
        sent = latent_part.reshape(blocks, dp_count, room, width).swapaxes(0, 1)
        return lax.all_to_all(sent, "dp", split_axis=0, concat_axis=0, tiled=True)

    first = routed(first)
    second = routed(second)
    terms_first = vox_summed(core_summed(first, voxel_count))
    terms_second = core_summed(second, terms_first[1])
    core_second = terms_second[1]
    pair_two = paired_weight(w_second, mid_chan)
    pair_three = paired_weight(w_third, last_chan)
    target_rows = spatial_first(target, core_second)
    terms_first, terms_second = lax.optimization_barrier((terms_first, terms_second))
    terms_second = vox_summed(terms_second)
    places = (place_first, place_second)
    own_rows = collected(places, returned(terms_first), returned(terms_second))
    own_rows = own_rows.reshape(holders, samp_dev // holders, own_rows.shape[1])
    latent = lax.all_to_all(own_rows, "vox", split_axis=0, concat_axis=0, tiled=True)
    count = latent.shape[1]
    decoded_rows, grad_one, kept_tail, sent_tail = decoder(side, latent, w_first, pair_two, pair_three, target_rows)
    parts_tail = [kept_tail, exchanged(sent_tail, vox_bits[:1], 1)]
    sent = first_grad(1 - side, latent, grad_one, grad_one)
    received = exchanged(sent, vox_bits[:1], 1)
    kept = first_grad(side, latent, grad_one, sent)
    third_rows = pair_three.shape[1]
    quarter = w_first.shape[0] // 4
    across = [[hop] for hop in vox_bits[1:]]
    near = [dp_bits[:1]]
    along = [[hop] for hop in dp_bits[1:]]
    routes = (across + near + along, near + across + along, along[:1] + across + near + along[1:])
    parts = [[kept[:quarter], received[:quarter]], [kept[quarter:], received[quarter:]], parts_tail]
    decoded = sample_first(decoded_rows, count, w_third.shape[1], received)
    for stage in range(len(routes[0])):
        parts = over_chains(shared, parts, [route[stage] for route in routes])
        *tied, decoded = lax.optimization_barrier(tuple(terms[1] for terms in parts) + (decoded,))
        parts = [terms[:1] + [arrived] + terms[2:] for terms, arrived in zip(parts, tied)]
    shares = [summed(terms).astype(jnp.bfloat16) for terms in parts]
    for stage in reversed(range(len(routes[0]))):
        shares = over_chains(gathered, shares, [route[stage] for route in routes])
        shares = list(lax.optimization_barrier(tuple(shares)))
    others = [exchanged(values, vox_bits[:1], 1) for values in shares]
    total_first, total_second, third = finished(side, shares, others, third_rows)
    total_third = third.T
    return (decoded, total_first, total_second, total_third)


def solution(mesh):
    placed = (
        P("dp", "vox"),
        P("dp", None),
        P("dp", "vox", None),
        P(),
        P(),
        P(),
        P(),
        P(("dp", "vox"), None, None, None),
    )
    return jax.shard_map(
        shards,
        mesh=mesh,
        in_specs=placed,
        out_specs=(P(("dp", "vox"), None, None, None), P(), P(), P()),
        check_vma=False,
    )
```

```python
import functools
import jax
import jax.numpy as jnp
from jax import lax
from jax.experimental import pallas as pl
from jax.sharding import PartitionSpec as P
from jax.experimental.pallas import tpu as pltpu

H0 = 2
W0 = 4
SAMP_DEV = 256
ROW_TAPS = ((1, 3), (2, 0))
ROW_SHIFT = (-1, 1)
COL_TAPS = (1, 2, 3, 0)


def paired_weight(weights, in_chan):
    out_chan = weights.shape[1]
    kernel = weights.reshape(4, 4, in_chan, out_chan)
    halves = []
    for parity in (0, 1):
        rows = []
        for row_tap in ROW_TAPS[parity]:
            rows.append(jnp.concatenate([kernel[row_tap, col_tap] for col_tap in COL_TAPS], axis=1))
        halves.append(jnp.concatenate(rows, axis=0))
    return jnp.stack(halves)


def product(left, right):
    return jnp.dot(left, right, preferred_element_type=jnp.float32)


def product_nt(left, right):
    return lax.dot_general(left, right, (((1,), (1,)), ((), ())), preferred_element_type=jnp.float32)


def product_tn(left, right):
    return lax.dot_general(left, right, (((0,), (0,)), ((), ())), preferred_element_type=jnp.float32)


def gelu_pair(value):
    root = 0.7978845608028654
    square = value * value
    tanh = jnp.tanh(root * (value + 0.044715 * (square * value)))
    half = 0.5 * (1.0 + tanh)
    slope = half + (0.5 * value) * (1.0 - tanh * tanh) * (root + (3 * 0.044715 * root) * square)
    return value * half, slope


def up_rows(product_ref, act_ref, slope_ref, act_row, slope_row, count, breadth, out_chan):
    width = 2 * out_chan
    for col in range(breadth):
        here = pl.ds(col * count, count)
        for col_par in (0, 1):
            lanes = pl.ds(col_par * out_chan, out_chan)
            side = pl.ds(width + col_par * out_chan, out_chan)
            value = product_ref[here, lanes]
            other = col - 1 if col_par == 0 else col + 1
            if 0 <= other < breadth:
                value = value + product_ref[pl.ds(other * count, count), side]
            act, slope = gelu_pair(value)
            rows = pl.ds((2 * col + col_par) * count, count)
            act_ref[act_row, rows, :] = act.astype(jnp.bfloat16)
            slope_ref[slope_row, rows, :] = slope


def holder_of(block, holders):
    bits = holders.bit_length() - 1
    depth = (H0 * W0).bit_length() - 1
    owner = sum(((block >> (depth - 1 - at)) & 1) << at for at in range(bits))
    return owner, block & (2 ** (depth - bits) - 1)


def latent_row(latent_ref, row):
    holders = latent_ref.shape[0]
    width = latent_ref.shape[2] * holders // (H0 * W0)
    pieces = []
    for col in range(W0):
        owner, place = holder_of(row * W0 + col, holders)
        pieces.append(latent_ref[owner, :, pl.ds(place * width, width)])
    return jnp.concatenate(pieces, axis=0)


def forward_part(count, latent_ref, w_one_ref, w_two_ref, act_one_ref, slope_one_ref, act_two_ref, slope_two_ref, tmp_one, tmp_two):
    in_chan = w_one_ref.shape[0] // 16
    mid_chan = w_two_ref.shape[1] // 2
    out_chan = w_two_ref.shape[2] // 4

    for row in range(H0):
        for parity in (0, 1):
            other = row + ROW_SHIFT[parity]
            for slot, col_tap in enumerate(COL_TAPS):
                lanes = pl.ds(slot * mid_chan, mid_chan)
                taps = pl.ds((ROW_TAPS[parity][0] * 4 + col_tap) * in_chan, in_chan)
                value = product(latent_row(latent_ref, row), w_one_ref[taps, :])
                if 0 <= other < H0:
                    taps = pl.ds((ROW_TAPS[parity][1] * 4 + col_tap) * in_chan, in_chan)
                    value = value + product(latent_row(latent_ref, other), w_one_ref[taps, :])
                tmp_one[:, lanes] = value
            at = 2 * row + parity
            up_rows(tmp_one, act_one_ref, slope_one_ref, at, at, count, W0, mid_chan)
    height = 2 * H0
    breadth = 2 * W0
    act_two_ref[0] = jnp.zeros_like(act_two_ref[0])
    act_two_ref[2 * height + 1] = jnp.zeros_like(act_two_ref[0])
    for row in range(height):
        for parity in (0, 1):
            tmp_two[...] = product(act_one_ref[row], w_two_ref[parity, :mid_chan, :])
            other = row + ROW_SHIFT[parity]
            if 0 <= other < height:
                tmp_two[...] += product(act_one_ref[other], w_two_ref[parity, mid_chan:, :])
            at = 2 * row + parity
            up_rows(tmp_two, act_two_ref, slope_two_ref, at + 1, at, count, breadth, out_chan)


def last_part(count, step, steps, act_ref, slope_ref, w_ref, target_ref, decoded_ref, grad_ref, kgrad_ref, tmp, grads, adj):
    breadth = act_ref.shape[1] // count
    in_chan = act_ref.shape[2]
    lanes = 2 * (w_ref.shape[2] // 4)

    @pl.when(step == 0)
    def _():
        adj[...] = jnp.zeros_like(adj)
        kgrad_ref[...] = jnp.zeros_like(kgrad_ref)
        grads[...] = jnp.zeros_like(grads)

    low = lax.broadcasted_iota(jnp.int32, (count, lanes), 1) < lanes // 2
    for parity in (0, 1):
        other = step + 1 + ROW_SHIFT[parity]
        left = jnp.concatenate([act_ref[step + 1], act_ref[other]], axis=1)
        tmp[...] = product(left, w_ref[parity])
        zero = jnp.zeros((count, lanes), jnp.float32)
        for col in range(breadth):
            here = pl.ds(col * count, count)
            before = tmp[pl.ds((col - 1) * count, count), lanes:] if col > 0 else zero
            after = tmp[pl.ds((col + 1) * count, count), lanes:] if col < breadth - 1 else zero
            value = tmp[here, :lanes] + jnp.where(low, before, after)
            decoded_ref[parity, here, :] = value.astype(jnp.bfloat16)
            grad = (value - target_ref[parity, here, :].astype(jnp.float32)) * (1.0 / SAMP_DEV)
            grads[pl.ds((col + 1) * count, count), :] = grad
        pieces = []
        for col in range(breadth):
            before = grads[pl.ds(col * count, count), :]
            here = grads[pl.ds((col + 1) * count, count), :]
            after = grads[pl.ds((col + 2) * count, count), :]
            side = jnp.where(low, after, before)
            pieces.append(jnp.concatenate([here.astype(jnp.bfloat16), side.astype(jnp.bfloat16)], axis=1))
        taps = jnp.concatenate(pieces, axis=0)
        kgrad_ref[parity] += product_tn(left, taps)
        back = product_nt(taps, w_ref[parity])
        adj[step + 1] += back[:, :in_chan]
        adj[other] += back[:, in_chan:]

    @pl.when(step == steps - 1)
    def _():
        def finish(row, carry):
            upstream = adj[row + 1].astype(jnp.bfloat16).astype(jnp.float32)
            grad_ref[row] = (upstream * slope_ref[row]).astype(jnp.bfloat16)
            return carry

        lax.fori_loop(0, steps, finish, 0)


def side_taps(grad_ref, row, count, breadth):
    def at(col):
        if 0 <= col < 2 * breadth:
            return grad_ref[row, pl.ds(col * count, count), :]
        return jnp.zeros((count, grad_ref.shape[2]), jnp.bfloat16)

    pieces = []
    for col in range(breadth):
        pieces.append(jnp.concatenate([at(2 * col), at(2 * col + 1), at(2 * col + 2), at(2 * col - 1)], axis=1))
    return jnp.concatenate(pieces, axis=0)


def backward_part(count, side_ref, latent_ref, act_ref, slope_ref, w_ref, grad_two_ref, third_ref, grad_one, kept_ref, sent_ref, adj, total_one, total_two):
    side = side_ref[0]

    def put(half, rows, values):
        @pl.when(side == half)
        def _():
            kept_ref[rows, :] = values().astype(jnp.bfloat16)

        @pl.when(side != half)
        def _():
            sent_ref[rows, :] = values().astype(jnp.bfloat16)

    height = act_ref.shape[0]
    breadth = act_ref.shape[1] // count
    mid_chan = act_ref.shape[2]
    out_chan = grad_two_ref.shape[2]
    for row in range(height):
        for parity in (0, 1):
            taps = side_taps(grad_two_ref, 2 * row + parity, count, breadth)
            back = product_nt(taps, w_ref[parity])
            other = row + ROW_SHIFT[parity]
            if parity == 0 and row == 0:
                adj[0] = back[:, :mid_chan]
            else:
                adj[row] += back[:, :mid_chan]
            if 0 <= other < height:
                if parity == 0:
                    adj[other] += back[:, mid_chan:]
                else:
                    adj[other] = back[:, mid_chan:]
            mine = product_tn(act_ref[row], taps)
            if row == 0:
                total_two[parity, :mid_chan, :] = mine
            else:
                total_two[parity, :mid_chan, :] += mine
            if 0 <= other < height:
                far = product_tn(act_ref[other], taps)
                if row == (1 if parity == 0 else 0):
                    total_two[parity, mid_chan:, :] = far
                else:
                    total_two[parity, mid_chan:, :] += far
    for row in range(height):
        upstream = adj[row].astype(jnp.bfloat16).astype(jnp.float32)
        grad_one[row] = (upstream * slope_ref[row]).astype(jnp.bfloat16)
    in_chan = latent_ref.shape[0] * latent_ref.shape[2] // (H0 * W0)
    tail = 8 * in_chan
    lanes = 2 * out_chan
    for parity in (0, 1):
        for which in (0, 1):
            for pair in (0, 1):
                rows = pl.ds(tail + (2 * which + pair) * mid_chan, mid_chan)
                above, left_edge = which * mid_chan, pair * lanes
                put(
                    parity,
                    rows,
                    lambda: total_two[parity, above:above + mid_chan, left_edge:left_edge + lanes],
                )
        put(parity, pl.ds(tail + 4 * mid_chan, third_ref.shape[1]), lambda: third_ref[parity])
    for row_tap in range(4):
        parity = 0 if row_tap in ROW_TAPS[0] else 1
        shift = ROW_SHIFT[parity] if ROW_TAPS[parity][1] == row_tap else 0
        rows = [row for row in range(H0) if 0 <= row + shift < H0]
        lefts = [latent_row(latent_ref, row + shift) for row in rows]
        rights = [side_taps(grad_one, 2 * row + parity, count, W0) for row in rows]
        left = jnp.concatenate(lefts, axis=0) if len(lefts) > 1 else lefts[0]
        right = jnp.concatenate(rights, axis=0) if len(rights) > 1 else rights[0]
        total_one[...] = product_tn(left, right)
        for slot, col_tap in enumerate(COL_TAPS):
            to = pl.ds(((row_tap % 2) * 4 + col_tap) * in_chan, in_chan)
            put(row_tap // 2, to, lambda: total_one[:, slot * mid_chan:(slot + 1) * mid_chan])


def decoder_kernel(
    count, side_ref, latent_ref, w_one_ref, w_two_ref, w_three_ref, target_ref,
    decoded_ref, kept_ref, sent_ref,
    grad_one, act_one, slope_one, act_two, slope_two, grad_two, kgrad_three, tmp_one, tmp_two, tmp_three, grads, adj_two, adj_one, total_one, total_two,
):
    step = pl.program_id(0)
    steps = pl.num_programs(0)

    @pl.when(step == 0)
    def _():
        forward_part(count, latent_ref, w_one_ref, w_two_ref, act_one, slope_one, act_two, slope_two, tmp_one, tmp_two)

    last_part(
        count, step, steps, act_two, slope_two, w_three_ref, target_ref, decoded_ref, grad_two, kgrad_three, tmp_three, grads, adj_two
    )

    @pl.when(step == steps - 1)
    def _():
        backward_part(
            count, side_ref, latent_ref, act_one, slope_one, w_two_ref, grad_two, kgrad_three,
            grad_one, kept_ref, sent_ref, adj_one, total_one, total_two,
        )


def params(mebibytes, gridded=False):
    order = ("arbitrary",) if gridded else None
    return pltpu.CompilerParams(vmem_limit_bytes=mebibytes * 1024 * 1024, dimension_semantics=order)


def decoder(side, latent, w_one, w_two, w_three, target):
    count = latent.shape[1]
    mid_chan = w_two.shape[1] // 2
    out_chan = w_two.shape[2] // 4
    height, breadth = 2 * H0, 2 * W0
    steps, flat, lanes = target.shape[0] // 2, target.shape[1], target.shape[2]
    third_rows = w_three.shape[1]

    def whole(shape):
        return pl.BlockSpec(shape, lambda step: (0,) * len(shape))

    act_one = (height, breadth * count, mid_chan)
    act_two = (2 * height, flat, out_chan)
    padded = (2 * height + 2, flat, out_chan)
    in_chan = w_one.shape[0] // 16
    share = (8 * in_chan + 4 * mid_chan + third_rows, mid_chan)
    single = pl.Buffered(1)
    return pl.pallas_call(
        functools.partial(decoder_kernel, count),
        name="decoder",
        grid=(steps,),
        in_specs=[
            pl.BlockSpec(memory_space=pltpu.SMEM),
            pl.BlockSpec(latent.shape, lambda step: (0, 0, 0), pipeline_mode=single),
            pl.BlockSpec(w_one.shape, lambda step: (0, 0), pipeline_mode=single),
            pl.BlockSpec(w_two.shape, lambda step: (0, 0, 0), pipeline_mode=single),
            pl.BlockSpec(w_three.shape, lambda step: (0, 0, 0), pipeline_mode=single),
            pl.BlockSpec((2, flat, lanes), lambda step: (step, 0, 0)),
        ],
        out_specs=(
            pl.BlockSpec((2, flat, lanes), lambda step: (step, 0, 0)),
            whole(share),
            whole(share),
        ),
        out_shape=(
            jax.ShapeDtypeStruct(target.shape, jnp.bfloat16),
            jax.ShapeDtypeStruct(share, jnp.bfloat16),
            jax.ShapeDtypeStruct(share, jnp.bfloat16),
        ),
        scratch_shapes=[
            pltpu.VMEM(act_one, jnp.bfloat16),
            pltpu.VMEM(act_one, jnp.bfloat16),
            pltpu.VMEM(act_one, jnp.float32),
            pltpu.VMEM(padded, jnp.bfloat16),
            pltpu.VMEM(act_two, jnp.float32),
            pltpu.VMEM(act_two, jnp.bfloat16),
            pltpu.VMEM(w_three.shape, jnp.float32),
            pltpu.VMEM((W0 * count, 4 * mid_chan), jnp.float32),
            pltpu.VMEM((breadth * count, 4 * out_chan), jnp.float32),
            pltpu.VMEM((flat, 2 * lanes), jnp.float32),
            pltpu.VMEM((flat + 2 * count, lanes), jnp.float32),
            pltpu.VMEM(padded, jnp.float32),
            pltpu.VMEM(act_one, jnp.float32),
            pltpu.VMEM((in_chan, 4 * mid_chan), jnp.float32),
            pltpu.VMEM(w_two.shape, jnp.float32),
        ],
        compiler_params=params(60, True),
    )(side, latent, w_one, w_two, w_three, target)


def spatial_first_kernel(grid_ref, after_ref, rows_ref, tmp):
    count, height, breadth, chan = grid_ref.shape
    for row in range(height):
        tmp[...] = grid_ref[:, row].astype(jnp.float32)
        even = tmp[:, pl.ds(0, breadth // 2, 2), :]
        odd = tmp[:, pl.ds(1, breadth // 2, 2), :]
        turned = jnp.swapaxes(jnp.concatenate([even, odd], axis=2), 0, 1)
        rows_ref[row] = turned.reshape(breadth // 2 * count, 2 * chan).astype(jnp.bfloat16)


def spatial_first(grid, after):
    count, height, breadth, chan = grid.shape
    per = 4
    flat = breadth // 2 * count
    return pl.pallas_call(
        spatial_first_kernel,
        name="spatial_first",
        grid=(height // per,),
        in_specs=[
            pl.BlockSpec((count, per, breadth, chan), lambda step: (0, step, 0, 0)),
            pl.BlockSpec(memory_space=pl.ANY),
        ],
        out_specs=pl.BlockSpec((per, flat, 2 * chan), lambda step: (step, 0, 0)),
        out_shape=jax.ShapeDtypeStruct((height, flat, 2 * chan), jnp.bfloat16),
        scratch_shapes=[pltpu.VMEM((count, breadth, chan), jnp.float32)],
        compiler_params=params(20, True),
        cost_estimate=pl.CostEstimate(flops=0, bytes_accessed=28000000, transcendentals=0),
    )(grid, after)


def sample_first_kernel(rows_ref, after_ref, out_ref, tmp):
    height = rows_ref.shape[0]
    count, _, breadth, chan = out_ref.shape
    for row in range(height):
        value = rows_ref[row].astype(jnp.float32).reshape(breadth // 2, count, 2 * chan)
        turned = jnp.swapaxes(value, 0, 1)
        tmp[:, pl.ds(0, breadth // 2, 2), :] = turned[:, :, :chan]
        tmp[:, pl.ds(1, breadth // 2, 2), :] = turned[:, :, chan:]
        out_ref[:, row] = tmp[...].astype(jnp.bfloat16)


def sample_first(rows, count, chan, after):
    height, flat, lanes = rows.shape
    breadth = 2 * flat // count
    per = 4
    return pl.pallas_call(
        sample_first_kernel,
        name="sample_first",
        grid=(height // per,),
        in_specs=[
            pl.BlockSpec((per, flat, lanes), lambda step: (step, 0, 0)),
            pl.BlockSpec(memory_space=pl.ANY),
        ],
        out_specs=pl.BlockSpec((count, per, breadth, chan), lambda step: (0, step, 0, 0)),
        out_shape=jax.ShapeDtypeStruct((count, height, breadth, chan), jnp.bfloat16),
        scratch_shapes=[pltpu.VMEM((count, breadth, chan), jnp.float32)],
        compiler_params=params(20, True),
        cost_estimate=pl.CostEstimate(flops=0, bytes_accessed=28000000, transcendentals=0),
    )(rows, after)


def bucket_kernel(half, subject_ref, count_ref, shift_ref, fmri_ref, after_ref, out_ref, place_ref):
    samples, voxels = fmri_ref.shape
    slots = out_ref.shape[0]
    subjects = count_ref.shape[0]
    room = slots // subjects
    owner = subject_ref[...]
    name = lax.broadcasted_iota(jnp.int32, (subjects, samples), 0)
    onehot = jnp.where(owner == name, 1.0, 0.0)
    row = lax.broadcasted_iota(jnp.int32, (samples, samples), 0)
    col = lax.broadcasted_iota(jnp.int32, (samples, samples), 1)
    before = jnp.where(row < col, 1.0, 0.0).astype(jnp.bfloat16)
    earlier = product(onehot.astype(jnp.bfloat16), before)
    rank = jnp.sum(earlier * onehot, axis=0, keepdims=True).astype(jnp.int32) - half * room
    position = jnp.where((rank >= 0) & (rank < room), owner * room + rank, -1)
    slot = lax.broadcasted_iota(jnp.int32, (slots, samples), 0)
    place_ref[...] = jnp.where(slot == position, 1.0, 0.0).astype(jnp.bfloat16)
    voxel = lax.broadcasted_iota(jnp.int32, (room, voxels), 1) + shift_ref[0]
    together = max(1, 64 // room)
    for start in range(0, subjects, together):
        rows = product(place_ref[pl.ds(start * room, together * room), :], fmri_ref[...])
        for inner in range(together):
            kept = jnp.where(voxel < count_ref[start + inner], rows[inner * room:(inner + 1) * room], 0.0)
            out_ref[pl.ds((start + inner) * room, room), :] = kept.astype(jnp.bfloat16)


def bucketed(half, subject, voxel_count, shift, fmri, after):
    samples, voxels = fmri.shape
    vmem = pl.BlockSpec(memory_space=pltpu.VMEM)
    smem = pl.BlockSpec(memory_space=pltpu.SMEM)
    return pl.pallas_call(
        functools.partial(bucket_kernel, half),
        name="bucket_rows",
        in_specs=[vmem, smem, smem, vmem, pl.BlockSpec(memory_space=pl.ANY)],
        out_specs=(vmem, vmem),
        out_shape=(
            jax.ShapeDtypeStruct((samples, voxels), jnp.bfloat16),
            jax.ShapeDtypeStruct((samples, samples), jnp.bfloat16),
        ),
        compiler_params=params(60),
    )(subject.reshape(1, samples), voxel_count, shift, fmri, after)


def project_kernel(quarter_ref, rows_ref, map_ref, *after_and_out):
    out_ref = after_and_out[-1]
    width = out_ref.shape[2]
    for block in range(out_ref.shape[0]):
        value = product(rows_ref[...], map_ref[0, :, block * width:(block + 1) * width])
        out_ref[block] = value.astype(jnp.bfloat16)


def projected(rows, maps, part, after, parts):
    count, voxels = rows.shape
    blocks = H0 * W0 // parts
    width = maps.shape[2] // (H0 * W0)
    step_blocks = max(1, blocks // 2)
    steps = blocks // step_blocks
    return pl.pallas_call(
        project_kernel,
        name="project_rows",
        grid_spec=pltpu.PrefetchScalarGridSpec(
            num_scalar_prefetch=1,
            grid=(steps,),
            in_specs=[
                pl.BlockSpec((count, voxels), lambda step, part: (0, 0)),
                pl.BlockSpec((1, voxels, step_blocks * width), lambda step, part: (0, 0, part[0] * steps + step)),
            ] + [pl.BlockSpec(memory_space=pl.ANY)] * len(after),
            out_specs=pl.BlockSpec((step_blocks, count, width), lambda step, part: (step, 0, 0)),
        ),
        out_shape=jax.ShapeDtypeStruct((blocks, count, width), jnp.bfloat16),
        compiler_params=params(60, True),
        cost_estimate=pl.CostEstimate(
            flops=2 * count * voxels * maps.shape[2] // parts,
            bytes_accessed=2 * voxels * maps.shape[2] // parts,
            transcendentals=0,
        ),
    )(part, rows, maps, *after)


def collect_kernel(place_a_ref, place_b_ref, first_ref, second_ref, *after_and_out):
    out_ref = after_and_out[-1]
    subjects, blocks, room, width = first_ref.shape
    for block in range(blocks):
        value = None
        for place_ref, ref in ((place_a_ref, first_ref), (place_b_ref, second_ref)):
            rows = jnp.concatenate([ref[subject, block] for subject in range(subjects)], axis=0)
            term = product_tn(place_ref[...], rows)
            value = term if value is None else value + term
        out_ref[:, pl.ds(block * width, width)] = value.astype(jnp.bfloat16)


def collected(places, first, second, after):
    samples = places[0].shape[1]
    vmem = pl.BlockSpec(memory_space=pltpu.VMEM)
    return pl.pallas_call(
        collect_kernel,
        name="collect_rows",
        in_specs=[vmem] * 4 + [pl.BlockSpec(memory_space=pl.ANY)] * len(after),
        out_specs=vmem,
        out_shape=jax.ShapeDtypeStruct((samples, first.shape[1] * first.shape[3]), jnp.bfloat16),
        compiler_params=params(16),
    )(*places, first, second, *after)


def finish_kernel(third_rows, side_ref, own_a, own_b, own_c, other_a, other_b, other_c, first_ref, second_ref, third_ref):
    side = side_ref[0]
    rows = own_a.shape[0]
    for at, (source, half) in enumerate(((own_a, side), (own_b, side), (other_a, 1 - side), (other_b, 1 - side))):
        start = pl.multiple_of((2 * half + at % 2) * rows, rows)
        first_ref[pl.ds(start, rows), :] = source[...]
    out_chan = second_ref.shape[1]
    mid_chan = second_ref.shape[0] // 16
    for parity in (0, 1):
        mine = side == parity
        for which in (0, 1):
            for pair in (0, 1):
                here = pl.ds((2 * which + pair) * mid_chan, mid_chan)
                value = jnp.where(mine, own_c[here, :].astype(jnp.float32), other_c[here, :].astype(jnp.float32))
                for inner in (0, 1):
                    col_tap = COL_TAPS[2 * pair + inner]
                    to = pl.ds((ROW_TAPS[parity][which] * 4 + col_tap) * mid_chan, mid_chan)
                    second_ref[to, :] = value[:, inner * out_chan:(inner + 1) * out_chan].astype(jnp.bfloat16)
        here = pl.ds(4 * mid_chan, third_rows)
        value = jnp.where(mine, own_c[here, :].astype(jnp.float32), other_c[here, :].astype(jnp.float32)).T
        chan = third_ref.shape[0]
        inputs = third_rows // 2
        for which in (0, 1):
            for slot, col_tap in enumerate(COL_TAPS):
                to = pl.ds((ROW_TAPS[parity][which] * 4 + col_tap) * inputs, inputs)
                piece = value[slot * chan:(slot + 1) * chan, which * inputs:(which + 1) * inputs]
                third_ref[:, to] = piece.astype(jnp.bfloat16)


def finished(side, own, other, third_rows):
    rows, lanes = own[0].shape
    mid_chan = (own[2].shape[0] - third_rows) // 4
    vmem = pl.BlockSpec(memory_space=pltpu.VMEM)
    return pl.pallas_call(
        functools.partial(finish_kernel, third_rows),
        name="finish_gradients",
        in_specs=[pl.BlockSpec(memory_space=pltpu.SMEM)] + [vmem] * 6,
        out_specs=(vmem, vmem, vmem),
        out_shape=(
            jax.ShapeDtypeStruct((4 * rows, lanes), jnp.bfloat16),
            jax.ShapeDtypeStruct((16 * mid_chan, lanes // 2), jnp.bfloat16),
            jax.ShapeDtypeStruct((lanes // 4, 8 * third_rows), jnp.bfloat16),
        ),
        compiler_params=params(24),
    )(side, *own, *other)


def rounded(values):
    return lax.optimization_barrier(values.astype(jnp.bfloat16))


def bit_pairs(axis):
    size = lax.axis_size(axis)
    bits = []
    bit = 1
    while bit < size:
        bits.append((axis, bit))
        bit *= 2
    return bits


def upper(hop):
    axis, bit = hop
    return (lax.axis_index(axis) // bit) % 2


def place_of(step):
    return sum(upper(hop) * 2 ** at for at, hop in enumerate(step))


def exchanged(values, step, change):
    axis = step[0][0]
    flip = sum(hop[1] for at, hop in enumerate(step) if change >> at & 1)
    return lax.ppermute(values, axis, [(at, at ^ flip) for at in range(lax.axis_size(axis))])


def summed(terms):
    value = terms[0]
    for term in terms[1:]:
        value = value.astype(jnp.float32) + term.astype(jnp.float32)
    return value


def shared(chains, step):
    ways = 2 ** len(step)
    place = place_of(step)

    def part(terms, which):
        cuts = []
        for term in terms:
            array, start, size = term if isinstance(term, tuple) else (term, 0, term.shape[0])
            cuts.append(lax.dynamic_slice_in_dim(array, start + which * (size // ways), size // ways, 0))
        return summed(cuts)

    arrived = []
    for change in range(1, ways):
        sent = [part(terms, place ^ change).astype(jnp.bfloat16) for terms in chains]
        joined = jnp.concatenate(sent, axis=0) if len(sent) > 1 else sent[0]
        arrived.append(exchanged(joined, step, change))
    result = []
    start = 0
    for terms in chains:
        size = (terms[0][2] if isinstance(terms[0], tuple) else terms[0].shape[0]) // ways
        result.append([part(terms, place)] + [values[start:start + size] for values in arrived])
        start += size
    return result


def gathered(chains, step):
    ways = 2 ** len(step)
    joined = jnp.concatenate(chains, axis=0) if len(chains) > 1 else chains[0]
    pieces = [joined] + [exchanged(joined, step, change) for change in range(1, ways)]
    place = place_of(step)
    result = []
    start = 0
    for values in chains:
        size = values.shape[0]
        out = jnp.concatenate([values] * ways, axis=0)
        for change in range(1, ways):
            piece = pieces[change][start:start + size]
            out = lax.dynamic_update_slice_in_dim(out, piece, (place ^ change) * size, 0)
        result.append(out)
        start += size
    return result


def over_chains(move, chains, steps):
    result = [None] * len(chains)
    for step in {tuple(step): step for step in steps}.values():
        members = [at for at, own in enumerate(steps) if own == step]
        for at, moved_chain in zip(members, move([chains[at] for at in members], step)):
            result[at] = moved_chain
    return result


def shards(fmri, subject, ridge_maps, voxel_count, w_first, w_second, w_third, target):
    dp_count = lax.axis_size("dp")
    holders = lax.axis_size("vox")
    samp_dev = fmri.shape[0]
    vox_local = fmri.shape[1]
    mid_chan = w_first.shape[1]
    last_chan = w_second.shape[1]
    room = samp_dev // dp_count
    vox_bits = bit_pairs("vox")
    dp_bits = bit_pairs("dp")
    side = upper(vox_bits[0]).astype(jnp.int32).reshape(1)
    shift = (lax.axis_index("vox") * vox_local).astype(jnp.int32).reshape(1)
    first, place_first = bucketed(0, subject, voxel_count, shift, fmri, voxel_count)
    second, place_second = bucketed(1, subject, voxel_count, shift, fmri, place_first)

    def routed(rows):
        sent = rows.reshape(dp_count, room, rows.shape[1])
        return lax.all_to_all(sent, "dp", split_axis=0, concat_axis=0, tiled=True).reshape(rows.shape)

    core_bit, cross_bit = upper(vox_bits[0]), upper(vox_bits[1])

    def part_of(*bits):
        return sum(bit * 2 ** at for at, bit in enumerate(bits[::-1])).astype(jnp.int32).reshape(1)

    def to_cross(rows, *after):
        for_core = projected(rows, ridge_maps, part_of(1 - core_bit), after, 2)
        received = exchanged(for_core, vox_bits[:1], 1)
        own = projected(rows, ridge_maps, part_of(core_bit, 1 - cross_bit), (for_core,), 4)
        half = received.shape[0] // 2
        added = lax.dynamic_slice_in_dim(received, (1 - cross_bit) * half, half, 0)
        return summed([own, added]).astype(jnp.bfloat16), lax.dynamic_slice_in_dim(received, cross_bit * half, half, 0)

    def own_part(rows, *after):
        return projected(rows, ridge_maps, part_of(core_bit, cross_bit), after, 4)

    def rest_summed(*terms):
        terms = list(terms)
        for hop in vox_bits[2:]:
            terms, = shared([terms], [hop])
        return terms

    def returned(terms):
        latent_part = rounded(summed(terms))
        blocks, _, width = latent_part.shape
        sent = latent_part.reshape(blocks, dp_count, room, width).swapaxes(0, 1)
        return lax.all_to_all(sent, "dp", split_axis=0, concat_axis=0, tiled=True)

    first = routed(first)
    second = routed(second)
    across_first, added_first = to_cross(first, voxel_count)
    arrived_first = exchanged(across_first, vox_bits[1:2], 1)
    own_first = own_part(first, across_first)
    across_second, added_second = to_cross(second, arrived_first, own_first)
    arrived_second = exchanged(across_second, vox_bits[1:2], 1)
    own_second = own_part(second, across_second)
    terms_first = rest_summed(own_first, added_first, arrived_first)
    pair_two = paired_weight(w_second, mid_chan)
    pair_three = paired_weight(w_third, last_chan)
    target_rows = spatial_first(target, across_second)
    places = (place_first, place_second)
    back_first = returned(terms_first)
    back_first, arrived_second = lax.optimization_barrier((back_first, arrived_second))
    back_second = returned(rest_summed(own_second, added_second, arrived_second))
    own_rows = collected(places, back_first, back_second, (target_rows, pair_two, pair_three))
    own_rows = own_rows.reshape(holders, samp_dev // holders, own_rows.shape[1])
    latent = lax.all_to_all(own_rows, "vox", split_axis=0, concat_axis=0, tiled=True)
    count = latent.shape[1]
    decoded_rows, kept, sent = decoder(side, latent, w_first, pair_two, pair_three, target_rows)
    third_rows = pair_three.shape[1]
    quarter = w_first.shape[0] // 4
    received = exchanged(sent, vox_bits[:1], 1)
    across = [[hop] for hop in vox_bits[1:]]
    near = [dp_bits[:1]]
    along = [[hop] for hop in dp_bits[1:]]
    routes = (across + near + along, near + across + along, along[:1] + across + near + along[1:])
    cuts = ((0, quarter), (quarter, quarter), (2 * quarter, kept.shape[0] - 2 * quarter))
    parts = [[(kept, *cut), (received, *cut)] for cut in cuts]
    decoded = sample_first(decoded_rows, count, w_third.shape[1], received)
    for stage in range(len(routes[0])):
        parts = over_chains(shared, parts, [route[stage] for route in routes])
        *tied, decoded = lax.optimization_barrier(tuple(terms[1] for terms in parts) + (decoded,))
        parts = [terms[:1] + [arrived] + terms[2:] for terms, arrived in zip(parts, tied)]
    shares = [summed(terms).astype(jnp.bfloat16) for terms in parts]
    for stage in reversed(range(len(routes[0]))):
        shares = over_chains(gathered, shares, [route[stage] for route in routes])
        shares = list(lax.optimization_barrier(tuple(shares)))
    others = [exchanged(values, vox_bits[:1], 1) for values in shares]
    total_first, total_second, third = finished(side, shares, others, third_rows)
    total_third = third.T
    return (decoded, total_first, total_second, total_third)


def solution(mesh):
    placed = (
        P("dp", "vox"),
        P("dp", None),
        P("dp", "vox", None),
        P(),
        P(),
        P(),
        P(),
        P(("dp", "vox"), None, None, None),
    )
    return jax.shard_map(
        shards,
        mesh=mesh,
        in_specs=placed,
        out_specs=(P(("dp", "vox"), None, None, None), P(), P(), P()),
        check_vma=False,
    )
```

```python
import functools
import jax
import jax.numpy as jnp
from jax import lax
from jax.experimental import pallas as pl
from jax.sharding import PartitionSpec as P
from jax.experimental.pallas import tpu as pltpu

H0 = 2
W0 = 4
SAMP_DEV = 256
ROW_TAPS = ((1, 3), (2, 0))
ROW_SHIFT = (-1, 1)
COL_TAPS = (1, 2, 3, 0)


def paired_weight(weights, in_chan):
    out_chan = weights.shape[1]
    kernel = weights.reshape(4, 4, in_chan, out_chan)
    halves = []
    for parity in (0, 1):
        rows = []
        for row_tap in ROW_TAPS[parity]:
            rows.append(jnp.concatenate([kernel[row_tap, col_tap] for col_tap in COL_TAPS], axis=1))
        halves.append(jnp.concatenate(rows, axis=0))
    return jnp.stack(halves)


def product(left, right):
    return jnp.dot(left, right, preferred_element_type=jnp.float32)


def product_nt(left, right):
    return lax.dot_general(left, right, (((1,), (1,)), ((), ())), preferred_element_type=jnp.float32)


def product_tn(left, right):
    return lax.dot_general(left, right, (((0,), (0,)), ((), ())), preferred_element_type=jnp.float32)


def gelu_pair(value):
    root = 0.7978845608028654
    square = value * value
    tanh = jnp.tanh(root * (value + 0.044715 * (square * value)))
    half = 0.5 * (1.0 + tanh)
    slope = half + (0.5 * value) * (1.0 - tanh * tanh) * (root + (3 * 0.044715 * root) * square)
    return value * half, slope


def up_rows(product_ref, act_ref, slope_ref, act_row, slope_row, count, breadth, out_chan):
    width = 2 * out_chan
    for col in range(breadth):
        here = pl.ds(col * count, count)
        for col_par in (0, 1):
            lanes = pl.ds(col_par * out_chan, out_chan)
            side = pl.ds(width + col_par * out_chan, out_chan)
            value = product_ref[here, lanes]
            other = col - 1 if col_par == 0 else col + 1
            if 0 <= other < breadth:
                value = value + product_ref[pl.ds(other * count, count), side]
            act, slope = gelu_pair(value)
            rows = pl.ds((2 * col + col_par) * count, count)
            act_ref[act_row, rows, :] = act.astype(jnp.bfloat16)
            slope_ref[slope_row, rows, :] = slope


def holder_of(block, holders):
    bits = holders.bit_length() - 1
    depth = (H0 * W0).bit_length() - 1
    owner = sum(((block >> (depth - 1 - at)) & 1) << at for at in range(bits))
    return owner, block & (2 ** (depth - bits) - 1)


def latent_row(latent_ref, row):
    holders = latent_ref.shape[0]
    width = latent_ref.shape[2] * holders // (H0 * W0)
    pieces = []
    for col in range(W0):
        owner, place = holder_of(row * W0 + col, holders)
        pieces.append(latent_ref[owner, :, pl.ds(place * width, width)])
    return jnp.concatenate(pieces, axis=0)


def forward_part(count, latent_ref, w_one_ref, w_two_ref, act_one_ref, slope_one_ref, act_two_ref, slope_two_ref, tmp_one, tmp_two):
    in_chan = w_one_ref.shape[0] // 16
    mid_chan = w_two_ref.shape[1] // 2
    out_chan = w_two_ref.shape[2] // 4

    for row in range(H0):
        for parity in (0, 1):
            other = row + ROW_SHIFT[parity]
            for slot, col_tap in enumerate(COL_TAPS):
                lanes = pl.ds(slot * mid_chan, mid_chan)
                taps = pl.ds((ROW_TAPS[parity][0] * 4 + col_tap) * in_chan, in_chan)
                value = product(latent_row(latent_ref, row), w_one_ref[taps, :])
                if 0 <= other < H0:
                    taps = pl.ds((ROW_TAPS[parity][1] * 4 + col_tap) * in_chan, in_chan)
                    value = value + product(latent_row(latent_ref, other), w_one_ref[taps, :])
                tmp_one[:, lanes] = value
            at = 2 * row + parity
            up_rows(tmp_one, act_one_ref, slope_one_ref, at, at, count, W0, mid_chan)
    height = 2 * H0
    breadth = 2 * W0
    act_two_ref[0] = jnp.zeros_like(act_two_ref[0])
    act_two_ref[2 * height + 1] = jnp.zeros_like(act_two_ref[0])
    for row in range(height):
        for parity in (0, 1):
            tmp_two[...] = product(act_one_ref[row], w_two_ref[parity, :mid_chan, :])
            other = row + ROW_SHIFT[parity]
            if 0 <= other < height:
                tmp_two[...] += product(act_one_ref[other], w_two_ref[parity, mid_chan:, :])
            at = 2 * row + parity
            up_rows(tmp_two, act_two_ref, slope_two_ref, at + 1, at, count, breadth, out_chan)


def last_part(count, step, steps, act_ref, slope_ref, w_ref, target_ref, decoded_ref, grad_ref, kgrad_ref, tmp, grads, adj):
    breadth = act_ref.shape[1] // count
    in_chan = act_ref.shape[2]
    lanes = 2 * (w_ref.shape[2] // 4)

    @pl.when(step == 0)
    def _():
        adj[...] = jnp.zeros_like(adj)
        kgrad_ref[...] = jnp.zeros_like(kgrad_ref)
        grads[...] = jnp.zeros_like(grads)

    low = lax.broadcasted_iota(jnp.int32, (count, lanes), 1) < lanes // 2
    for parity in (0, 1):
        other = step + 1 + ROW_SHIFT[parity]
        left = jnp.concatenate([act_ref[step + 1], act_ref[other]], axis=1)
        tmp[...] = product(left, w_ref[parity])
        zero = jnp.zeros((count, lanes), jnp.float32)
        for col in range(breadth):
            here = pl.ds(col * count, count)
            before = tmp[pl.ds((col - 1) * count, count), lanes:] if col > 0 else zero
            after = tmp[pl.ds((col + 1) * count, count), lanes:] if col < breadth - 1 else zero
            value = tmp[here, :lanes] + jnp.where(low, before, after)
            decoded_ref[parity, here, :] = value.astype(jnp.bfloat16)
            grad = (value - target_ref[parity, here, :].astype(jnp.float32)) * (1.0 / SAMP_DEV)
            grads[pl.ds((col + 1) * count, count), :] = grad
        pieces = []
        for col in range(breadth):
            before = grads[pl.ds(col * count, count), :]
            here = grads[pl.ds((col + 1) * count, count), :]
            after = grads[pl.ds((col + 2) * count, count), :]
            side = jnp.where(low, after, before)
            pieces.append(jnp.concatenate([here.astype(jnp.bfloat16), side.astype(jnp.bfloat16)], axis=1))
        taps = jnp.concatenate(pieces, axis=0)
        kgrad_ref[parity] += product_tn(left, taps)
        back = product_nt(taps, w_ref[parity])
        adj[step + 1] += back[:, :in_chan]
        adj[other] += back[:, in_chan:]

    @pl.when(step == steps - 1)
    def _():
        def finish(row, carry):
            upstream = adj[row + 1].astype(jnp.bfloat16).astype(jnp.float32)
            grad_ref[row] = (upstream * slope_ref[row]).astype(jnp.bfloat16)
            return carry

        lax.fori_loop(0, steps, finish, 0)


def side_taps(grad_ref, row, count, breadth):
    def at(col):
        if 0 <= col < 2 * breadth:
            return grad_ref[row, pl.ds(col * count, count), :]
        return jnp.zeros((count, grad_ref.shape[2]), jnp.bfloat16)

    pieces = []
    for col in range(breadth):
        pieces.append(jnp.concatenate([at(2 * col), at(2 * col + 1), at(2 * col + 2), at(2 * col - 1)], axis=1))
    return jnp.concatenate(pieces, axis=0)


def backward_part(count, side_ref, latent_ref, act_ref, slope_ref, w_ref, grad_two_ref, third_ref, grad_one, kept_refs, sent_refs, adj, total_one, total_two):
    side = side_ref[0]

    def put(half, first, size, values):
        at = min(first // sent_refs[0].shape[0], 2)
        rows = pl.ds(first - at * sent_refs[0].shape[0], size)

        @pl.when(side == half)
        def _():
            kept_refs[at][rows, :] = values().astype(jnp.bfloat16)

        @pl.when(side != half)
        def _():
            sent_refs[at][rows, :] = values().astype(jnp.bfloat16)

    height = act_ref.shape[0]
    breadth = act_ref.shape[1] // count
    mid_chan = act_ref.shape[2]
    out_chan = grad_two_ref.shape[2]
    for row in range(height):
        for parity in (0, 1):
            taps = side_taps(grad_two_ref, 2 * row + parity, count, breadth)
            back = product_nt(taps, w_ref[parity])
            other = row + ROW_SHIFT[parity]
            if parity == 0 and row == 0:
                adj[0] = back[:, :mid_chan]
            else:
                adj[row] += back[:, :mid_chan]
            if 0 <= other < height:
                if parity == 0:
                    adj[other] += back[:, mid_chan:]
                else:
                    adj[other] = back[:, mid_chan:]
            mine = product_tn(act_ref[row], taps)
            if row == 0:
                total_two[parity, :mid_chan, :] = mine
            else:
                total_two[parity, :mid_chan, :] += mine
            if 0 <= other < height:
                far = product_tn(act_ref[other], taps)
                if row == (1 if parity == 0 else 0):
                    total_two[parity, mid_chan:, :] = far
                else:
                    total_two[parity, mid_chan:, :] += far
    for row in range(height):
        upstream = adj[row].astype(jnp.bfloat16).astype(jnp.float32)
        grad_one[row] = (upstream * slope_ref[row]).astype(jnp.bfloat16)
    in_chan = latent_ref.shape[0] * latent_ref.shape[2] // (H0 * W0)
    tail = 8 * in_chan
    lanes = 2 * out_chan
    for parity in (0, 1):
        for which in (0, 1):
            for pair in (0, 1):
                above, left_edge = which * mid_chan, pair * lanes
                put(
                    parity,
                    tail + (2 * which + pair) * mid_chan,
                    mid_chan,
                    lambda: total_two[parity, above:above + mid_chan, left_edge:left_edge + lanes],
                )
        put(parity, tail + 4 * mid_chan, third_ref.shape[1], lambda: third_ref[parity])
    for row_tap in range(4):
        parity = 0 if row_tap in ROW_TAPS[0] else 1
        shift = ROW_SHIFT[parity] if ROW_TAPS[parity][1] == row_tap else 0
        rows = [row for row in range(H0) if 0 <= row + shift < H0]
        lefts = [latent_row(latent_ref, row + shift) for row in rows]
        rights = [side_taps(grad_one, 2 * row + parity, count, W0) for row in rows]
        left = jnp.concatenate(lefts, axis=0) if len(lefts) > 1 else lefts[0]
        right = jnp.concatenate(rights, axis=0) if len(rights) > 1 else rights[0]
        total_one[...] = product_tn(left, right)
        for slot, col_tap in enumerate(COL_TAPS):
            to = ((row_tap % 2) * 4 + col_tap) * in_chan
            put(row_tap // 2, to, in_chan, lambda: total_one[:, slot * mid_chan:(slot + 1) * mid_chan])


def decoder_kernel(
    count, side_ref, latent_ref, w_one_ref, w_two_ref, w_three_ref, target_ref,
    decoded_ref, kept_a_ref, kept_b_ref, kept_c_ref, sent_a_ref, sent_b_ref, sent_c_ref,
    grad_one, act_one, slope_one, act_two, slope_two, grad_two, kgrad_three, tmp_one, tmp_two, tmp_three, grads, adj_two, adj_one, total_one, total_two,
):
    step = pl.program_id(0)
    steps = pl.num_programs(0)

    @pl.when(step == 0)
    def _():
        forward_part(count, latent_ref, w_one_ref, w_two_ref, act_one, slope_one, act_two, slope_two, tmp_one, tmp_two)

    last_part(
        count, step, steps, act_two, slope_two, w_three_ref, target_ref, decoded_ref, grad_two, kgrad_three, tmp_three, grads, adj_two
    )

    @pl.when(step == steps - 1)
    def _():
        backward_part(
            count, side_ref, latent_ref, act_one, slope_one, w_two_ref, grad_two, kgrad_three,
            grad_one, (kept_a_ref, kept_b_ref, kept_c_ref), (sent_a_ref, sent_b_ref, sent_c_ref), adj_one, total_one, total_two,
        )


def params(mebibytes, gridded=False):
    order = ("arbitrary",) if gridded else None
    return pltpu.CompilerParams(vmem_limit_bytes=mebibytes * 1024 * 1024, dimension_semantics=order)


def decoder(side, latent, w_one, w_two, w_three, target):
    count = latent.shape[1]
    mid_chan = w_two.shape[1] // 2
    out_chan = w_two.shape[2] // 4
    height, breadth = 2 * H0, 2 * W0
    steps, flat, lanes = target.shape[0] // 2, target.shape[1], target.shape[2]
    third_rows = w_three.shape[1]

    def whole(shape):
        return pl.BlockSpec(shape, lambda step: (0,) * len(shape))

    act_one = (height, breadth * count, mid_chan)
    act_two = (2 * height, flat, out_chan)
    padded = (2 * height + 2, flat, out_chan)
    in_chan = w_one.shape[0] // 16
    quarter, tail = (4 * in_chan, mid_chan), (4 * mid_chan + third_rows, mid_chan)
    single = pl.Buffered(1)
    return pl.pallas_call(
        functools.partial(decoder_kernel, count),
        name="decoder",
        grid=(steps,),
        in_specs=[
            pl.BlockSpec(memory_space=pltpu.SMEM),
            pl.BlockSpec(latent.shape, lambda step: (0, 0, 0), pipeline_mode=single),
            pl.BlockSpec(w_one.shape, lambda step: (0, 0), pipeline_mode=single),
            pl.BlockSpec(w_two.shape, lambda step: (0, 0, 0), pipeline_mode=single),
            pl.BlockSpec(w_three.shape, lambda step: (0, 0, 0), pipeline_mode=single),
            pl.BlockSpec((2, flat, lanes), lambda step: (step, 0, 0)),
        ],
        out_specs=(
            pl.BlockSpec((2, flat, lanes), lambda step: (step, 0, 0)),
            *map(whole, 2 * (quarter, quarter, tail)),
        ),
        out_shape=(
            jax.ShapeDtypeStruct(target.shape, jnp.bfloat16),
            *(jax.ShapeDtypeStruct(shape, jnp.bfloat16) for shape in 2 * (quarter, quarter, tail)),
        ),
        scratch_shapes=[
            pltpu.VMEM(act_one, jnp.bfloat16),
            pltpu.VMEM(act_one, jnp.bfloat16),
            pltpu.VMEM(act_one, jnp.float32),
            pltpu.VMEM(padded, jnp.bfloat16),
            pltpu.VMEM(act_two, jnp.float32),
            pltpu.VMEM(act_two, jnp.bfloat16),
            pltpu.VMEM(w_three.shape, jnp.float32),
            pltpu.VMEM((W0 * count, 4 * mid_chan), jnp.float32),
            pltpu.VMEM((breadth * count, 4 * out_chan), jnp.float32),
            pltpu.VMEM((flat, 2 * lanes), jnp.float32),
            pltpu.VMEM((flat + 2 * count, lanes), jnp.float32),
            pltpu.VMEM(padded, jnp.float32),
            pltpu.VMEM(act_one, jnp.float32),
            pltpu.VMEM((in_chan, 4 * mid_chan), jnp.float32),
            pltpu.VMEM(w_two.shape, jnp.float32),
        ],
        compiler_params=params(60, True),
    )(side, latent, w_one, w_two, w_three, target)


def spatial_first_kernel(grid_ref, after_ref, rows_ref, tmp):
    count, height, breadth, chan = grid_ref.shape
    for row in range(height):
        tmp[...] = grid_ref[:, row].astype(jnp.float32)
        even = tmp[:, pl.ds(0, breadth // 2, 2), :]
        odd = tmp[:, pl.ds(1, breadth // 2, 2), :]
        turned = jnp.swapaxes(jnp.concatenate([even, odd], axis=2), 0, 1)
        rows_ref[row] = turned.reshape(breadth // 2 * count, 2 * chan).astype(jnp.bfloat16)


def spatial_first(grid, after):
    count, height, breadth, chan = grid.shape
    per = 4
    flat = breadth // 2 * count
    return pl.pallas_call(
        spatial_first_kernel,
        name="spatial_first",
        grid=(height // per,),
        in_specs=[
            pl.BlockSpec((count, per, breadth, chan), lambda step: (0, step, 0, 0)),
            pl.BlockSpec(memory_space=pl.ANY),
        ],
        out_specs=pl.BlockSpec((per, flat, 2 * chan), lambda step: (step, 0, 0)),
        out_shape=jax.ShapeDtypeStruct((height, flat, 2 * chan), jnp.bfloat16),
        scratch_shapes=[pltpu.VMEM((count, breadth, chan), jnp.float32)],
        compiler_params=params(20, True),
        cost_estimate=pl.CostEstimate(flops=0, bytes_accessed=28000000, transcendentals=0),
    )(grid, after)


def sample_first_kernel(rows_ref, after_ref, out_ref, tmp):
    height = rows_ref.shape[0]
    count, _, breadth, chan = out_ref.shape
    for row in range(height):
        value = rows_ref[row].astype(jnp.float32).reshape(breadth // 2, count, 2 * chan)
        turned = jnp.swapaxes(value, 0, 1)
        tmp[:, pl.ds(0, breadth // 2, 2), :] = turned[:, :, :chan]
        tmp[:, pl.ds(1, breadth // 2, 2), :] = turned[:, :, chan:]
        out_ref[:, row] = tmp[...].astype(jnp.bfloat16)


def sample_first(rows, count, chan, after):
    height, flat, lanes = rows.shape
    breadth = 2 * flat // count
    per = 4
    return pl.pallas_call(
        sample_first_kernel,
        name="sample_first",
        grid=(height // per,),
        in_specs=[
            pl.BlockSpec((per, flat, lanes), lambda step: (step, 0, 0)),
            pl.BlockSpec(memory_space=pl.ANY),
        ],
        out_specs=pl.BlockSpec((count, per, breadth, chan), lambda step: (0, step, 0, 0)),
        out_shape=jax.ShapeDtypeStruct((count, height, breadth, chan), jnp.bfloat16),
        scratch_shapes=[pltpu.VMEM((count, breadth, chan), jnp.float32)],
        compiler_params=params(20, True),
        cost_estimate=pl.CostEstimate(flops=0, bytes_accessed=28000000, transcendentals=0),
    )(rows, after)


def bucket_kernel(half, subject_ref, count_ref, shift_ref, fmri_ref, after_ref, out_ref, place_ref):
    samples, voxels = fmri_ref.shape
    slots = out_ref.shape[0]
    subjects = count_ref.shape[0]
    room = slots // subjects
    owner = subject_ref[...]
    name = lax.broadcasted_iota(jnp.int32, (subjects, samples), 0)
    onehot = jnp.where(owner == name, 1.0, 0.0)
    row = lax.broadcasted_iota(jnp.int32, (samples, samples), 0)
    col = lax.broadcasted_iota(jnp.int32, (samples, samples), 1)
    before = jnp.where(row < col, 1.0, 0.0).astype(jnp.bfloat16)
    earlier = product(onehot.astype(jnp.bfloat16), before)
    rank = jnp.sum(earlier * onehot, axis=0, keepdims=True).astype(jnp.int32) - half * room
    position = jnp.where((rank >= 0) & (rank < room), owner * room + rank, -1)
    slot = lax.broadcasted_iota(jnp.int32, (slots, samples), 0)
    place_ref[...] = jnp.where(slot == position, 1.0, 0.0).astype(jnp.bfloat16)
    voxel = lax.broadcasted_iota(jnp.int32, (room, voxels), 1) + shift_ref[0]
    together = max(1, 64 // room)
    for start in range(0, subjects, together):
        rows = product(place_ref[pl.ds(start * room, together * room), :], fmri_ref[...])
        for inner in range(together):
            kept = jnp.where(voxel < count_ref[start + inner], rows[inner * room:(inner + 1) * room], 0.0)
            out_ref[pl.ds((start + inner) * room, room), :] = kept.astype(jnp.bfloat16)


def bucketed(half, subject, voxel_count, shift, fmri, after):
    samples, voxels = fmri.shape
    vmem = pl.BlockSpec(memory_space=pltpu.VMEM)
    smem = pl.BlockSpec(memory_space=pltpu.SMEM)
    return pl.pallas_call(
        functools.partial(bucket_kernel, half),
        name="bucket_rows",
        in_specs=[vmem, smem, smem, vmem, pl.BlockSpec(memory_space=pl.ANY)],
        out_specs=(vmem, vmem),
        out_shape=(
            jax.ShapeDtypeStruct((samples, voxels), jnp.bfloat16),
            jax.ShapeDtypeStruct((samples, samples), jnp.bfloat16),
        ),
        compiler_params=params(60),
    )(subject.reshape(1, samples), voxel_count, shift, fmri, after)


def project_kernel(quarter_ref, rows_ref, map_ref, *after_and_out):
    out_ref = after_and_out[-1]
    width = out_ref.shape[2]
    for block in range(out_ref.shape[0]):
        value = product(rows_ref[...], map_ref[0, :, block * width:(block + 1) * width])
        out_ref[block] = value.astype(jnp.bfloat16)


def projected(rows, maps, part, after, parts):
    count, voxels = rows.shape
    blocks = H0 * W0 // parts
    width = maps.shape[2] // (H0 * W0)
    step_blocks = max(1, blocks // 2)
    steps = blocks // step_blocks
    return pl.pallas_call(
        project_kernel,
        name="project_rows",
        grid_spec=pltpu.PrefetchScalarGridSpec(
            num_scalar_prefetch=1,
            grid=(steps,),
            in_specs=[
                pl.BlockSpec((count, voxels), lambda step, part: (0, 0)),
                pl.BlockSpec((1, voxels, step_blocks * width), lambda step, part: (0, 0, part[0] * steps + step)),
            ] + [pl.BlockSpec(memory_space=pl.ANY)] * len(after),
            out_specs=pl.BlockSpec((step_blocks, count, width), lambda step, part: (step, 0, 0)),
        ),
        out_shape=jax.ShapeDtypeStruct((blocks, count, width), jnp.bfloat16),
        compiler_params=params(60, True),
        cost_estimate=pl.CostEstimate(
            flops=2 * count * voxels * maps.shape[2] // parts,
            bytes_accessed=2 * voxels * maps.shape[2] // parts,
            transcendentals=0,
        ),
    )(part, rows, maps, *after)


def collect_kernel(place_a_ref, place_b_ref, first_ref, second_ref, *after_and_out):
    out_ref = after_and_out[-1]
    subjects, blocks, room, width = first_ref.shape
    for block in range(blocks):
        value = None
        for place_ref, ref in ((place_a_ref, first_ref), (place_b_ref, second_ref)):
            rows = jnp.concatenate([ref[subject, block] for subject in range(subjects)], axis=0)
            term = product_tn(place_ref[...], rows)
            value = term if value is None else value + term
        out_ref[:, pl.ds(block * width, width)] = value.astype(jnp.bfloat16)


def collected(places, first, second, after):
    samples = places[0].shape[1]
    vmem = pl.BlockSpec(memory_space=pltpu.VMEM)
    return pl.pallas_call(
        collect_kernel,
        name="collect_rows",
        in_specs=[vmem] * 4 + [pl.BlockSpec(memory_space=pl.ANY)] * len(after),
        out_specs=vmem,
        out_shape=jax.ShapeDtypeStruct((samples, first.shape[1] * first.shape[3]), jnp.bfloat16),
        compiler_params=params(16),
    )(*places, first, second, *after)


def finish_kernel(third_rows, side_ref, own_a, own_b, own_c, other_a, other_b, other_c, first_ref, second_ref, third_ref):
    side = side_ref[0]
    rows = own_a.shape[0]
    for at, (source, half) in enumerate(((own_a, side), (own_b, side), (other_a, 1 - side), (other_b, 1 - side))):
        start = pl.multiple_of((2 * half + at % 2) * rows, rows)
        first_ref[pl.ds(start, rows), :] = source[...]
    out_chan = second_ref.shape[1]
    mid_chan = second_ref.shape[0] // 16
    for parity in (0, 1):
        mine = side == parity
        for which in (0, 1):
            for pair in (0, 1):
                here = pl.ds((2 * which + pair) * mid_chan, mid_chan)
                value = jnp.where(mine, own_c[here, :].astype(jnp.float32), other_c[here, :].astype(jnp.float32))
                for inner in (0, 1):
                    col_tap = COL_TAPS[2 * pair + inner]
                    to = pl.ds((ROW_TAPS[parity][which] * 4 + col_tap) * mid_chan, mid_chan)
                    second_ref[to, :] = value[:, inner * out_chan:(inner + 1) * out_chan].astype(jnp.bfloat16)
        here = pl.ds(4 * mid_chan, third_rows)
        value = jnp.where(mine, own_c[here, :].astype(jnp.float32), other_c[here, :].astype(jnp.float32)).T
        chan = third_ref.shape[0]
        inputs = third_rows // 2
        for which in (0, 1):
            for slot, col_tap in enumerate(COL_TAPS):
                to = pl.ds((ROW_TAPS[parity][which] * 4 + col_tap) * inputs, inputs)
                piece = value[slot * chan:(slot + 1) * chan, which * inputs:(which + 1) * inputs]
                third_ref[:, to] = piece.astype(jnp.bfloat16)


def finished(side, own, other, third_rows):
    rows, lanes = own[0].shape
    mid_chan = (own[2].shape[0] - third_rows) // 4
    vmem = pl.BlockSpec(memory_space=pltpu.VMEM)
    return pl.pallas_call(
        functools.partial(finish_kernel, third_rows),
        name="finish_gradients",
        in_specs=[pl.BlockSpec(memory_space=pltpu.SMEM)] + [vmem] * 6,
        out_specs=(vmem, vmem, vmem),
        out_shape=(
            jax.ShapeDtypeStruct((4 * rows, lanes), jnp.bfloat16),
            jax.ShapeDtypeStruct((16 * mid_chan, lanes // 2), jnp.bfloat16),
            jax.ShapeDtypeStruct((lanes // 4, 8 * third_rows), jnp.bfloat16),
        ),
        compiler_params=params(24),
    )(side, *own, *other)


def rounded(values):
    return lax.optimization_barrier(values.astype(jnp.bfloat16))


def bit_pairs(axis):
    size = lax.axis_size(axis)
    bits = []
    bit = 1
    while bit < size:
        bits.append((axis, bit))
        bit *= 2
    return bits


def upper(hop):
    axis, bit = hop
    return (lax.axis_index(axis) // bit) % 2


def place_of(step):
    return sum(upper(hop) * 2 ** at for at, hop in enumerate(step))


def exchanged(values, step, change):
    axis = step[0][0]
    flip = sum(hop[1] for at, hop in enumerate(step) if change >> at & 1)
    return lax.ppermute(values, axis, [(at, at ^ flip) for at in range(lax.axis_size(axis))])


def summed(terms):
    value = terms[0]
    for term in terms[1:]:
        value = value.astype(jnp.float32) + term.astype(jnp.float32)
    return value


def shared(chains, step):
    ways = 2 ** len(step)
    place = place_of(step)

    def part(terms, which):
        size = terms[0].shape[0] // ways
        return summed([lax.dynamic_slice_in_dim(term, which * size, size, 0) for term in terms])

    arrived = []
    for change in range(1, ways):
        sent = [part(terms, place ^ change).astype(jnp.bfloat16) for terms in chains]
        joined = jnp.concatenate(sent, axis=0) if len(sent) > 1 else sent[0]
        arrived.append(exchanged(joined, step, change))
    result = []
    start = 0
    for terms in chains:
        size = terms[0].shape[0] // ways
        result.append([part(terms, place)] + [values[start:start + size] for values in arrived])
        start += size
    return result


def gathered(chains, step):
    ways = 2 ** len(step)
    joined = jnp.concatenate(chains, axis=0) if len(chains) > 1 else chains[0]
    pieces = [joined] + [exchanged(joined, step, change) for change in range(1, ways)]
    place = place_of(step)
    result = []
    start = 0
    for values in chains:
        size = values.shape[0]
        out = jnp.concatenate([values] * ways, axis=0)
        for change in range(1, ways):
            piece = pieces[change][start:start + size]
            out = lax.dynamic_update_slice_in_dim(out, piece, (place ^ change) * size, 0)
        result.append(out)
        start += size
    return result


def over_chains(move, chains, steps):
    result = [None] * len(chains)
    for step in {tuple(step): step for step in steps}.values():
        members = [at for at, own in enumerate(steps) if own == step]
        for at, moved_chain in zip(members, move([chains[at] for at in members], step)):
            result[at] = moved_chain
    return result


def shards(fmri, subject, ridge_maps, voxel_count, w_first, w_second, w_third, target):
    dp_count = lax.axis_size("dp")
    holders = lax.axis_size("vox")
    samp_dev = fmri.shape[0]
    vox_local = fmri.shape[1]
    mid_chan = w_first.shape[1]
    last_chan = w_second.shape[1]
    room = samp_dev // dp_count
    vox_bits = bit_pairs("vox")
    dp_bits = bit_pairs("dp")
    side = upper(vox_bits[0]).astype(jnp.int32).reshape(1)
    shift = (lax.axis_index("vox") * vox_local).astype(jnp.int32).reshape(1)
    first, place_first = bucketed(0, subject, voxel_count, shift, fmri, voxel_count)
    second, place_second = bucketed(1, subject, voxel_count, shift, fmri, place_first)

    def routed(rows):
        sent = rows.reshape(dp_count, room, rows.shape[1])
        return lax.all_to_all(sent, "dp", split_axis=0, concat_axis=0, tiled=True).reshape(rows.shape)

    core_bit, cross_bit = upper(vox_bits[0]), upper(vox_bits[1])

    def part_of(*bits):
        return sum(bit * 2 ** at for at, bit in enumerate(bits[::-1])).astype(jnp.int32).reshape(1)

    def to_cross(rows, *after):
        for_core = projected(rows, ridge_maps, part_of(1 - core_bit), after, 2)
        received = exchanged(for_core, vox_bits[:1], 1)
        own = projected(rows, ridge_maps, part_of(core_bit, 1 - cross_bit), (for_core,), 4)
        half = received.shape[0] // 2
        added = lax.dynamic_slice_in_dim(received, (1 - cross_bit) * half, half, 0)
        return summed([own, added]).astype(jnp.bfloat16), lax.dynamic_slice_in_dim(received, cross_bit * half, half, 0)

    def own_part(rows, *after):
        return projected(rows, ridge_maps, part_of(core_bit, cross_bit), after, 4)

    def rest_summed(*terms):
        terms = list(terms)
        for hop in vox_bits[2:]:
            terms, = shared([terms], [hop])
        return terms

    def returned(terms):
        latent_part = rounded(summed(terms))
        blocks, _, width = latent_part.shape
        sent = latent_part.reshape(blocks, dp_count, room, width).swapaxes(0, 1)
        return lax.all_to_all(sent, "dp", split_axis=0, concat_axis=0, tiled=True)

    first = routed(first)
    second = routed(second)
    across_first, added_first = to_cross(first, voxel_count)
    arrived_first = exchanged(across_first, vox_bits[1:2], 1)
    own_first = own_part(first, across_first)
    across_second, added_second = to_cross(second, arrived_first, own_first)
    arrived_second = exchanged(across_second, vox_bits[1:2], 1)
    own_second = own_part(second, across_second)
    terms_first = rest_summed(own_first, added_first, arrived_first)
    pair_two = paired_weight(w_second, mid_chan)
    pair_three = paired_weight(w_third, last_chan)
    target_rows = spatial_first(target, across_second)
    places = (place_first, place_second)
    back_first = returned(terms_first)
    back_first, arrived_second = lax.optimization_barrier((back_first, arrived_second))
    back_second = returned(rest_summed(own_second, added_second, arrived_second))
    own_rows = collected(places, back_first, back_second, (target_rows, pair_two, pair_three))
    own_rows = own_rows.reshape(holders, samp_dev // holders, own_rows.shape[1])
    latent = lax.all_to_all(own_rows, "vox", split_axis=0, concat_axis=0, tiled=True)
    count = latent.shape[1]
    decoded_rows, *shares = decoder(side, latent, w_first, pair_two, pair_three, target_rows)
    third_rows = pair_three.shape[1]
    received = [exchanged(values, vox_bits[:1], 1) for values in shares[3:]]
    across = [[hop] for hop in vox_bits[1:]]
    near = [dp_bits[:1]]
    along = [[hop] for hop in dp_bits[1:]]
    routes = (across + near + along, near + across + along, along[:1] + across + near + along[1:])
    parts = [list(pair) for pair in zip(shares[:3], received)]
    decoded = sample_first(decoded_rows, count, w_third.shape[1], received[1])
    for stage in range(len(routes[0])):
        parts = over_chains(shared, parts, [route[stage] for route in routes])
        *tied, decoded = lax.optimization_barrier(tuple(terms[1] for terms in parts) + (decoded,))
        parts = [terms[:1] + [arrived] + terms[2:] for terms, arrived in zip(parts, tied)]
    shares = [summed(terms).astype(jnp.bfloat16) for terms in parts]
    for stage in reversed(range(len(routes[0]))):
        shares = over_chains(gathered, shares, [route[stage] for route in routes])
        shares = list(lax.optimization_barrier(tuple(shares)))
    others = [exchanged(values, vox_bits[:1], 1) for values in shares]
    total_first, total_second, third = finished(side, shares, others, third_rows)
    total_third = third.T
    return (decoded, total_first, total_second, total_third)


def solution(mesh):
    placed = (
        P("dp", "vox"),
        P("dp", None),
        P("dp", "vox", None),
        P(),
        P(),
        P(),
        P(),
        P(("dp", "vox"), None, None, None),
    )
    return jax.shard_map(
        shards,
        mesh=mesh,
        in_specs=placed,
        out_specs=(P(("dp", "vox"), None, None, None), P(), P(), P()),
        check_vma=False,
    )
```

```python
import functools
import jax
import jax.numpy as jnp
from jax import lax
from jax.experimental import pallas as pl
from jax.sharding import PartitionSpec as P
from jax.experimental.pallas import tpu as pltpu

H0 = 2
W0 = 4
SAMP_DEV = 256
ROW_TAPS = ((1, 3), (2, 0))
ROW_SHIFT = (-1, 1)
COL_TAPS = (1, 2, 3, 0)


def paired_weight(weights, in_chan):
    out_chan = weights.shape[1]
    kernel = weights.reshape(4, 4, in_chan, out_chan)
    halves = []
    for parity in (0, 1):
        rows = []
        for row_tap in ROW_TAPS[parity]:
            rows.append(jnp.concatenate([kernel[row_tap, col_tap] for col_tap in COL_TAPS], axis=1))
        halves.append(jnp.concatenate(rows, axis=0))
    return jnp.stack(halves)


def product(left, right):
    return jnp.dot(left, right, preferred_element_type=jnp.float32)


def product_nt(left, right):
    return lax.dot_general(left, right, (((1,), (1,)), ((), ())), preferred_element_type=jnp.float32)


def product_tn(left, right):
    return lax.dot_general(left, right, (((0,), (0,)), ((), ())), preferred_element_type=jnp.float32)


def gelu_pair(value):
    root = 0.7978845608028654
    square = value * value
    tanh = jnp.tanh(root * (value + 0.044715 * (square * value)))
    half = 0.5 * (1.0 + tanh)
    slope = half + (0.5 * value) * (1.0 - tanh * tanh) * (root + (3 * 0.044715 * root) * square)
    return value * half, slope


def up_rows(product_ref, act_ref, slope_ref, act_row, slope_row, count, breadth, out_chan):
    width = 2 * out_chan
    for col in range(breadth):
        here = pl.ds(col * count, count)
        for col_par in (0, 1):
            lanes = pl.ds(col_par * out_chan, out_chan)
            side = pl.ds(width + col_par * out_chan, out_chan)
            value = product_ref[here, lanes]
            other = col - 1 if col_par == 0 else col + 1
            if 0 <= other < breadth:
                value = value + product_ref[pl.ds(other * count, count), side]
            act, slope = gelu_pair(value)
            rows = pl.ds((2 * col + col_par) * count, count)
            act_ref[act_row, rows, :] = act.astype(jnp.bfloat16)
            slope_ref[slope_row, rows, :] = slope


def holder_of(block, holders):
    bits = holders.bit_length() - 1
    depth = (H0 * W0).bit_length() - 1
    owner = sum(((block >> (depth - 1 - at)) & 1) << at for at in range(bits))
    return owner, block & (2 ** (depth - bits) - 1)


def latent_row(latent_ref, row):
    holders = latent_ref.shape[0]
    width = latent_ref.shape[2] * holders // (H0 * W0)
    pieces = []
    for col in range(W0):
        owner, place = holder_of(row * W0 + col, holders)
        pieces.append(latent_ref[owner, :, pl.ds(place * width, width)])
    return jnp.concatenate(pieces, axis=0)


def forward_part(count, latent_ref, w_one_ref, w_two_ref, act_one_ref, slope_one_ref, act_two_ref, slope_two_ref, tmp_one, tmp_two):
    in_chan = w_one_ref.shape[0] // 16
    mid_chan = w_two_ref.shape[1] // 2
    out_chan = w_two_ref.shape[2] // 4

    for row in range(H0):
        for parity in (0, 1):
            other = row + ROW_SHIFT[parity]
            for slot, col_tap in enumerate(COL_TAPS):
                lanes = pl.ds(slot * mid_chan, mid_chan)
                taps = pl.ds((ROW_TAPS[parity][0] * 4 + col_tap) * in_chan, in_chan)
                value = product(latent_row(latent_ref, row), w_one_ref[taps, :])
                if 0 <= other < H0:
                    taps = pl.ds((ROW_TAPS[parity][1] * 4 + col_tap) * in_chan, in_chan)
                    value = value + product(latent_row(latent_ref, other), w_one_ref[taps, :])
                tmp_one[:, lanes] = value
            at = 2 * row + parity
            up_rows(tmp_one, act_one_ref, slope_one_ref, at, at, count, W0, mid_chan)
    height = 2 * H0
    breadth = 2 * W0
    act_two_ref[0] = jnp.zeros_like(act_two_ref[0])
    act_two_ref[2 * height + 1] = jnp.zeros_like(act_two_ref[0])
    for row in range(height):
        for parity in (0, 1):
            tmp_two[...] = product(act_one_ref[row], w_two_ref[parity, :mid_chan, :])
            other = row + ROW_SHIFT[parity]
            if 0 <= other < height:
                tmp_two[...] += product(act_one_ref[other], w_two_ref[parity, mid_chan:, :])
            at = 2 * row + parity
            up_rows(tmp_two, act_two_ref, slope_two_ref, at + 1, at, count, breadth, out_chan)


def last_part(count, step, steps, act_ref, slope_ref, w_ref, target_ref, decoded_ref, grad_ref, kgrad_ref, tmp, grads, adj):
    breadth = act_ref.shape[1] // count
    in_chan = act_ref.shape[2]
    lanes = 2 * (w_ref.shape[2] // 4)

    @pl.when(step == 0)
    def _():
        adj[...] = jnp.zeros_like(adj)
        kgrad_ref[...] = jnp.zeros_like(kgrad_ref)
        grads[...] = jnp.zeros_like(grads)

    low = lax.broadcasted_iota(jnp.int32, (count, lanes), 1) < lanes // 2
    for parity in (0, 1):
        other = step + 1 + ROW_SHIFT[parity]
        left = jnp.concatenate([act_ref[step + 1], act_ref[other]], axis=1)
        tmp[...] = product(left, w_ref[parity])
        zero = jnp.zeros((count, lanes), jnp.float32)
        for col in range(breadth):
            here = pl.ds(col * count, count)
            before = tmp[pl.ds((col - 1) * count, count), lanes:] if col > 0 else zero
            after = tmp[pl.ds((col + 1) * count, count), lanes:] if col < breadth - 1 else zero
            value = tmp[here, :lanes] + jnp.where(low, before, after)
            decoded_ref[parity, here, :] = value.astype(jnp.bfloat16)
            grad = (value - target_ref[parity, here, :].astype(jnp.float32)) * (1.0 / SAMP_DEV)
            grads[pl.ds((col + 1) * count, count), :] = grad
        pieces = []
        for col in range(breadth):
            before = grads[pl.ds(col * count, count), :]
            here = grads[pl.ds((col + 1) * count, count), :]
            after = grads[pl.ds((col + 2) * count, count), :]
            side = jnp.where(low, after, before)
            pieces.append(jnp.concatenate([here.astype(jnp.bfloat16), side.astype(jnp.bfloat16)], axis=1))
        taps = jnp.concatenate(pieces, axis=0)
        kgrad_ref[parity] += product_tn(left, taps)
        back = product_nt(taps, w_ref[parity])
        adj[step + 1] += back[:, :in_chan]
        adj[other] += back[:, in_chan:]

    @pl.when(step == steps - 1)
    def _():
        def finish(row, carry):
            upstream = adj[row + 1].astype(jnp.bfloat16).astype(jnp.float32)
            grad_ref[row] = (upstream * slope_ref[row]).astype(jnp.bfloat16)
            return carry

        lax.fori_loop(0, steps, finish, 0)


def side_taps(grad_ref, row, count, breadth):
    def at(col):
        if 0 <= col < 2 * breadth:
            return grad_ref[row, pl.ds(col * count, count), :]
        return jnp.zeros((count, grad_ref.shape[2]), jnp.bfloat16)

    pieces = []
    for col in range(breadth):
        pieces.append(jnp.concatenate([at(2 * col), at(2 * col + 1), at(2 * col + 2), at(2 * col - 1)], axis=1))
    return jnp.concatenate(pieces, axis=0)


def backward_part(count, side_ref, latent_ref, act_ref, slope_ref, w_ref, grad_two_ref, third_ref, grad_one, kept_refs, sent_refs, adj, total_one, total_two):
    side = side_ref[0]

    def put(half, first, size, values):
        at = min(first // sent_refs[0].shape[0], 2)
        rows = pl.ds(first - at * sent_refs[0].shape[0], size)

        @pl.when(side == half)
        def _():
            kept_refs[at][rows, :] = values().astype(jnp.bfloat16)

        @pl.when(side != half)
        def _():
            sent_refs[at][rows, :] = values().astype(jnp.bfloat16)

    height = act_ref.shape[0]
    breadth = act_ref.shape[1] // count
    mid_chan = act_ref.shape[2]
    out_chan = grad_two_ref.shape[2]
    for row in range(height):
        for parity in (0, 1):
            taps = side_taps(grad_two_ref, 2 * row + parity, count, breadth)
            back = product_nt(taps, w_ref[parity])
            other = row + ROW_SHIFT[parity]
            if parity == 0 and row == 0:
                adj[0] = back[:, :mid_chan]
            else:
                adj[row] += back[:, :mid_chan]
            if 0 <= other < height:
                if parity == 0:
                    adj[other] += back[:, mid_chan:]
                else:
                    adj[other] = back[:, mid_chan:]
            mine = product_tn(act_ref[row], taps)
            if row == 0:
                total_two[parity, :mid_chan, :] = mine
            else:
                total_two[parity, :mid_chan, :] += mine
            if 0 <= other < height:
                far = product_tn(act_ref[other], taps)
                if row == (1 if parity == 0 else 0):
                    total_two[parity, mid_chan:, :] = far
                else:
                    total_two[parity, mid_chan:, :] += far
    for row in range(height):
        upstream = adj[row].astype(jnp.bfloat16).astype(jnp.float32)
        grad_one[row] = (upstream * slope_ref[row]).astype(jnp.bfloat16)
    in_chan = latent_ref.shape[0] * latent_ref.shape[2] // (H0 * W0)
    tail = 8 * in_chan
    lanes = 2 * out_chan
    for parity in (0, 1):
        for which in (0, 1):
            for pair in (0, 1):
                above, left_edge = which * mid_chan, pair * lanes
                put(
                    parity,
                    tail + (2 * which + pair) * mid_chan,
                    mid_chan,
                    lambda: total_two[parity, above:above + mid_chan, left_edge:left_edge + lanes],
                )
        put(parity, tail + 4 * mid_chan, third_ref.shape[1], lambda: third_ref[parity])
    for row_tap in range(4):
        parity = 0 if row_tap in ROW_TAPS[0] else 1
        shift = ROW_SHIFT[parity] if ROW_TAPS[parity][1] == row_tap else 0
        rows = [row for row in range(H0) if 0 <= row + shift < H0]
        lefts = [latent_row(latent_ref, row + shift) for row in rows]
        rights = [side_taps(grad_one, 2 * row + parity, count, W0) for row in rows]
        left = jnp.concatenate(lefts, axis=0) if len(lefts) > 1 else lefts[0]
        right = jnp.concatenate(rights, axis=0) if len(rights) > 1 else rights[0]
        total_one[...] = product_tn(left, right)
        for slot, col_tap in enumerate(COL_TAPS):
            to = ((row_tap % 2) * 4 + col_tap) * in_chan
            put(row_tap // 2, to, in_chan, lambda: total_one[:, slot * mid_chan:(slot + 1) * mid_chan])


def decoder_kernel(
    count, side_ref, latent_ref, w_one_ref, w_two_ref, w_three_ref, target_ref,
    decoded_ref, kept_a_ref, kept_b_ref, kept_c_ref, sent_a_ref, sent_b_ref, sent_c_ref,
    grad_one, act_one, slope_one, act_two, slope_two, grad_two, kgrad_three, tmp_one, tmp_two, tmp_three, grads, adj_two, adj_one, total_one, total_two,
):
    step = pl.program_id(0)
    steps = pl.num_programs(0)

    @pl.when(step == 0)
    def _():
        forward_part(count, latent_ref, w_one_ref, w_two_ref, act_one, slope_one, act_two, slope_two, tmp_one, tmp_two)

    last_part(
        count, step, steps, act_two, slope_two, w_three_ref, target_ref, decoded_ref, grad_two, kgrad_three, tmp_three, grads, adj_two
    )

    @pl.when(step == steps - 1)
    def _():
        backward_part(
            count, side_ref, latent_ref, act_one, slope_one, w_two_ref, grad_two, kgrad_three,
            grad_one, (kept_a_ref, kept_b_ref, kept_c_ref), (sent_a_ref, sent_b_ref, sent_c_ref), adj_one, total_one, total_two,
        )


def params(mebibytes, gridded=False):
    order = ("arbitrary",) if gridded else None
    return pltpu.CompilerParams(vmem_limit_bytes=mebibytes * 1024 * 1024, dimension_semantics=order)


def decoder(side, latent, w_one, w_two, w_three, target):
    count = latent.shape[1]
    mid_chan = w_two.shape[1] // 2
    out_chan = w_two.shape[2] // 4
    height, breadth = 2 * H0, 2 * W0
    steps, flat, lanes = target.shape[0] // 2, target.shape[1], target.shape[2]
    third_rows = w_three.shape[1]

    def whole(shape):
        return pl.BlockSpec(shape, lambda step: (0,) * len(shape))

    act_one = (height, breadth * count, mid_chan)
    act_two = (2 * height, flat, out_chan)
    padded = (2 * height + 2, flat, out_chan)
    in_chan = w_one.shape[0] // 16
    quarter, tail = (4 * in_chan, mid_chan), (4 * mid_chan + third_rows, mid_chan)
    single = pl.Buffered(1)
    return pl.pallas_call(
        functools.partial(decoder_kernel, count),
        name="decoder",
        grid=(steps,),
        in_specs=[
            pl.BlockSpec(memory_space=pltpu.SMEM),
            pl.BlockSpec(latent.shape, lambda step: (0, 0, 0), pipeline_mode=single),
            pl.BlockSpec(w_one.shape, lambda step: (0, 0), pipeline_mode=single),
            pl.BlockSpec(w_two.shape, lambda step: (0, 0, 0), pipeline_mode=single),
            pl.BlockSpec(w_three.shape, lambda step: (0, 0, 0), pipeline_mode=single),
            pl.BlockSpec((2, flat, lanes), lambda step: (step, 0, 0)),
        ],
        out_specs=(
            pl.BlockSpec((2, flat, lanes), lambda step: (step, 0, 0)),
            *map(whole, 2 * (quarter, quarter, tail)),
        ),
        out_shape=(
            jax.ShapeDtypeStruct(target.shape, jnp.bfloat16),
            *(jax.ShapeDtypeStruct(shape, jnp.bfloat16) for shape in 2 * (quarter, quarter, tail)),
        ),
        scratch_shapes=[
            pltpu.VMEM(act_one, jnp.bfloat16),
            pltpu.VMEM(act_one, jnp.bfloat16),
            pltpu.VMEM(act_one, jnp.float32),
            pltpu.VMEM(padded, jnp.bfloat16),
            pltpu.VMEM(act_two, jnp.float32),
            pltpu.VMEM(act_two, jnp.bfloat16),
            pltpu.VMEM(w_three.shape, jnp.float32),
            pltpu.VMEM((W0 * count, 4 * mid_chan), jnp.float32),
            pltpu.VMEM((breadth * count, 4 * out_chan), jnp.float32),
            pltpu.VMEM((flat, 2 * lanes), jnp.float32),
            pltpu.VMEM((flat + 2 * count, lanes), jnp.float32),
            pltpu.VMEM(padded, jnp.float32),
            pltpu.VMEM(act_one, jnp.float32),
            pltpu.VMEM((in_chan, 4 * mid_chan), jnp.float32),
            pltpu.VMEM(w_two.shape, jnp.float32),
        ],
        compiler_params=params(60, True),
    )(side, latent, w_one, w_two, w_three, target)


def spatial_first_kernel(grid_ref, after_ref, rows_ref, tmp):
    count, height, breadth, chan = grid_ref.shape
    for row in range(height):
        tmp[...] = grid_ref[:, row].astype(jnp.float32)
        even = tmp[:, pl.ds(0, breadth // 2, 2), :]
        odd = tmp[:, pl.ds(1, breadth // 2, 2), :]
        turned = jnp.swapaxes(jnp.concatenate([even, odd], axis=2), 0, 1)
        rows_ref[row] = turned.reshape(breadth // 2 * count, 2 * chan).astype(jnp.bfloat16)


def spatial_first(grid, after):
    count, height, breadth, chan = grid.shape
    per = 4
    flat = breadth // 2 * count
    return pl.pallas_call(
        spatial_first_kernel,
        name="spatial_first",
        grid=(height // per,),
        in_specs=[
            pl.BlockSpec((count, per, breadth, chan), lambda step: (0, step, 0, 0)),
            pl.BlockSpec(memory_space=pl.ANY),
        ],
        out_specs=pl.BlockSpec((per, flat, 2 * chan), lambda step: (step, 0, 0)),
        out_shape=jax.ShapeDtypeStruct((height, flat, 2 * chan), jnp.bfloat16),
        scratch_shapes=[pltpu.VMEM((count, breadth, chan), jnp.float32)],
        compiler_params=params(20, True),
        cost_estimate=pl.CostEstimate(flops=0, bytes_accessed=28000000, transcendentals=0),
    )(grid, after)


def sample_first_kernel(rows_ref, after_ref, out_ref, tmp):
    height = rows_ref.shape[0]
    count, _, breadth, chan = out_ref.shape
    for row in range(height):
        value = rows_ref[row].astype(jnp.float32).reshape(breadth // 2, count, 2 * chan)
        turned = jnp.swapaxes(value, 0, 1)
        tmp[:, pl.ds(0, breadth // 2, 2), :] = turned[:, :, :chan]
        tmp[:, pl.ds(1, breadth // 2, 2), :] = turned[:, :, chan:]
        out_ref[:, row] = tmp[...].astype(jnp.bfloat16)


def sample_first(rows, count, chan, after):
    height, flat, lanes = rows.shape
    breadth = 2 * flat // count
    per = 4
    return pl.pallas_call(
        sample_first_kernel,
        name="sample_first",
        grid=(height // per,),
        in_specs=[
            pl.BlockSpec((per, flat, lanes), lambda step: (step, 0, 0)),
            pl.BlockSpec(memory_space=pl.ANY),
        ],
        out_specs=pl.BlockSpec((count, per, breadth, chan), lambda step: (0, step, 0, 0)),
        out_shape=jax.ShapeDtypeStruct((count, height, breadth, chan), jnp.bfloat16),
        scratch_shapes=[pltpu.VMEM((count, breadth, chan), jnp.float32)],
        compiler_params=params(20, True),
        cost_estimate=pl.CostEstimate(flops=0, bytes_accessed=28000000, transcendentals=0),
    )(rows, after)


def bucket_kernel(half, subject_ref, count_ref, shift_ref, fmri_ref, after_ref, out_ref, place_ref):
    samples, voxels = fmri_ref.shape
    slots = out_ref.shape[0]
    subjects = count_ref.shape[0]
    room = slots // subjects
    owner = subject_ref[...]
    name = lax.broadcasted_iota(jnp.int32, (subjects, samples), 0)
    onehot = jnp.where(owner == name, 1.0, 0.0)
    row = lax.broadcasted_iota(jnp.int32, (samples, samples), 0)
    col = lax.broadcasted_iota(jnp.int32, (samples, samples), 1)
    before = jnp.where(row < col, 1.0, 0.0).astype(jnp.bfloat16)
    earlier = product(onehot.astype(jnp.bfloat16), before)
    rank = jnp.sum(earlier * onehot, axis=0, keepdims=True).astype(jnp.int32) - half * room
    position = jnp.where((rank >= 0) & (rank < room), owner * room + rank, -1)
    slot = lax.broadcasted_iota(jnp.int32, (slots, samples), 0)
    place_ref[...] = jnp.where(slot == position, 1.0, 0.0).astype(jnp.bfloat16)
    voxel = lax.broadcasted_iota(jnp.int32, (room, voxels), 1) + shift_ref[0]
    together = max(1, 64 // room)
    for start in range(0, subjects, together):
        rows = product(place_ref[pl.ds(start * room, together * room), :], fmri_ref[...])
        for inner in range(together):
            kept = jnp.where(voxel < count_ref[start + inner], rows[inner * room:(inner + 1) * room], 0.0)
            out_ref[pl.ds((start + inner) * room, room), :] = kept.astype(jnp.bfloat16)


def bucketed(half, subject, voxel_count, shift, fmri, after):
    samples, voxels = fmri.shape
    vmem = pl.BlockSpec(memory_space=pltpu.VMEM)
    smem = pl.BlockSpec(memory_space=pltpu.SMEM)
    return pl.pallas_call(
        functools.partial(bucket_kernel, half),
        name="bucket_rows",
        in_specs=[vmem, smem, smem, vmem, pl.BlockSpec(memory_space=pl.ANY)],
        out_specs=(vmem, vmem),
        out_shape=(
            jax.ShapeDtypeStruct((samples, voxels), jnp.bfloat16),
            jax.ShapeDtypeStruct((samples, samples), jnp.bfloat16),
        ),
        compiler_params=params(60),
    )(subject.reshape(1, samples), voxel_count, shift, fmri, after)


def project_kernel(quarter_ref, rows_ref, map_ref, *after_and_out):
    out_ref = after_and_out[-1]
    width = out_ref.shape[2]
    for block in range(out_ref.shape[0]):
        value = product(rows_ref[...], map_ref[0, :, block * width:(block + 1) * width])
        out_ref[block] = value.astype(jnp.bfloat16)


def projected(rows, maps, part, after, parts):
    count, voxels = rows.shape
    blocks = H0 * W0 // parts
    width = maps.shape[2] // (H0 * W0)
    step_blocks = max(1, blocks // 2)
    steps = blocks // step_blocks
    return pl.pallas_call(
        project_kernel,
        name="project_rows",
        grid_spec=pltpu.PrefetchScalarGridSpec(
            num_scalar_prefetch=1,
            grid=(steps,),
            in_specs=[
                pl.BlockSpec((count, voxels), lambda step, part: (0, 0)),
                pl.BlockSpec((1, voxels, step_blocks * width), lambda step, part: (0, 0, part[0] * steps + step)),
            ] + [pl.BlockSpec(memory_space=pl.ANY)] * len(after),
            out_specs=pl.BlockSpec((step_blocks, count, width), lambda step, part: (step, 0, 0)),
        ),
        out_shape=jax.ShapeDtypeStruct((blocks, count, width), jnp.bfloat16),
        compiler_params=params(60, True),
        cost_estimate=pl.CostEstimate(
            flops=2 * count * voxels * maps.shape[2] // parts,
            bytes_accessed=2 * voxels * maps.shape[2] // parts,
            transcendentals=0,
        ),
    )(part, rows, maps, *after)


def collect_kernel(place_a_ref, place_b_ref, first_ref, second_ref, *after_and_out):
    out_ref = after_and_out[-1]
    subjects, blocks, room, width = first_ref.shape
    for block in range(blocks):
        value = None
        for place_ref, ref in ((place_a_ref, first_ref), (place_b_ref, second_ref)):
            rows = jnp.concatenate([ref[subject, block] for subject in range(subjects)], axis=0)
            term = product_tn(place_ref[...], rows)
            value = term if value is None else value + term
        out_ref[:, pl.ds(block * width, width)] = value.astype(jnp.bfloat16)


def collected(places, first, second, after):
    samples = places[0].shape[1]
    vmem = pl.BlockSpec(memory_space=pltpu.VMEM)
    return pl.pallas_call(
        collect_kernel,
        name="collect_rows",
        in_specs=[vmem] * 4 + [pl.BlockSpec(memory_space=pl.ANY)] * len(after),
        out_specs=vmem,
        out_shape=jax.ShapeDtypeStruct((samples, first.shape[1] * first.shape[3]), jnp.bfloat16),
        compiler_params=params(16),
    )(*places, first, second, *after)


def finish_kernel(third_rows, side_ref, own_a, own_b, own_c, other_a, other_b, other_c, first_ref, second_ref, third_ref):
    side = side_ref[0]
    rows = own_a.shape[0]
    for at, (source, half) in enumerate(((own_a, side), (own_b, side), (other_a, 1 - side), (other_b, 1 - side))):
        start = pl.multiple_of((2 * half + at % 2) * rows, rows)
        first_ref[pl.ds(start, rows), :] = source[...]
    out_chan = second_ref.shape[1]
    mid_chan = second_ref.shape[0] // 16
    for parity in (0, 1):
        mine = side == parity
        for which in (0, 1):
            for pair in (0, 1):
                here = pl.ds((2 * which + pair) * mid_chan, mid_chan)
                value = jnp.where(mine, own_c[here, :].astype(jnp.float32), other_c[here, :].astype(jnp.float32))
                for inner in (0, 1):
                    col_tap = COL_TAPS[2 * pair + inner]
                    to = pl.ds((ROW_TAPS[parity][which] * 4 + col_tap) * mid_chan, mid_chan)
                    second_ref[to, :] = value[:, inner * out_chan:(inner + 1) * out_chan].astype(jnp.bfloat16)
        here = pl.ds(4 * mid_chan, third_rows)
        value = jnp.where(mine, own_c[here, :].astype(jnp.float32), other_c[here, :].astype(jnp.float32)).T
        chan = third_ref.shape[0]
        inputs = third_rows // 2
        for which in (0, 1):
            for slot, col_tap in enumerate(COL_TAPS):
                to = pl.ds((ROW_TAPS[parity][which] * 4 + col_tap) * inputs, inputs)
                piece = value[slot * chan:(slot + 1) * chan, which * inputs:(which + 1) * inputs]
                third_ref[:, to] = piece.astype(jnp.bfloat16)


def finished(side, own, other, third_rows):
    rows, lanes = own[0].shape
    mid_chan = (own[2].shape[0] - third_rows) // 4
    vmem = pl.BlockSpec(memory_space=pltpu.VMEM)
    return pl.pallas_call(
        functools.partial(finish_kernel, third_rows),
        name="finish_gradients",
        in_specs=[pl.BlockSpec(memory_space=pltpu.SMEM)] + [vmem] * 6,
        out_specs=(vmem, vmem, vmem),
        out_shape=(
            jax.ShapeDtypeStruct((4 * rows, lanes), jnp.bfloat16),
            jax.ShapeDtypeStruct((16 * mid_chan, lanes // 2), jnp.bfloat16),
            jax.ShapeDtypeStruct((lanes // 4, 8 * third_rows), jnp.bfloat16),
        ),
        compiler_params=params(24),
    )(side, *own, *other)


def rounded(values):
    return lax.optimization_barrier(values.astype(jnp.bfloat16))


def bit_pairs(axis):
    size = lax.axis_size(axis)
    bits = []
    bit = 1
    while bit < size:
        bits.append((axis, bit))
        bit *= 2
    return bits


def upper(hop):
    axis, bit = hop
    return (lax.axis_index(axis) // bit) % 2


def place_of(step):
    return sum(upper(hop) * 2 ** at for at, hop in enumerate(step))


def exchanged(values, step, change):
    axis = step[0][0]
    flip = sum(hop[1] for at, hop in enumerate(step) if change >> at & 1)
    return lax.ppermute(values, axis, [(at, at ^ flip) for at in range(lax.axis_size(axis))])


def summed(terms):
    value = terms[0]
    for term in terms[1:]:
        value = value.astype(jnp.float32) + term.astype(jnp.float32)
    return value


def shared(chains, step):
    ways = 2 ** len(step)
    place = place_of(step)

    def part(terms, which):
        size = terms[0].shape[0] // ways
        return summed([lax.dynamic_slice_in_dim(term, which * size, size, 0) for term in terms])

    arrived = []
    for change in range(1, ways):
        sent = [part(terms, place ^ change).astype(jnp.bfloat16) for terms in chains]
        joined = jnp.concatenate(sent, axis=0) if len(sent) > 1 else sent[0]
        arrived.append(exchanged(joined, step, change))
    result = []
    start = 0
    for terms in chains:
        size = terms[0].shape[0] // ways
        result.append([part(terms, place)] + [values[start:start + size] for values in arrived])
        start += size
    return result


def gathered(chains, step):
    ways = 2 ** len(step)
    joined = jnp.concatenate(chains, axis=0) if len(chains) > 1 else chains[0]
    pieces = [joined] + [exchanged(joined, step, change) for change in range(1, ways)]
    place = place_of(step)
    result = []
    start = 0
    for values in chains:
        size = values.shape[0]
        out = jnp.concatenate([values] * ways, axis=0)
        for change in range(1, ways):
            piece = pieces[change][start:start + size]
            out = lax.dynamic_update_slice_in_dim(out, piece, (place ^ change) * size, 0)
        result.append(out)
        start += size
    return result


def over_chains(move, chains, steps):
    result = [None] * len(chains)
    for step in {tuple(step): step for step in steps}.values():
        members = [at for at, own in enumerate(steps) if own == step]
        for at, moved_chain in zip(members, move([chains[at] for at in members], step)):
            result[at] = moved_chain
    return result


def shards(fmri, subject, ridge_maps, voxel_count, w_first, w_second, w_third, target):
    dp_count = lax.axis_size("dp")
    holders = lax.axis_size("vox")
    samp_dev = fmri.shape[0]
    vox_local = fmri.shape[1]
    mid_chan = w_first.shape[1]
    last_chan = w_second.shape[1]
    room = samp_dev // dp_count
    vox_bits = bit_pairs("vox")
    dp_bits = bit_pairs("dp")
    side = upper(vox_bits[0]).astype(jnp.int32).reshape(1)
    shift = (lax.axis_index("vox") * vox_local).astype(jnp.int32).reshape(1)
    first, place_first = bucketed(0, subject, voxel_count, shift, fmri, voxel_count)
    second, place_second = bucketed(1, subject, voxel_count, shift, fmri, place_first)

    def routed(rows):
        sent = rows.reshape(dp_count, room, rows.shape[1])
        return lax.all_to_all(sent, "dp", split_axis=0, concat_axis=0, tiled=True).reshape(rows.shape)

    core_bit, cross_bit = upper(vox_bits[0]), upper(vox_bits[1])

    def part_of(*bits):
        return sum(bit * 2 ** at for at, bit in enumerate(bits[::-1])).astype(jnp.int32).reshape(1)

    def to_cross(rows, *after):
        for_core = projected(rows, ridge_maps, part_of(1 - core_bit), after, 2)
        received = exchanged(for_core, vox_bits[:1], 1)
        own = projected(rows, ridge_maps, part_of(core_bit, 1 - cross_bit), (for_core,), 4)
        half = received.shape[0] // 2
        added = lax.dynamic_slice_in_dim(received, (1 - cross_bit) * half, half, 0)
        return summed([own, added]).astype(jnp.bfloat16), lax.dynamic_slice_in_dim(received, cross_bit * half, half, 0)

    def own_part(rows, *after):
        return projected(rows, ridge_maps, part_of(core_bit, cross_bit), after, 4)

    def rest_summed(*terms):
        terms = list(terms)
        for hop in vox_bits[2:]:
            terms, = shared([terms], [hop])
        return terms

    def returned(terms):
        latent_part = rounded(summed(terms))
        blocks, _, width = latent_part.shape
        sent = latent_part.reshape(blocks, dp_count, room, width).swapaxes(0, 1)
        return lax.all_to_all(sent, "dp", split_axis=0, concat_axis=0, tiled=True)

    first = routed(first)
    second = routed(second)
    across_first, added_first = to_cross(first, voxel_count)
    arrived_first = exchanged(across_first, vox_bits[1:2], 1)
    own_first = own_part(first, across_first)
    across_second, added_second = to_cross(second, arrived_first, own_first)
    arrived_second = exchanged(across_second, vox_bits[1:2], 1)
    own_second = own_part(second, across_second)
    terms_first = rest_summed(own_first, added_first, arrived_first)
    pair_two = paired_weight(w_second, mid_chan)
    pair_three = paired_weight(w_third, last_chan)
    target_rows = spatial_first(target, across_second)
    places = (place_first, place_second)
    back_first = returned(terms_first)
    back_first, arrived_second = lax.optimization_barrier((back_first, arrived_second))
    back_second = returned(rest_summed(own_second, added_second, arrived_second))
    own_rows = collected(places, back_first, back_second, (target_rows, pair_two, pair_three))
    own_rows = own_rows.reshape(holders, samp_dev // holders, own_rows.shape[1])
    latent = lax.all_to_all(own_rows, "vox", split_axis=0, concat_axis=0, tiled=True)
    count = latent.shape[1]
    decoded_rows, *shares = decoder(side, latent, w_first, pair_two, pair_three, target_rows)
    third_rows = pair_three.shape[1]
    received = [exchanged(values, vox_bits[:1], 1) for values in shares[3:]]
    across = [[hop] for hop in vox_bits[1:]]
    near = [dp_bits[:1]]
    along = [[hop] for hop in dp_bits[1:]]
    routes = (across + near + along, near + across + along, along[:1] + across + near + along[1:])
    parts = [list(pair) for pair in zip(shares[:3], received)]
    decoded = sample_first(decoded_rows, count, w_third.shape[1], received[1])
    for stage in range(len(routes[0])):
        parts = over_chains(shared, parts, [route[stage] for route in routes])
        *tied, decoded = lax.optimization_barrier(tuple(terms[1] for terms in parts) + (decoded,))
        parts = [terms[:1] + [arrived] + terms[2:] for terms, arrived in zip(parts, tied)]
    shares = [summed(terms).astype(jnp.bfloat16) for terms in parts]
    for stage in reversed(range(len(routes[0]))):
        shares = over_chains(gathered, shares, [route[stage] for route in routes])
        if stage > 1:
            shares = list(lax.optimization_barrier(tuple(shares)))
    others = [exchanged(values, vox_bits[:1], 1) for values in shares]
    total_first, total_second, third = finished(side, shares, others, third_rows)
    total_third = third.T
    return (decoded, total_first, total_second, total_third)


def solution(mesh):
    placed = (
        P("dp", "vox"),
        P("dp", None),
        P("dp", "vox", None),
        P(),
        P(),
        P(),
        P(),
        P(("dp", "vox"), None, None, None),
    )
    return jax.shard_map(
        shards,
        mesh=mesh,
        in_specs=placed,
        out_specs=(P(("dp", "vox"), None, None, None), P(), P(), P()),
        check_vma=False,
    )
```

```python
import functools
import jax
import jax.numpy as jnp
from jax import lax
from jax.experimental import pallas as pl
from jax.sharding import PartitionSpec as P
from jax.experimental.pallas import tpu as pltpu

H0 = 2
W0 = 4
SAMP_DEV = 256
ROW_TAPS = ((1, 3), (2, 0))
ROW_SHIFT = (-1, 1)
COL_TAPS = (1, 2, 3, 0)


def paired_weight(weights, in_chan):
    out_chan = weights.shape[1]
    kernel = weights.reshape(4, 4, in_chan, out_chan)
    halves = []
    for parity in (0, 1):
        rows = []
        for row_tap in ROW_TAPS[parity]:
            rows.append(jnp.concatenate([kernel[row_tap, col_tap] for col_tap in COL_TAPS], axis=1))
        halves.append(jnp.concatenate(rows, axis=0))
    return jnp.stack(halves)


def product(left, right):
    return jnp.dot(left, right, preferred_element_type=jnp.float32)


def product_nt(left, right):
    return lax.dot_general(left, right, (((1,), (1,)), ((), ())), preferred_element_type=jnp.float32)


def product_tn(left, right):
    return lax.dot_general(left, right, (((0,), (0,)), ((), ())), preferred_element_type=jnp.float32)


def gelu_pair(value):
    root = 0.7978845608028654
    square = value * value
    tanh = jnp.tanh(root * (value + 0.044715 * (square * value)))
    half = 0.5 * (1.0 + tanh)
    slope = half + (0.5 * value) * (1.0 - tanh * tanh) * (root + (3 * 0.044715 * root) * square)
    return value * half, slope


def up_rows(product_ref, act_ref, slope_ref, act_row, slope_row, count, breadth, out_chan):
    width = 2 * out_chan
    for col in range(breadth):
        here = pl.ds(col * count, count)
        for col_par in (0, 1):
            lanes = pl.ds(col_par * out_chan, out_chan)
            side = pl.ds(width + col_par * out_chan, out_chan)
            value = product_ref[here, lanes]
            other = col - 1 if col_par == 0 else col + 1
            if 0 <= other < breadth:
                value = value + product_ref[pl.ds(other * count, count), side]
            act, slope = gelu_pair(value)
            rows = pl.ds((2 * col + col_par) * count, count)
            act_ref[act_row, rows, :] = act.astype(jnp.bfloat16)
            slope_ref[slope_row, rows, :] = slope


def holder_of(block, holders):
    bits = holders.bit_length() - 1
    depth = (H0 * W0).bit_length() - 1
    owner = sum(((block >> (depth - 1 - at)) & 1) << at for at in range(bits))
    return owner, block & (2 ** (depth - bits) - 1)


def latent_row(latent_ref, row):
    holders = latent_ref.shape[0]
    width = latent_ref.shape[2] * holders // (H0 * W0)
    pieces = []
    for col in range(W0):
        owner, place = holder_of(row * W0 + col, holders)
        pieces.append(latent_ref[owner, :, pl.ds(place * width, width)])
    return jnp.concatenate(pieces, axis=0)


def forward_part(count, latent_ref, w_one_ref, w_two_ref, act_one_ref, slope_one_ref, act_two_ref, slope_two_ref, tmp_one, tmp_two):
    in_chan = w_one_ref.shape[0] // 16
    mid_chan = w_two_ref.shape[1] // 2
    out_chan = w_two_ref.shape[2] // 4

    for row in range(H0):
        for parity in (0, 1):
            other = row + ROW_SHIFT[parity]
            for slot, col_tap in enumerate(COL_TAPS):
                lanes = pl.ds(slot * mid_chan, mid_chan)
                taps = pl.ds((ROW_TAPS[parity][0] * 4 + col_tap) * in_chan, in_chan)
                value = product(latent_row(latent_ref, row), w_one_ref[taps, :])
                if 0 <= other < H0:
                    taps = pl.ds((ROW_TAPS[parity][1] * 4 + col_tap) * in_chan, in_chan)
                    value = value + product(latent_row(latent_ref, other), w_one_ref[taps, :])
                tmp_one[:, lanes] = value
            at = 2 * row + parity
            up_rows(tmp_one, act_one_ref, slope_one_ref, at, at, count, W0, mid_chan)
    height = 2 * H0
    breadth = 2 * W0
    act_two_ref[0] = jnp.zeros_like(act_two_ref[0])
    act_two_ref[2 * height + 1] = jnp.zeros_like(act_two_ref[0])
    for row in range(height):
        for parity in (0, 1):
            tmp_two[...] = product(act_one_ref[row], w_two_ref[parity, :mid_chan, :])
            other = row + ROW_SHIFT[parity]
            if 0 <= other < height:
                tmp_two[...] += product(act_one_ref[other], w_two_ref[parity, mid_chan:, :])
            at = 2 * row + parity
            up_rows(tmp_two, act_two_ref, slope_two_ref, at + 1, at, count, breadth, out_chan)


def last_part(count, step, steps, act_ref, slope_ref, w_ref, target_ref, decoded_ref, grad_ref, kgrad_ref, tmp, grads, adj):
    breadth = act_ref.shape[1] // count
    in_chan = act_ref.shape[2]
    lanes = 2 * (w_ref.shape[2] // 4)

    @pl.when(step == 0)
    def _():
        adj[...] = jnp.zeros_like(adj)
        kgrad_ref[...] = jnp.zeros_like(kgrad_ref)
        grads[...] = jnp.zeros_like(grads)

    low = lax.broadcasted_iota(jnp.int32, (count, lanes), 1) < lanes // 2
    for parity in (0, 1):
        other = step + 1 + ROW_SHIFT[parity]
        left = jnp.concatenate([act_ref[step + 1], act_ref[other]], axis=1)
        tmp[...] = product(left, w_ref[parity])
        zero = jnp.zeros((count, lanes), jnp.float32)
        for col in range(breadth):
            here = pl.ds(col * count, count)
            before = tmp[pl.ds((col - 1) * count, count), lanes:] if col > 0 else zero
            after = tmp[pl.ds((col + 1) * count, count), lanes:] if col < breadth - 1 else zero
            value = tmp[here, :lanes] + jnp.where(low, before, after)
            decoded_ref[parity, here, :] = value.astype(jnp.bfloat16)
            grad = (value - target_ref[parity, here, :].astype(jnp.float32)) * (1.0 / SAMP_DEV)
            grads[pl.ds((col + 1) * count, count), :] = grad
        pieces = []
        for col in range(breadth):
            before = grads[pl.ds(col * count, count), :]
            here = grads[pl.ds((col + 1) * count, count), :]
            after = grads[pl.ds((col + 2) * count, count), :]
            side = jnp.where(low, after, before)
            pieces.append(jnp.concatenate([here.astype(jnp.bfloat16), side.astype(jnp.bfloat16)], axis=1))
        taps = jnp.concatenate(pieces, axis=0)
        kgrad_ref[parity] += product_tn(left, taps)
        back = product_nt(taps, w_ref[parity])
        adj[step + 1] += back[:, :in_chan]
        adj[other] += back[:, in_chan:]

    @pl.when(step == steps - 1)
    def _():
        def finish(row, carry):
            upstream = adj[row + 1].astype(jnp.bfloat16).astype(jnp.float32)
            grad_ref[row] = (upstream * slope_ref[row]).astype(jnp.bfloat16)
            return carry

        lax.fori_loop(0, steps, finish, 0)


def side_taps(grad_ref, row, count, breadth):
    def at(col):
        if 0 <= col < 2 * breadth:
            return grad_ref[row, pl.ds(col * count, count), :]
        return jnp.zeros((count, grad_ref.shape[2]), jnp.bfloat16)

    pieces = []
    for col in range(breadth):
        pieces.append(jnp.concatenate([at(2 * col), at(2 * col + 1), at(2 * col + 2), at(2 * col - 1)], axis=1))
    return jnp.concatenate(pieces, axis=0)


def backward_part(count, side_ref, latent_ref, act_ref, slope_ref, w_ref, grad_two_ref, third_ref, grad_one, kept_refs, sent_refs, adj, total_one, total_two):
    side = side_ref[0]

    def put(half, first, size, values):
        at = min(first // sent_refs[0].shape[0], 2)
        rows = pl.ds(first - at * sent_refs[0].shape[0], size)

        @pl.when(side == half)
        def _():
            kept_refs[at][rows, :] = values().astype(jnp.bfloat16)

        @pl.when(side != half)
        def _():
            sent_refs[at][rows, :] = values().astype(jnp.bfloat16)

    height = act_ref.shape[0]
    breadth = act_ref.shape[1] // count
    mid_chan = act_ref.shape[2]
    out_chan = grad_two_ref.shape[2]
    for row in range(height):
        for parity in (0, 1):
            taps = side_taps(grad_two_ref, 2 * row + parity, count, breadth)
            back = product_nt(taps, w_ref[parity])
            other = row + ROW_SHIFT[parity]
            if parity == 0 and row == 0:
                adj[0] = back[:, :mid_chan]
            else:
                adj[row] += back[:, :mid_chan]
            if 0 <= other < height:
                if parity == 0:
                    adj[other] += back[:, mid_chan:]
                else:
                    adj[other] = back[:, mid_chan:]
            mine = product_tn(act_ref[row], taps)
            if row == 0:
                total_two[parity, :mid_chan, :] = mine
            else:
                total_two[parity, :mid_chan, :] += mine
            if 0 <= other < height:
                far = product_tn(act_ref[other], taps)
                if row == (1 if parity == 0 else 0):
                    total_two[parity, mid_chan:, :] = far
                else:
                    total_two[parity, mid_chan:, :] += far
    for row in range(height):
        upstream = adj[row].astype(jnp.bfloat16).astype(jnp.float32)
        grad_one[row] = (upstream * slope_ref[row]).astype(jnp.bfloat16)
    in_chan = latent_ref.shape[0] * latent_ref.shape[2] // (H0 * W0)
    tail = 8 * in_chan
    lanes = 2 * out_chan
    for parity in (0, 1):
        for which in (0, 1):
            for pair in (0, 1):
                above, left_edge = which * mid_chan, pair * lanes
                put(
                    parity,
                    tail + (2 * which + pair) * mid_chan,
                    mid_chan,
                    lambda: total_two[parity, above:above + mid_chan, left_edge:left_edge + lanes],
                )
        put(parity, tail + 4 * mid_chan, third_ref.shape[1], lambda: third_ref[parity])
    for row_tap in range(4):
        parity = 0 if row_tap in ROW_TAPS[0] else 1
        shift = ROW_SHIFT[parity] if ROW_TAPS[parity][1] == row_tap else 0
        rows = [row for row in range(H0) if 0 <= row + shift < H0]
        lefts = [latent_row(latent_ref, row + shift) for row in rows]
        rights = [side_taps(grad_one, 2 * row + parity, count, W0) for row in rows]
        left = jnp.concatenate(lefts, axis=0) if len(lefts) > 1 else lefts[0]
        right = jnp.concatenate(rights, axis=0) if len(rights) > 1 else rights[0]
        total_one[...] = product_tn(left, right)
        for slot, col_tap in enumerate(COL_TAPS):
            to = ((row_tap % 2) * 4 + col_tap) * in_chan
            put(row_tap // 2, to, in_chan, lambda: total_one[:, slot * mid_chan:(slot + 1) * mid_chan])


def decoder_kernel(
    count, side_ref, latent_ref, w_one_ref, w_two_ref, w_three_ref, target_ref,
    decoded_ref, kept_a_ref, kept_b_ref, kept_c_ref, sent_a_ref, sent_b_ref, sent_c_ref,
    grad_one, act_one, slope_one, act_two, slope_two, grad_two, kgrad_three, tmp_one, tmp_two, tmp_three, grads, adj_two, adj_one, total_one, total_two,
):
    step = pl.program_id(0)
    steps = pl.num_programs(0)

    @pl.when(step == 0)
    def _():
        forward_part(count, latent_ref, w_one_ref, w_two_ref, act_one, slope_one, act_two, slope_two, tmp_one, tmp_two)

    last_part(
        count, step, steps, act_two, slope_two, w_three_ref, target_ref, decoded_ref, grad_two, kgrad_three, tmp_three, grads, adj_two
    )

    @pl.when(step == steps - 1)
    def _():
        backward_part(
            count, side_ref, latent_ref, act_one, slope_one, w_two_ref, grad_two, kgrad_three,
            grad_one, (kept_a_ref, kept_b_ref, kept_c_ref), (sent_a_ref, sent_b_ref, sent_c_ref), adj_one, total_one, total_two,
        )


def params(mebibytes, gridded=False):
    order = ("arbitrary",) if gridded else None
    return pltpu.CompilerParams(vmem_limit_bytes=mebibytes * 1024 * 1024, dimension_semantics=order)


def decoder(side, latent, w_one, w_two, w_three, target):
    count = latent.shape[1]
    mid_chan = w_two.shape[1] // 2
    out_chan = w_two.shape[2] // 4
    height, breadth = 2 * H0, 2 * W0
    steps, flat, lanes = target.shape[0] // 2, target.shape[1], target.shape[2]
    third_rows = w_three.shape[1]

    def whole(shape):
        return pl.BlockSpec(shape, lambda step: (0,) * len(shape))

    act_one = (height, breadth * count, mid_chan)
    act_two = (2 * height, flat, out_chan)
    padded = (2 * height + 2, flat, out_chan)
    in_chan = w_one.shape[0] // 16
    quarter, tail = (4 * in_chan, mid_chan), (4 * mid_chan + third_rows, mid_chan)
    single = pl.Buffered(1)
    return pl.pallas_call(
        functools.partial(decoder_kernel, count),
        name="decoder",
        grid=(steps,),
        in_specs=[
            pl.BlockSpec(memory_space=pltpu.SMEM),
            pl.BlockSpec(latent.shape, lambda step: (0, 0, 0), pipeline_mode=single),
            pl.BlockSpec(w_one.shape, lambda step: (0, 0), pipeline_mode=single),
            pl.BlockSpec(w_two.shape, lambda step: (0, 0, 0), pipeline_mode=single),
            pl.BlockSpec(w_three.shape, lambda step: (0, 0, 0), pipeline_mode=single),
            pl.BlockSpec((2, flat, lanes), lambda step: (step, 0, 0)),
        ],
        out_specs=(
            pl.BlockSpec((2, flat, lanes), lambda step: (step, 0, 0)),
            *map(whole, 2 * (quarter, quarter, tail)),
        ),
        out_shape=(
            jax.ShapeDtypeStruct(target.shape, jnp.bfloat16),
            *(jax.ShapeDtypeStruct(shape, jnp.bfloat16) for shape in 2 * (quarter, quarter, tail)),
        ),
        scratch_shapes=[
            pltpu.VMEM(act_one, jnp.bfloat16),
            pltpu.VMEM(act_one, jnp.bfloat16),
            pltpu.VMEM(act_one, jnp.float32),
            pltpu.VMEM(padded, jnp.bfloat16),
            pltpu.VMEM(act_two, jnp.float32),
            pltpu.VMEM(act_two, jnp.bfloat16),
            pltpu.VMEM(w_three.shape, jnp.float32),
            pltpu.VMEM((W0 * count, 4 * mid_chan), jnp.float32),
            pltpu.VMEM((breadth * count, 4 * out_chan), jnp.float32),
            pltpu.VMEM((flat, 2 * lanes), jnp.float32),
            pltpu.VMEM((flat + 2 * count, lanes), jnp.float32),
            pltpu.VMEM(padded, jnp.float32),
            pltpu.VMEM(act_one, jnp.float32),
            pltpu.VMEM((in_chan, 4 * mid_chan), jnp.float32),
            pltpu.VMEM(w_two.shape, jnp.float32),
        ],
        compiler_params=params(60, True),
    )(side, latent, w_one, w_two, w_three, target)


def spatial_first_kernel(grid_ref, after_ref, rows_ref, tmp):
    count, height, breadth, chan = grid_ref.shape
    for row in range(height):
        tmp[...] = grid_ref[:, row].astype(jnp.float32)
        even = tmp[:, pl.ds(0, breadth // 2, 2), :]
        odd = tmp[:, pl.ds(1, breadth // 2, 2), :]
        turned = jnp.swapaxes(jnp.concatenate([even, odd], axis=2), 0, 1)
        rows_ref[row] = turned.reshape(breadth // 2 * count, 2 * chan).astype(jnp.bfloat16)


def spatial_first(grid, after):
    count, height, breadth, chan = grid.shape
    per = 4
    flat = breadth // 2 * count
    return pl.pallas_call(
        spatial_first_kernel,
        name="spatial_first",
        grid=(height // per,),
        in_specs=[
            pl.BlockSpec((count, per, breadth, chan), lambda step: (0, step, 0, 0)),
            pl.BlockSpec(memory_space=pl.ANY),
        ],
        out_specs=pl.BlockSpec((per, flat, 2 * chan), lambda step: (step, 0, 0)),
        out_shape=jax.ShapeDtypeStruct((height, flat, 2 * chan), jnp.bfloat16),
        scratch_shapes=[pltpu.VMEM((count, breadth, chan), jnp.float32)],
        compiler_params=params(20, True),
        cost_estimate=pl.CostEstimate(flops=0, bytes_accessed=28000000, transcendentals=0),
    )(grid, after)


def sample_first_kernel(rows_ref, after_ref, out_ref, tmp):
    height = rows_ref.shape[0]
    count, _, breadth, chan = out_ref.shape
    for row in range(height):
        value = rows_ref[row].astype(jnp.float32).reshape(breadth // 2, count, 2 * chan)
        turned = jnp.swapaxes(value, 0, 1)
        tmp[:, pl.ds(0, breadth // 2, 2), :] = turned[:, :, :chan]
        tmp[:, pl.ds(1, breadth // 2, 2), :] = turned[:, :, chan:]
        out_ref[:, row] = tmp[...].astype(jnp.bfloat16)


def sample_first(rows, count, chan, after):
    height, flat, lanes = rows.shape
    breadth = 2 * flat // count
    per = 4
    return pl.pallas_call(
        sample_first_kernel,
        name="sample_first",
        grid=(height // per,),
        in_specs=[
            pl.BlockSpec((per, flat, lanes), lambda step: (step, 0, 0)),
            pl.BlockSpec(memory_space=pl.ANY),
        ],
        out_specs=pl.BlockSpec((count, per, breadth, chan), lambda step: (0, step, 0, 0)),
        out_shape=jax.ShapeDtypeStruct((count, height, breadth, chan), jnp.bfloat16),
        scratch_shapes=[pltpu.VMEM((count, breadth, chan), jnp.float32)],
        compiler_params=params(20, True),
        cost_estimate=pl.CostEstimate(flops=0, bytes_accessed=28000000, transcendentals=0),
    )(rows, after)


def bucket_kernel(half, subject_ref, count_ref, shift_ref, fmri_ref, after_ref, out_ref, place_ref):
    samples, voxels = fmri_ref.shape
    slots = out_ref.shape[0]
    subjects = count_ref.shape[0]
    room = slots // subjects
    owner = subject_ref[...]
    name = lax.broadcasted_iota(jnp.int32, (subjects, samples), 0)
    onehot = jnp.where(owner == name, 1.0, 0.0)
    row = lax.broadcasted_iota(jnp.int32, (samples, samples), 0)
    col = lax.broadcasted_iota(jnp.int32, (samples, samples), 1)
    before = jnp.where(row < col, 1.0, 0.0).astype(jnp.bfloat16)
    earlier = product(onehot.astype(jnp.bfloat16), before)
    rank = jnp.sum(earlier * onehot, axis=0, keepdims=True).astype(jnp.int32) - half * room
    position = jnp.where((rank >= 0) & (rank < room), owner * room + rank, -1)
    slot = lax.broadcasted_iota(jnp.int32, (slots, samples), 0)
    place_ref[...] = jnp.where(slot == position, 1.0, 0.0).astype(jnp.bfloat16)
    voxel = lax.broadcasted_iota(jnp.int32, (room, voxels), 1) + shift_ref[0]
    together = max(1, 64 // room)
    for start in range(0, subjects, together):
        rows = product(place_ref[pl.ds(start * room, together * room), :], fmri_ref[...])
        for inner in range(together):
            kept = jnp.where(voxel < count_ref[start + inner], rows[inner * room:(inner + 1) * room], 0.0)
            out_ref[pl.ds((start + inner) * room, room), :] = kept.astype(jnp.bfloat16)


def bucketed(half, subject, voxel_count, shift, fmri, after):
    samples, voxels = fmri.shape
    vmem = pl.BlockSpec(memory_space=pltpu.VMEM)
    smem = pl.BlockSpec(memory_space=pltpu.SMEM)
    return pl.pallas_call(
        functools.partial(bucket_kernel, half),
        name="bucket_rows",
        in_specs=[vmem, smem, smem, vmem, pl.BlockSpec(memory_space=pl.ANY)],
        out_specs=(vmem, vmem),
        out_shape=(
            jax.ShapeDtypeStruct((samples, voxels), jnp.bfloat16),
            jax.ShapeDtypeStruct((samples, samples), jnp.bfloat16),
        ),
        compiler_params=params(60),
    )(subject.reshape(1, samples), voxel_count, shift, fmri, after)


def project_kernel(quarter_ref, rows_ref, map_ref, *after_and_out):
    out_ref = after_and_out[-1]
    width = out_ref.shape[2]
    for block in range(out_ref.shape[0]):
        value = product(rows_ref[...], map_ref[0, :, block * width:(block + 1) * width])
        out_ref[block] = value.astype(jnp.bfloat16)


def projected(rows, maps, part, after, parts):
    count, voxels = rows.shape
    blocks = H0 * W0 // parts
    width = maps.shape[2] // (H0 * W0)
    step_blocks = max(1, blocks // 2)
    steps = blocks // step_blocks
    return pl.pallas_call(
        project_kernel,
        name="project_rows",
        grid_spec=pltpu.PrefetchScalarGridSpec(
            num_scalar_prefetch=1,
            grid=(steps,),
            in_specs=[
                pl.BlockSpec((count, voxels), lambda step, part: (0, 0)),
                pl.BlockSpec((1, voxels, step_blocks * width), lambda step, part: (0, 0, part[0] * steps + step)),
            ] + [pl.BlockSpec(memory_space=pl.ANY)] * len(after),
            out_specs=pl.BlockSpec((step_blocks, count, width), lambda step, part: (step, 0, 0)),
        ),
        out_shape=jax.ShapeDtypeStruct((blocks, count, width), jnp.bfloat16),
        compiler_params=params(60, True),
        cost_estimate=pl.CostEstimate(
            flops=2 * count * voxels * maps.shape[2] // parts,
            bytes_accessed=2 * voxels * maps.shape[2] // parts,
            transcendentals=0,
        ),
    )(part, rows, maps, *after)


def collect_kernel(place_a_ref, place_b_ref, first_ref, second_ref, *after_and_out):
    out_ref = after_and_out[-1]
    subjects, blocks, room, width = first_ref.shape
    for block in range(blocks):
        value = None
        for place_ref, ref in ((place_a_ref, first_ref), (place_b_ref, second_ref)):
            rows = jnp.concatenate([ref[subject, block] for subject in range(subjects)], axis=0)
            term = product_tn(place_ref[...], rows)
            value = term if value is None else value + term
        out_ref[:, pl.ds(block * width, width)] = value.astype(jnp.bfloat16)


def collected(places, first, second, after):
    samples = places[0].shape[1]
    vmem = pl.BlockSpec(memory_space=pltpu.VMEM)
    return pl.pallas_call(
        collect_kernel,
        name="collect_rows",
        in_specs=[vmem] * 4 + [pl.BlockSpec(memory_space=pl.ANY)] * len(after),
        out_specs=vmem,
        out_shape=jax.ShapeDtypeStruct((samples, first.shape[1] * first.shape[3]), jnp.bfloat16),
        compiler_params=params(16),
    )(*places, first, second, *after)


def finish_kernel(third_rows, side_ref, own_a, own_b, own_c, other_a, other_b, other_c, first_ref, second_ref, third_ref):
    side = side_ref[0]
    rows = own_a.shape[0]
    for at, (source, half) in enumerate(((own_a, side), (own_b, side), (other_a, 1 - side), (other_b, 1 - side))):
        start = pl.multiple_of((2 * half + at % 2) * rows, rows)
        first_ref[pl.ds(start, rows), :] = source[...]
    out_chan = second_ref.shape[1]
    mid_chan = second_ref.shape[0] // 16
    for parity in (0, 1):
        mine = side == parity
        for which in (0, 1):
            for pair in (0, 1):
                here = pl.ds((2 * which + pair) * mid_chan, mid_chan)
                value = jnp.where(mine, own_c[here, :].astype(jnp.float32), other_c[here, :].astype(jnp.float32))
                for inner in (0, 1):
                    col_tap = COL_TAPS[2 * pair + inner]
                    to = pl.ds((ROW_TAPS[parity][which] * 4 + col_tap) * mid_chan, mid_chan)
                    second_ref[to, :] = value[:, inner * out_chan:(inner + 1) * out_chan].astype(jnp.bfloat16)
        here = pl.ds(4 * mid_chan, third_rows)
        value = jnp.where(mine, own_c[here, :].astype(jnp.float32), other_c[here, :].astype(jnp.float32)).T
        chan = third_ref.shape[0]
        inputs = third_rows // 2
        for which in (0, 1):
            for slot, col_tap in enumerate(COL_TAPS):
                to = pl.ds((ROW_TAPS[parity][which] * 4 + col_tap) * inputs, inputs)
                piece = value[slot * chan:(slot + 1) * chan, which * inputs:(which + 1) * inputs]
                third_ref[:, to] = piece.astype(jnp.bfloat16)


def finished(side, own, other, third_rows):
    rows, lanes = own[0].shape
    mid_chan = (own[2].shape[0] - third_rows) // 4
    vmem = pl.BlockSpec(memory_space=pltpu.VMEM)
    return pl.pallas_call(
        functools.partial(finish_kernel, third_rows),
        name="finish_gradients",
        in_specs=[pl.BlockSpec(memory_space=pltpu.SMEM)] + [vmem] * 6,
        out_specs=(vmem, vmem, vmem),
        out_shape=(
            jax.ShapeDtypeStruct((4 * rows, lanes), jnp.bfloat16),
            jax.ShapeDtypeStruct((16 * mid_chan, lanes // 2), jnp.bfloat16),
            jax.ShapeDtypeStruct((lanes // 4, 8 * third_rows), jnp.bfloat16),
        ),
        compiler_params=params(24),
    )(side, *own, *other)


def rounded(values):
    return lax.optimization_barrier(values.astype(jnp.bfloat16))


def bit_pairs(axis):
    size = lax.axis_size(axis)
    bits = []
    bit = 1
    while bit < size:
        bits.append((axis, bit))
        bit *= 2
    return bits


def upper(hop):
    axis, bit = hop
    return (lax.axis_index(axis) // bit) % 2


def place_of(step):
    return sum(upper(hop) * 2 ** at for at, hop in enumerate(step))


def exchanged(values, step, change):
    axis = step[0][0]
    flip = sum(hop[1] for at, hop in enumerate(step) if change >> at & 1)
    return lax.ppermute(values, axis, [(at, at ^ flip) for at in range(lax.axis_size(axis))])


def summed(terms):
    value = terms[0]
    for term in terms[1:]:
        value = value.astype(jnp.float32) + term.astype(jnp.float32)
    return value


def shared(chains, step):
    ways = 2 ** len(step)
    place = place_of(step)

    def part(terms, which):
        size = terms[0].shape[0] // ways
        return summed([lax.dynamic_slice_in_dim(term, which * size, size, 0) for term in terms])

    arrived = []
    for change in range(1, ways):
        sent = [part(terms, place ^ change).astype(jnp.bfloat16) for terms in chains]
        joined = jnp.concatenate(sent, axis=0) if len(sent) > 1 else sent[0]
        arrived.append(exchanged(joined, step, change))
    result = []
    start = 0
    for terms in chains:
        size = terms[0].shape[0] // ways
        result.append([part(terms, place)] + [values[start:start + size] for values in arrived])
        start += size
    return result


def gathered(chains, step):
    ways = 2 ** len(step)
    joined = jnp.concatenate(chains, axis=0) if len(chains) > 1 else chains[0]
    pieces = [joined] + [exchanged(joined, step, change) for change in range(1, ways)]
    place = place_of(step)
    result = []
    start = 0
    for values in chains:
        size = values.shape[0]
        out = jnp.concatenate([values] * ways, axis=0)
        for change in range(1, ways):
            piece = pieces[change][start:start + size]
            out = lax.dynamic_update_slice_in_dim(out, piece, (place ^ change) * size, 0)
        result.append(out)
        start += size
    return result


def over_chains(move, chains, steps):
    result = [None] * len(chains)
    for step in {tuple(step): step for step in steps}.values():
        members = [at for at, own in enumerate(steps) if own == step]
        for at, moved_chain in zip(members, move([chains[at] for at in members], step)):
            result[at] = moved_chain
    return result


def shards(fmri, subject, ridge_maps, voxel_count, w_first, w_second, w_third, target):
    dp_count = lax.axis_size("dp")
    holders = lax.axis_size("vox")
    samp_dev = fmri.shape[0]
    vox_local = fmri.shape[1]
    mid_chan = w_first.shape[1]
    last_chan = w_second.shape[1]
    room = samp_dev // dp_count
    vox_bits = bit_pairs("vox")
    dp_bits = bit_pairs("dp")
    side = upper(vox_bits[0]).astype(jnp.int32).reshape(1)
    shift = (lax.axis_index("vox") * vox_local).astype(jnp.int32).reshape(1)
    first, place_first = bucketed(0, subject, voxel_count, shift, fmri, voxel_count)
    second, place_second = bucketed(1, subject, voxel_count, shift, fmri, place_first)

    def routed(rows):
        sent = rows.reshape(dp_count, room, rows.shape[1])
        return lax.all_to_all(sent, "dp", split_axis=0, concat_axis=0, tiled=True).reshape(rows.shape)

    core_bit, cross_bit = upper(vox_bits[0]), upper(vox_bits[1])

    def part_of(*bits):
        return sum(bit * 2 ** at for at, bit in enumerate(bits[::-1])).astype(jnp.int32).reshape(1)

    def to_cross(rows, *after):
        for_core = projected(rows, ridge_maps, part_of(1 - core_bit), after, 2)
        received = exchanged(for_core, vox_bits[:1], 1)
        own = projected(rows, ridge_maps, part_of(core_bit, 1 - cross_bit), (for_core,), 4)
        half = received.shape[0] // 2
        added = lax.dynamic_slice_in_dim(received, (1 - cross_bit) * half, half, 0)
        return summed([own, added]).astype(jnp.bfloat16), lax.dynamic_slice_in_dim(received, cross_bit * half, half, 0)

    def own_part(rows, *after):
        return projected(rows, ridge_maps, part_of(core_bit, cross_bit), after, 4)

    def rest_summed(*terms):
        terms = list(terms)
        for hop in vox_bits[2:]:
            terms, = shared([terms], [hop])
        return terms

    def returned(terms):
        latent_part = rounded(summed(terms))
        blocks, _, width = latent_part.shape
        sent = latent_part.reshape(blocks, dp_count, room, width).swapaxes(0, 1)
        return lax.all_to_all(sent, "dp", split_axis=0, concat_axis=0, tiled=True)

    first = routed(first)
    second = routed(second)
    across_first, added_first = to_cross(first, voxel_count)
    arrived_first = exchanged(across_first, vox_bits[1:2], 1)
    own_first = own_part(first, across_first)
    across_second, added_second = to_cross(second, arrived_first, own_first)
    arrived_second = exchanged(across_second, vox_bits[1:2], 1)
    own_second = own_part(second, across_second)
    terms_first = rest_summed(own_first, added_first, arrived_first)
    pair_two = paired_weight(w_second, mid_chan)
    pair_three = paired_weight(w_third, last_chan)
    target_rows = spatial_first(target, across_second)
    places = (place_first, place_second)
    back_first = returned(terms_first)
    back_first, arrived_second = lax.optimization_barrier((back_first, arrived_second))
    back_second = returned(rest_summed(own_second, added_second, arrived_second))
    own_rows = collected(places, back_first, back_second, (target_rows, pair_two, pair_three))
    own_rows = own_rows.reshape(holders, samp_dev // holders, own_rows.shape[1])
    latent = lax.all_to_all(own_rows, "vox", split_axis=0, concat_axis=0, tiled=True)
    count = latent.shape[1]
    decoded_rows, *shares = decoder(side, latent, w_first, pair_two, pair_three, target_rows)
    third_rows = pair_three.shape[1]
    received = [exchanged(values, vox_bits[:1], 1) for values in shares[3:]]
    across = [[hop] for hop in vox_bits[1:]]
    near = [dp_bits[:1]]
    along = [[hop] for hop in dp_bits[1:]]
    routes = (across + near + along, near + across + along, along[:1] + across + near + along[1:])
    parts = [list(pair) for pair in zip(shares[:3], received)]
    decoded = sample_first(decoded_rows, count, w_third.shape[1], received[1])
    for stage in range(len(routes[0])):
        parts = over_chains(shared, parts, [route[stage] for route in routes])
        if stage < len(routes[0]) - 1:
            *tied, decoded = lax.optimization_barrier(tuple(terms[1] for terms in parts) + (decoded,))
            parts = [terms[:1] + [arrived] + terms[2:] for terms, arrived in zip(parts, tied)]
    shares = [summed(terms).astype(jnp.bfloat16) for terms in parts]
    for stage in reversed(range(len(routes[0]))):
        shares = over_chains(gathered, shares, [route[stage] for route in routes])
        if stage > 1:
            shares = list(lax.optimization_barrier(tuple(shares)))
    others = [exchanged(values, vox_bits[:1], 1) for values in shares]
    total_first, total_second, third = finished(side, shares, others, third_rows)
    total_third = third.T
    return (decoded, total_first, total_second, total_third)


def solution(mesh):
    placed = (
        P("dp", "vox"),
        P("dp", None),
        P("dp", "vox", None),
        P(),
        P(),
        P(),
        P(),
        P(("dp", "vox"), None, None, None),
    )
    return jax.shard_map(
        shards,
        mesh=mesh,
        in_specs=placed,
        out_specs=(P(("dp", "vox"), None, None, None), P(), P(), P()),
        check_vma=False,
    )
```
